32 devices in a mesh: blk: 8 (over z, y), grp: 4 (over x, core).
Axes of the slice: x: 2, y: 2, z: 4, core: 2. Of those that a mesh axis runs over, the one named last changes fastest.
Arguments:
- token_ids: int32 [128, 2, 128], P(('blk', 'grp')), may hold values from 0 to 30719
- lengths: int32 [128, 2], P(('blk', 'grp')), may hold values from 32 to 128, as said below
- valid: int32 [128], P(('blk', 'grp')), may hold values from 0 to 1
- false_neg: int32 [128, 128], P(('blk', 'grp')), may hold values from 0 to 1, as said below
- word_table: bfloat16 [30720, 768], P('grp'), may hold values from -1.75 to 1.75
- qkv_weight: bfloat16 [768, 2304], replicated, may hold values from -0.21875 to 0.21875
- out_weight: bfloat16 [768, 768], replicated, may hold values from -1.75 to 1.75
- up_weight: bfloat16 [768, 3072], replicated, may hold values from -0.21875 to 0.21875
- down_weight: bfloat16 [3072, 768], replicated, may hold values from -0.109375 to 0.109375
- word_master: float32 [30720, 768], P('blk'), may hold values from -1.75 to 1.75
- qkv_master: float32 [768, 2304], P('blk'), may hold values from -0.21875 to 0.21875
- out_master: float32 [768, 768], P('blk'), may hold values from -1.75 to 1.75
- up_master: float32 [768, 3072], P('blk'), may hold values from -0.21875 to 0.21875
- down_master: float32 [3072, 768], P('blk'), may hold values from -0.109375 to 0.109375
- word_moments: float32 [2, 30720, 768], P(None, 'blk'), as said below
- qkv_moments: float32 [2, 768, 2304], P(None, 'blk'), as said below
- out_moments: float32 [2, 768, 768], P(None, 'blk'), as said below
- up_moments: float32 [2, 768, 3072], P(None, 'blk'), as said below
- down_moments: float32 [2, 3072, 768], P(None, 'blk'), as said below
- small_rows: float32 [142, 768], replicated
- small_moments: float32 [2, 142, 768], replicated, as said below
Outputs:
- loss_sum: float32 [], replicated
- pair_count: float32 [], replicated
- grad_norm: float32 [], replicated
- word_first: float32 [30720, 768], P('blk')
- word_second: float32 [30720, 768], P('blk')
- word_updated: float32 [30720, 768], P('blk')
- qkv_first: float32 [768, 2304], P('blk')
- qkv_second: float32 [768, 2304], P('blk')
- qkv_updated: float32 [768, 2304], P('blk')
- out_first: float32 [768, 768], P('blk')
- out_second: float32 [768, 768], P('blk')
- out_updated: float32 [768, 768], P('blk')
- up_first: float32 [768, 3072], P('blk')
- up_second: float32 [768, 3072], P('blk')
- up_updated: float32 [768, 3072], P('blk')
- down_first: float32 [3072, 768], P('blk')
- down_second: float32 [3072, 768], P('blk')
- down_updated: float32 [3072, 768], P('blk')
- small_first: float32 [142, 768], replicated
- small_second: float32 [142, 768], replicated
- small_updated: float32 [142, 768], replicated
The draws below stay inside these ranges and needn't reach their ends.
Inputs may be any that keep to these rules, and one draw needn't show every extreme that they name: `lengths`: at least one sequence has length exactly 128. `false_neg`: symmetric, zero on the diagonal. `word_moments`: the second of the two stacked moments is positive. `qkv_moments`: the second of the two stacked moments is positive. `out_moments`: the second of the two stacked moments is positive. `up_moments`: the second of the two stacked moments is positive. `down_moments`: the second of the two stacked moments is positive. `small_moments`: the second of the two stacked moments is positive.
All inputs are finite; a program needn't handle non-finite values.
Results may differ from the reference program's by a relative error of at most 0.011.
Values may be sent and summed in bfloat16 or wider, within the bound.
No kernel may reach another device: no remote copies, remote signals or barrier semaphores. Data moves between devices by JAX's collectives and lax.ppermute only.
A program may use at most 384 MiB of HBM per device.

```python
import math
import jax
import jax.numpy as jnp
import numpy as np
from jax import lax

D = 768
HEADS = 12
HEAD_DIM = 64
FF = 3072
VOCAB = 30720
SEQ = 128
PAIRS_DEV = 4
STEP = 5
PAIRS = 128
SMALL_ROWS = 142
NPARAM = 30779904
N_BLK = 8
N_GRP = 4


def moment_pair(key, shape, size):
    keys = jax.random.split(key, 3)
    magnitude = jax.random.uniform(keys[0], shape, jnp.float32, 0.5, 1.5)
    signs = jnp.where(jax.random.bernoulli(keys[1], 0.5, shape), 1.0, -1.0)
    second = size * size * jnp.exp(jax.random.uniform(keys[2], shape, jnp.float32, 0.0, math.log(4.0)))
    return jnp.stack([size * magnitude * signs, second])


def gradient_size():
    return 0.001 / math.sqrt(NPARAM)


def matrix_size():
    return 0.001 / math.sqrt(4 * D * D + 2 * D * FF)


def draw_lengths(key, part):
    key = jax.random.fold_in(key, 3)
    keys = jax.random.split(key, 2)
    drawn = jax.random.randint(keys[0], (PAIRS * 2,), SEQ // 4, SEQ + 1)
    pick = jax.random.randint(keys[1], (), 0, PAIRS * 2)
    filled = jnp.where(jnp.arange(PAIRS * 2) == pick, SEQ, drawn)
    return filled.reshape(PAIRS, 2).astype(jnp.int32)


def draw_valid(key, part):
    key = jax.random.fold_in(key, 5)
    device = jnp.arange(PAIRS) // PAIRS_DEV
    block = device // N_GRP
    group = device % N_GRP
    limit = 150 + 350 * block // max(N_BLK - 1, 1) + 350 * group // max(N_GRP - 1, 1)
    drawn = jax.random.randint(key, (PAIRS,), 0, 1000)
    return (drawn < limit).astype(jnp.int32)


def draw_false_neg(key, part):
    key = jax.random.fold_in(key, 7)
    upper = jax.random.randint(key, (PAIRS, PAIRS), 0, 16)
    total = upper + upper.T
    diagonal = jnp.arange(PAIRS)[:, None] == jnp.arange(PAIRS)[None, :]
    return jnp.where((total < 3) & ~diagonal, 1, 0).astype(jnp.int32)


def draw_word_moments(key, part):
    key = jax.random.fold_in(key, 11)
    return moment_pair(key, (VOCAB, D), gradient_size())


def draw_qkv_moments(key, part):
    key = jax.random.fold_in(key, 13)
    return moment_pair(key, (D, 3 * D), matrix_size())


def draw_out_moments(key, part):
    key = jax.random.fold_in(key, 17)
    return moment_pair(key, (D, D), matrix_size())


def draw_up_moments(key, part):
    key = jax.random.fold_in(key, 19)
    return moment_pair(key, (D, FF), matrix_size())


def draw_down_moments(key, part):
    key = jax.random.fold_in(key, 23)
    return moment_pair(key, (FF, D), matrix_size())


def draw_small_moments(key, part):
    key = jax.random.fold_in(key, 29)
    rows = jnp.arange(SMALL_ROWS)[:, None]
    sizes = jnp.where(rows < SEQ, matrix_size() / math.sqrt(SEQ), matrix_size()) * jnp.ones((SMALL_ROWS, D), jnp.float32)
    return moment_pair(key, (SMALL_ROWS, D), sizes)


def draw_small_rows(key, part):
    key = jax.random.fold_in(key, 31)
    keys = jax.random.split(key, 3)
    positions = 0.3 * jax.random.normal(keys[0], (SEQ, D), jnp.float32)
    rising = 0.6 * 3.0 ** (jnp.arange(D).astype(jnp.float32) / max(D - 1, 1))
    gains = rising * (1.0 + 0.1 * jax.random.normal(keys[1], (3, D), jnp.float32))
    shifts = 0.3 * jax.random.normal(keys[2], (11, D), jnp.float32)
    rows = [gains[0], shifts[0], shifts[1], shifts[2], shifts[3], gains[1], shifts[4], shifts[5], gains[2], shifts[6]]
    return jnp.concatenate([positions, jnp.stack(rows), shifts[7:11]], 0)


def plant(array, stream_key, smallest, high):
    index_at = [jax.random.randint(jax.random.fold_in(stream_key, axis), (), 0, length) for axis, length in enumerate(array.shape)]
    widest = array.shape.index(max(array.shape))
    next_to = index_at[:widest] + [(index_at[widest] + 1) % array.shape[widest]] + index_at[widest + 1:]
    return array.at[tuple(index_at)].set(smallest).at[tuple(next_to)].set(high)


def block_levels(rng, shape, cuts, least, high):
    level = 1.0
    for position, shards_of in cuts:
        draws = jax.random.uniform(jax.random.fold_in(jax.random.fold_in(rng, 6), position), (shards_of,), jnp.float32, least / len(cuts), high / len(cuts))
        level = level * jnp.repeat(jnp.exp(draws), shape[position] // shards_of).reshape((-1,) + (1,) * (len(shape) - 1 - position))
    return level


def rank_bounds(amount, lean):
    weights = [(1 << 20) // math.isqrt(grade ** lean) + 1 for grade in range(1, amount + 1)]
    width = 1 + sum(weights) // (1 << 30)
    return np.cumsum(np.array([max(1, weight // width) for weight in weights]))


def skewed_ids(key, dims, amount, slope):
    listing = rank_bounds(amount, slope)
    lot = jax.random.randint(jax.random.fold_in(key, 1), dims, 0, int(listing[amount - 1]))
    grade = jnp.searchsorted(jnp.asarray(listing, jnp.int32), lot, side="right")
    return jax.random.permutation(jax.random.fold_in(key, 2), amount)[grade].astype(jnp.int32)


def gaussian(own_key, shape, width, most, cuts=(), kind=jnp.bfloat16):
    factor_of = block_levels(own_key, shape, cuts, -0.22, 0.18) if cuts else 1.0
    values = jax.random.normal(own_key, shape, jnp.float32) * width * factor_of
    return jnp.minimum(jnp.maximum(values, -most), most).astype(kind)


def setup_inputs(seed: int = 0) -> dict:
    arg_keys = jax.random.split(jax.random.key(seed), 22)
    token_ids = plant(skewed_ids(arg_keys[0], (PAIRS, 2, SEQ), VOCAB, 2), jax.random.fold_in(arg_keys[0], 3), 0, VOCAB - 1).astype(jnp.int32)
    lengths = draw_lengths(jax.random.fold_in(arg_keys[21], 71), 0)
    valid = draw_valid(jax.random.fold_in(arg_keys[21], 71), 0)
    false_neg = draw_false_neg(jax.random.fold_in(arg_keys[21], 71), 0)
    word_table = gaussian(arg_keys[4], (VOCAB, D), 0.3, 1.75, ((0, 4),))
    qkv_weight = gaussian(arg_keys[5], (D, 3 * D), D ** -0.5, 0.21875)
    out_weight = gaussian(arg_keys[6], (D, D), (D * 2 // SEQ) ** -0.5, 1.75)
    up_weight = gaussian(arg_keys[7], (D, FF), D ** -0.5, 0.21875)
    down_weight = gaussian(arg_keys[8], (FF, D), FF ** -0.5, 0.109375)
    word_master = gaussian(arg_keys[9], (VOCAB, D), 0.3, 1.75, ((0, 8),), jnp.float32)
    qkv_master = gaussian(arg_keys[10], (D, 3 * D), D ** -0.5, 0.21875, ((0, 8),), jnp.float32)
    out_master = gaussian(arg_keys[11], (D, D), (D * 2 // SEQ) ** -0.5, 1.75, ((0, 8),), jnp.float32)
    up_master = gaussian(arg_keys[12], (D, FF), D ** -0.5, 0.21875, ((0, 8),), jnp.float32)
    down_master = gaussian(arg_keys[13], (FF, D), FF ** -0.5, 0.109375, ((0, 8),), jnp.float32)
    word_moments = draw_word_moments(jax.random.fold_in(arg_keys[21], 71), 0)
    qkv_moments = draw_qkv_moments(jax.random.fold_in(arg_keys[21], 71), 0)
    out_moments = draw_out_moments(jax.random.fold_in(arg_keys[21], 71), 0)
    up_moments = draw_up_moments(jax.random.fold_in(arg_keys[21], 71), 0)
    down_moments = draw_down_moments(jax.random.fold_in(arg_keys[21], 71), 0)
    small_rows = draw_small_rows(jax.random.fold_in(arg_keys[21], 71), 0)
    small_moments = draw_small_moments(jax.random.fold_in(arg_keys[21], 71), 0)
    return dict(token_ids=token_ids, lengths=lengths, valid=valid, false_neg=false_neg, word_table=word_table, qkv_weight=qkv_weight, out_weight=out_weight, up_weight=up_weight, down_weight=down_weight, word_master=word_master, qkv_master=qkv_master, out_master=out_master, up_master=up_master, down_master=down_master, word_moments=word_moments, qkv_moments=qkv_moments, out_moments=out_moments, up_moments=up_moments, down_moments=down_moments, small_rows=small_rows, small_moments=small_moments)


@jax.custom_vjp
def low(v):
    return lax.optimization_barrier(v.astype(jnp.bfloat16)).astype(jnp.float32)

@jax.custom_vjp
def low_back(v):
    return v

def low_keep(v):
    return (low(v), None)

def reduced_width_forward(kept, grad):
    return (grad,)

def back_keep(v):
    return (v, None)

def back_low(kept, grad):
    return (low(grad),)
low.defvjp(low_keep, reduced_width_forward)
low_back.defvjp(back_keep, back_low)
logit_divisor_constant = 0.01
clip_bound = 0.001
beta_first = 0.5
beta_second = 0.5
decay_weight = 0.01
epsilon = 1e-08
rate_table = (0.1, 0.02, 0.1, 0.02, 0.01, 0.2)
finest_arithmetic = lax.Precision.HIGHEST

def layer_norm(states, gain, shift):
    mean = lax.optimization_barrier(jnp.mean(states, -1, keepdims=True))
    centered = states - mean
    variance = lax.optimization_barrier(jnp.mean(centered * centered, -1, keepdims=True))
    return centered * lax.rsqrt(variance + 1e-06) * gain + shift

def exact_gelu(values):
    return jax.nn.gelu(values, approximate=False)

def pool_unit(states, lengths_flat):
    positions = jnp.arange(states.shape[1])
    weights = (positions[None, :] < lengths_flat[:, None]).astype(jnp.float32)
    pooled = lax.optimization_barrier(jnp.sum(states * weights[:, :, None], 1)) / lengths_flat[:, None].astype(jnp.float32)
    return pooled * lax.rsqrt(lax.optimization_barrier(jnp.sum(pooled * pooled, -1, keepdims=True)) + 1e-06)

def project(inputs, matrix):
    return jnp.einsum('gsd,de->gse', inputs, matrix, precision=finest_arithmetic)

def adam_update(grad, moments, master, rate):
    first = beta_first * moments[0] + (1.0 - beta_first) * grad
    second = beta_second * moments[1] + (1.0 - beta_second) * grad * grad
    first_hat = first / (1.0 - beta_first ** STEP)
    second_hat = second / (1.0 - beta_second ** STEP)
    updated = master - rate * (first_hat / (jnp.sqrt(second_hat) + epsilon) + decay_weight * master)
    return (first, second, updated)

def encode(params, token_block, length_block):
    word, qkv_matrix, out_matrix, up_matrix, down_matrix, small = params
    vectors = small[SEQ:]
    embedded = word[token_block] + small[:SEQ]
    normed = layer_norm(embedded, vectors[0], vectors[1])
    qkv_bias = jnp.concatenate([vectors[2], jnp.zeros_like(vectors[2]), vectors[3]])
    projected = low(low_back(project(low(normed), qkv_matrix) + qkv_bias))
    shape = token_block.shape + (HEADS, HEAD_DIM)
    query = projected[..., :D].reshape(shape)
    keys = projected[..., D:2 * D].reshape(shape)
    values = projected[..., 2 * D:].reshape(shape)
    unnormalized_affinity = jnp.einsum('gqhe,gkhe->ghqk', query, keys, precision=finest_arithmetic) * HEAD_DIM ** (-0.5)
    key_live = (jnp.arange(SEQ)[None, :] < length_block[:, None])[:, None, None, :]
    probs = low(jax.nn.softmax(jnp.where(key_live, unnormalized_affinity, -1000000000.0), axis=-1))
    attended = jnp.einsum('ghqk,gkhe->gqhe', probs, values, precision=finest_arithmetic)
    attended = low(low_back(attended.reshape(token_block.shape + (D,))))
    branch = low_back(project(attended, out_matrix) + vectors[4])
    middle = layer_norm(normed + branch, vectors[5], vectors[6])
    lifted = low_back(project(low(middle), up_matrix) + vectors[10:14].reshape(FF))
    activated = low(exact_gelu(lifted))
    lowered = low_back(project(activated, down_matrix) + vectors[7])
    final = layer_norm(middle + lowered, vectors[8], vectors[9])
    return low(pool_unit(final, length_block))

def masked_lse(pairwise_affinity_matrix, allowed):
    masked = jnp.where(allowed, pairwise_affinity_matrix, -1000000000.0)
    top = lax.optimization_barrier(jnp.max(masked, -1, keepdims=True))
    total = lax.optimization_barrier(jnp.sum(jnp.where(allowed, jnp.exp(masked - top), 0.0), -1))
    return top[:, 0] + jnp.log(total)

def pair_loss(lexicon_vectors, valid, false_neg):
    pairwise_affinity_matrix = jnp.dot(lexicon_vectors[:, 0], lexicon_vectors[:, 1].T, precision=finest_arithmetic) / logit_divisor_constant
    number = pairwise_affinity_matrix.shape[0]
    identity_mask = jnp.arange(number)[:, None] == jnp.arange(number)[None, :]
    allowed = (valid[None, :] > 0) & ((false_neg == 0) | identity_mask)
    query_lse = masked_lse(pairwise_affinity_matrix, allowed)
    doc_lse = masked_lse(pairwise_affinity_matrix.T, allowed)
    weights_valid = valid.astype(jnp.float32)
    loss_sum = jnp.sum(weights_valid * (query_lse + doc_lse - 2.0 * jnp.diagonal(pairwise_affinity_matrix))) / 2.0
    pair_count = jnp.maximum(jnp.sum(weights_valid), 1.0)
    return (loss_sum, pair_count)

def reference(token_ids, lengths, valid, false_neg, word_table, qkv_weight, out_weight, up_weight, down_weight, word_master, qkv_master, out_master, up_master, down_master, word_moments, qkv_moments, out_moments, up_moments, down_moments, small_rows, small_moments):
    params = tuple((item.astype(jnp.float32) for item in (word_table, qkv_weight, out_weight, up_weight, down_weight))) + (small_rows,)
    seq_total = 2 * PAIRS
    group = math.gcd(seq_total, max(1, 4096 // SEQ))
    token_blocks = token_ids.reshape(seq_total // group, group, SEQ)
    length_blocks = lengths.reshape(seq_total // group, group)

    def objective(weights):
        encode_block = jax.checkpoint(lambda block: encode(weights, block[0], block[1]))
        lexicon_vectors = lax.map(encode_block, (token_blocks, length_blocks)).reshape(PAIRS, 2, D)
        loss_sum, pair_count = pair_loss(lexicon_vectors, valid, false_neg)
        return (loss_sum / pair_count, (loss_sum, pair_count))
    primal, backward, extras = jax.vjp(objective, params, has_aux=True)
    loss_sum, pair_count = extras
    grads, = backward(jnp.ones_like(primal))
    squares = jnp.sum(jnp.stack([jnp.sum(grad * grad) for grad in grads]))
    grad_norm = jnp.sqrt(squares)
    factor = clip_bound / jnp.maximum(grad_norm, clip_bound)
    parameter_replicas_full = (word_master, qkv_master, out_master, up_master, down_master, small_rows)
    moments = (word_moments, qkv_moments, out_moments, up_moments, down_moments, small_moments)
    results = []
    for grad, moment, master, rate in zip(grads, moments, parameter_replicas_full, rate_table):
        first, second, updated = adam_update(grad * factor, moment, master, rate)
        results.append(first)
        results.append(second)
        results.append(updated)
    return (loss_sum, pair_count, grad_norm, results[0], results[1], results[2], results[3], results[4], results[5], results[6], results[7], results[8], results[9], results[10], results[11], results[12], results[13], results[14], results[15], results[16], results[17])
```

```python
import jax
import jax.numpy as jnp
from jax import lax
from jax.sharding import PartitionSpec as P

HEADS = 12
STEP = 5


logit_divisor_constant = 0.01
clip_bound = 0.001
beta_first = 0.5
beta_second = 0.5
decay_weight = 0.01
epsilon = 1e-08
rate_table = (0.1, 0.02, 0.1, 0.02, 0.01, 0.2)
finest_arithmetic = lax.Precision.HIGHEST
both = ("blk", "grp")
strip = 384


def layer_norm(states, gain, shift):
    mean = jnp.mean(states, -1, keepdims=True)
    centered = states - mean
    variance = jnp.mean(centered * centered, -1, keepdims=True)
    return centered * lax.rsqrt(variance + 1e-06) * gain + shift


def exact_gelu(values):
    return jax.nn.gelu(values, approximate=False)


def pool_unit(states, lengths_flat):
    positions = jnp.arange(states.shape[1])
    weights = (positions[None, :] < lengths_flat[:, None]).astype(jnp.float32)
    pooled = jnp.sum(states * weights[:, :, None], 1) / lengths_flat[:, None].astype(jnp.float32)
    return pooled * lax.rsqrt(jnp.sum(pooled * pooled, -1, keepdims=True) + 1e-06)


def contract_rows(left, right):
    return lax.dot_general(
        left, right, (((0,), (0,)), ((), ())), preferred_element_type=jnp.float32
    )


def contract_cols(left, right):
    return lax.dot_general(
        left, right, (((1,), (1,)), ((), ())), preferred_element_type=jnp.float32
    )


def adam_update(grad, moments, master, rate):
    first = beta_first * moments[0] + (1.0 - beta_first) * grad
    second = beta_second * moments[1] + (1.0 - beta_second) * grad * grad
    first_hat = first / (1.0 - beta_first**STEP)
    second_hat = second / (1.0 - beta_second**STEP)
    updated = master - rate * (first_hat / (jnp.sqrt(second_hat) + epsilon) + decay_weight * master)
    return (first, second, updated)


def masked_softmax(pairwise_affinity_matrix, allowed):
    masked = jnp.where(allowed, pairwise_affinity_matrix, -1000000000.0)
    top = jnp.max(masked, -1, keepdims=True)
    expo = jnp.where(allowed, jnp.exp(masked - top), 0.0)
    total = jnp.sum(expo, -1, keepdims=True)
    return (top[:, 0] + jnp.log(total[:, 0]), expo / total)


class Place:
    def __init__(self):
        self.blk, self.grp = lax.axis_size("blk"), lax.axis_size("grp")
        self.count = self.blk * self.grp
        self.b, self.g = lax.axis_index("blk"), lax.axis_index("grp")
        self.xs, self.far = self.grp // 2, self.blk // 2
        self.core, self.x = self.g % 2, self.g // 2
        self.y, self.z = self.b % 2, self.b // 2
        self.core_masks = [0, 1]
        self.x_masks = [2 * i for i in range(self.xs)]
        self.y_masks = [0, self.grp]
        self.z_masks = [2 * self.grp * i for i in range(self.far)]

    def send(self, value, mask):
        pairs = [(i, i ^ mask) for i in range(self.count)]
        return lax.ppermute(value, both, pairs)


def in_order(pieces, index):
    step = 1
    while step < len(pieces):
        odd = (index & step) != 0
        pieces = [jnp.where(odd, pieces[i ^ step], pieces[i]) for i in range(len(pieces))]
        step *= 2
    return pieces


def gather_stage(place, value, masks, index):
    pieces = [value] + [place.send(value, mask) for mask in masks[1:]]
    return jnp.stack(in_order(pieces, index))


def gather_far_first(place, value):
    shape = value.shape
    value = gather_stage(place, value, place.z_masks, place.z)
    middle = [a + b for a in place.y_masks for b in place.x_masks]
    value = gather_stage(place, value, middle, place.y * place.xs + place.x)
    value = gather_stage(place, value, place.core_masks, place.core)
    value = value.reshape((2, 2, place.xs, place.far) + shape)
    return jnp.transpose(value, (3, 1, 2, 0) + tuple(range(4, 4 + len(shape)))).reshape(
        (place.blk, place.grp) + shape
    )


def reduce_stage(place, value, masks, index):
    total = lax.dynamic_index_in_dim(value, index, 0, keepdims=False)
    arrived = [
        place.send(lax.dynamic_index_in_dim(value, index ^ k, 0, keepdims=False), masks[k])
        for k in range(1, len(masks))
    ]
    terms = [total.astype(jnp.float32)] + [a.astype(jnp.float32) for a in arrived]
    while len(terms) > 1:
        terms = [terms[i] + terms[i + 1] for i in range(0, len(terms), 2)]
    return terms[0]


def reduce_rest(place, value, x_first):
    rows = value.shape[2]
    value = value.reshape(place.far, 2, place.xs, rows, value.shape[3])
    low = jnp.bfloat16
    if x_first:
        value = reduce_stage(
            place, jnp.moveaxis(value, 2, 0), place.x_masks, place.x
        ).astype(low)
        value = reduce_stage(
            place, jnp.moveaxis(value, 1, 0), place.y_masks, place.y
        ).astype(low)
    else:
        value = reduce_stage(
            place, jnp.moveaxis(value, 1, 0), place.y_masks, place.y
        ).astype(low)
        value = reduce_stage(
            place, jnp.moveaxis(value, 1, 0), place.x_masks, place.x
        ).astype(low)
    return reduce_stage(place, value, place.z_masks, place.z)


def half_gradient(place, left, right, core):
    width = right.shape[1] // 2
    part = lax.dynamic_slice_in_dim(right, core * width, width, 1)
    grad = contract_rows(left, part).astype(jnp.bfloat16)
    rows = grad.shape[0] // place.blk // place.xs
    strips = width // strip
    grad = grad.reshape(place.blk, place.xs, rows, strips, strip)
    return jnp.transpose(grad, (0, 1, 3, 2, 4)).reshape(
        place.blk, place.xs, strips * rows, strip
    )


def reduce_group(place, pairs, extra):
    mine = [half_gradient(place, a, b, place.core) for a, b in pairs]
    theirs = [half_gradient(place, a, b, 1 - place.core) for a, b in pairs]
    for item in extra:
        mine.append(lax.dynamic_index_in_dim(item, place.core, 2, keepdims=False))
        theirs.append(lax.dynamic_index_in_dim(item, 1 - place.core, 2, keepdims=False))
    mine, theirs = jnp.concatenate(mine, 2), jnp.concatenate(theirs, 2)
    arrived = place.send(theirs, 1)
    value = (mine.astype(jnp.float32) + arrived.astype(jnp.float32)).astype(jnp.bfloat16)
    cut = value.shape[2] // 32 * 16
    return jnp.concatenate(
        [
            reduce_rest(place, value[:, :, :cut], True),
            reduce_rest(place, value[:, :, cut:], False),
        ]
    )


def whole_rows(place, pieces, rows, width):
    strips = width // 2 // strip
    pieces = pieces.reshape(place.xs, 2, strips, rows, strip)
    return jnp.transpose(pieces, (0, 3, 1, 2, 4)).reshape(place.xs * rows, width)


def on_device(
    token_ids,
    lengths,
    valid,
    false_neg,
    word_table,
    qkv_weight,
    out_weight,
    up_weight,
    down_weight,
    word_master,
    qkv_master,
    out_master,
    up_master,
    down_master,
    word_moments,
    qkv_moments,
    out_moments,
    up_moments,
    down_moments,
    small_rows,
    small_moments,
):
    place = Place()
    pairs_here = token_ids.shape[0]
    total_pairs = pairs_here * place.count
    seq_count = 2 * pairs_here
    seq_len = token_ids.shape[2]
    width = word_table.shape[1]
    head_dim = width // HEADS
    scale = head_dim ** (-0.5)
    flat_ids = token_ids.reshape(-1)
    tokens = flat_ids.shape[0]
    lengths_flat = lengths.reshape(-1)
    vectors = small_rows[seq_len:]

    shard_rows = word_master.shape[0]
    table_rows = word_table.shape[0]
    per_owner = table_rows // shard_rows
    room = max(16, tokens // place.blk)
    shard = flat_ids // shard_rows
    same_id = flat_ids[:, None] == flat_ids[None, :]
    before = jnp.arange(tokens)[:, None] < jnp.arange(tokens)[None, :]
    first = ~jnp.any(same_id & before, 0)
    smaller = (
        (shard[:, None] == shard[None, :])
        & (flat_ids[None, :] < flat_ids[:, None])
        & first[None, :]
    )
    rank = jnp.sum(smaller.astype(jnp.int32), 1)
    slots = place.blk * room

    def slot_ids_of(round_number):
        at = rank - round_number * room
        slot = jnp.where((at >= 0) & (at < room), shard * room + at, slots)
        hit = slot[None, :] == jnp.arange(slots)[:, None]
        return jnp.max(jnp.where(hit, flat_ids[None, :], -1), 1)

    def lookup_slots(round_number):
        at = rank - round_number * room
        owner = shard // per_owner
        relative = ((owner ^ place.g) * per_owner + shard % per_owner) * room + at
        return jnp.where((at >= 0) & (at < room), relative, slots)

    def gradient_slots(round_number):
        at = rank - round_number * room
        relative = (shard ^ place.b) * room + at
        return jnp.where((at >= 0) & (at < room), relative, slots)

    def fetch(grp_ids, round_number):
        span = per_owner * room
        asked = [lax.dynamic_slice_in_dim(ids, place.g * span, span) for ids in grp_ids]
        local = jnp.concatenate(asked) - place.g * table_rows
        found = word_table.at[jnp.clip(local, 0, table_rows - 1)].get(mode="clip")
        parts = [found[k * span : (k + 1) * span] for k in range(place.grp)]
        rows = [parts[0]] + [place.send(parts[k], k) for k in range(1, place.grp)]
        rows = jnp.concatenate(rows)
        pick = lookup_slots(round_number)[:, None] == jnp.arange(slots)[None, :]
        return jnp.dot(pick.astype(jnp.bfloat16), rows, preferred_element_type=jnp.float32)

    def pack(values, length):
        return jnp.concatenate([values, jnp.zeros((length - values.shape[0],), values.dtype)])

    slot_ids = slot_ids_of(0)
    early = jnp.concatenate(
        [slot_ids, false_neg.reshape(-1), valid, jnp.max(rank)[None]]
    )
    early = pack(early, -(-early.shape[0] // 1024) * 1024).reshape(-1, 128)
    grp_early = [early] + [place.send(early, k) for k in range(1, place.grp)]
    grp_ids = [item.reshape(-1)[:slots] for item in grp_early]
    looked_up = fetch(grp_ids, 0)
    early_all = jnp.stack(in_order(grp_early, place.g))
    early_all = gather_stage(place, early_all, place.y_masks, place.y)
    early_all = gather_stage(place, early_all, place.z_masks, place.z)
    early_all = early_all.reshape(place.count, -1)
    ids_all = early_all[:, :slots]
    at = slots
    false_neg_all = early_all[:, at : at + pairs_here * total_pairs].reshape(
        total_pairs, total_pairs
    )
    at += pairs_here * total_pairs
    valid_all = early_all[:, at : at + pairs_here].reshape(-1)
    at += pairs_here
    rounds = jnp.max(early_all[:, at]) // room + 1

    def more_lookups(carry):
        number, held = carry
        ids = slot_ids_of(number)
        ids = [ids] + [place.send(ids, k) for k in range(1, place.grp)]
        return (number + 1, held + fetch(ids, number))

    _, looked_up = lax.while_loop(
        lambda carry: carry[0] < rounds, more_lookups, (jnp.int32(1), looked_up)
    )

    embedded = looked_up.reshape(seq_count, seq_len, width) + small_rows[:seq_len]
    normed, first_back = jax.vjp(layer_norm, embedded, vectors[0], vectors[1])
    normed_low = normed.reshape(-1, width).astype(jnp.bfloat16)
    qkv_bias = jnp.concatenate([vectors[2], jnp.zeros((width,), jnp.float32), vectors[3]])
    projected = (
        jnp.dot(normed_low, qkv_weight, preferred_element_type=jnp.float32) + qkv_bias
    ).astype(jnp.bfloat16)
    shape = (seq_count, seq_len, HEADS, head_dim)
    query = projected[:, :width].reshape(shape)
    keys = projected[:, width : 2 * width].reshape(shape)
    values = projected[:, 2 * width :].reshape(shape)
    key_live = (jnp.arange(seq_len)[None, :] < lengths_flat[:, None])[:, None, None, :]

    def masked_logits():
        unnormalized_affinity = (
            jnp.einsum("sqhe,skhe->shqk", query, keys, preferred_element_type=jnp.float32) * scale
        )
        return jnp.where(key_live, unnormalized_affinity, -1000000000.0)

    unnormalized_affinity = masked_logits()
    top = jnp.max(unnormalized_affinity, -1, keepdims=True)
    log_total = top + jnp.log(jnp.sum(jnp.exp(unnormalized_affinity - top), -1, keepdims=True))
    probs_low = jnp.exp(unnormalized_affinity - log_total).astype(jnp.bfloat16)
    attended = jnp.einsum("shqk,skhe->sqhe", probs_low, values, preferred_element_type=jnp.float32)
    attended = attended.reshape(-1, width).astype(jnp.bfloat16)
    branch = jnp.dot(attended, out_weight, preferred_element_type=jnp.float32) + vectors[4]
    middle, second_back = jax.vjp(
        layer_norm, normed.reshape(-1, width) + branch, vectors[5], vectors[6]
    )
    middle_low = middle.astype(jnp.bfloat16)
    lifted = jnp.dot(middle_low, up_weight, preferred_element_type=jnp.float32) + vectors[
        10:14
    ].reshape(-1)
    activated, gelu_back = jax.vjp(exact_gelu, lifted)
    activated_low = activated.astype(jnp.bfloat16)
    lowered = jnp.dot(activated_low, down_weight, preferred_element_type=jnp.float32) + vectors[7]
    final, third_back = jax.vjp(layer_norm, middle + lowered, vectors[8], vectors[9])
    unit, pool_back = jax.vjp(
        lambda states: pool_unit(states.reshape(seq_count, seq_len, width), lengths_flat), final
    )
    own_embed = unit.astype(jnp.bfloat16)

    gathered = gather_far_first(place, own_embed).reshape(total_pairs, 2, width)
    queries, documents = gathered[:, 0], gathered[:, 1]
    diagonal = jnp.arange(total_pairs)[:, None] == jnp.arange(total_pairs)[None, :]
    allowed = (valid_all[None, :] > 0) & ((false_neg_all == 0) | diagonal)
    scores = contract_cols(queries, documents) / logit_divisor_constant
    query_lse, query_probs = masked_softmax(scores, allowed)
    doc_lse, doc_probs = masked_softmax(scores.T, allowed)
    diag = jnp.sum(jnp.where(diagonal, scores, 0.0), -1)
    valid_floats = valid_all.astype(jnp.float32)
    pair_count = jnp.maximum(jnp.sum(valid_floats), 1.0)
    loss_total = jnp.sum(valid_floats * (query_lse + doc_lse - 2.0 * diag)) / 2.0
    row_weight = valid_floats / (2.0 * pair_count)
    identity_mask = diagonal.astype(jnp.float32)
    score_grad = (
        row_weight[:, None] * (query_probs - identity_mask)
        + (row_weight[:, None] * (doc_probs - identity_mask)).T
    )
    row_start = (place.b * place.grp + place.g) * pairs_here
    query_grad_rows = lax.dynamic_slice_in_dim(score_grad, row_start, pairs_here, 0)
    doc_grad_rows = lax.dynamic_slice_in_dim(score_grad, row_start, pairs_here, 1).T
    embed_grad = (
        jnp.stack(
            [
                jnp.dot(
                    query_grad_rows, documents.astype(jnp.float32), precision=finest_arithmetic
                ),
                jnp.dot(doc_grad_rows, queries.astype(jnp.float32), precision=finest_arithmetic),
            ],
            1,
        )
        / logit_divisor_constant
    )

    (final_grad,) = pool_back(embed_grad.reshape(seq_count, width))
    third_input_grad, third_gain_grad, third_shift_grad = third_back(final_grad)
    lowered_grad = third_input_grad.astype(jnp.bfloat16)
    down_bias_grad = jnp.sum(lowered_grad.astype(jnp.float32), 0)
    (lifted_grad,) = gelu_back(contract_cols(lowered_grad, down_weight))
    lifted_low = lifted_grad.astype(jnp.bfloat16)
    up_bias_grad = jnp.sum(lifted_low.astype(jnp.float32), 0)
    group_one = reduce_group(
        place, [(activated_low, lowered_grad), (middle_low, lifted_low)], []
    )
    middle_grad = third_input_grad + contract_cols(lifted_low, up_weight)
    second_input_grad, second_gain_grad, second_shift_grad = second_back(middle_grad)
    branch_grad = second_input_grad.astype(jnp.bfloat16)
    out_bias_grad = jnp.sum(branch_grad.astype(jnp.float32), 0)
    attended_grad = contract_cols(branch_grad, out_weight).astype(jnp.bfloat16).reshape(shape)
    probs = jnp.exp(masked_logits() - log_total)
    probs_low = probs.astype(jnp.bfloat16)
    probs_grad = jnp.einsum(
        "sqhe,skhe->shqk", attended_grad, values, preferred_element_type=jnp.float32
    )
    values_grad = jnp.einsum(
        "shqk,sqhe->skhe", probs_low, attended_grad, preferred_element_type=jnp.float32
    )
    logits_grad = probs * (probs_grad - jnp.sum(probs * probs_grad, -1, keepdims=True)) * scale
    logits_grad = logits_grad.astype(jnp.bfloat16)
    query_grad = jnp.einsum(
        "shqk,skhe->sqhe", logits_grad, keys, preferred_element_type=jnp.float32
    )
    keys_grad = jnp.einsum(
        "shqk,sqhe->skhe", logits_grad, query, preferred_element_type=jnp.float32
    )
    projected_grad = jnp.concatenate(
        [
            query_grad.reshape(-1, width),
            keys_grad.reshape(-1, width),
            values_grad.reshape(-1, width),
        ],
        1,
    ).astype(jnp.bfloat16)
    qkv_bias_grad = jnp.sum(projected_grad.astype(jnp.float32), 0)
    normed_grad = second_input_grad + contract_cols(projected_grad, qkv_weight)
    embedded_grad, first_gain_grad, first_shift_grad = first_back(
        normed_grad.reshape(seq_count, seq_len, width)
    )
    position_grad = jnp.sum(embedded_grad, 0)
    token_grads = embedded_grad.reshape(-1, width).astype(jnp.bfloat16)

    grid_ids = lax.dynamic_slice_in_dim(
        ids_all.reshape(place.blk, place.grp, place.blk, room), place.b, 1, 2
    )[:, :, 0]

    def word_rows_of(round_number, source_ids, held):
        hit = gradient_slots(round_number)[None, :] == jnp.arange(slots)[:, None]
        rows = jnp.dot(hit.astype(jnp.bfloat16), token_grads, preferred_element_type=jnp.float32)
        rows = rows.astype(jnp.bfloat16).reshape(place.blk, room, width)
        arrived = [rows[0]] + [
            place.send(rows[k], k * place.grp) for k in range(1, place.blk)
        ]
        arrived = jnp.concatenate(arrived)
        arrived = gather_stage(place, arrived, place.x_masks, place.x)
        arrived = gather_stage(place, arrived, place.core_masks, place.core)
        arrived = jnp.swapaxes(arrived, 0, 1).reshape(-1, width)
        ids = jnp.stack(in_order([source_ids[i] for i in range(place.blk)], place.b))
        local = jnp.swapaxes(ids, 0, 1).reshape(-1) - place.b * shard_rows
        inside = (local >= 0) & (local < shard_rows)
        return held.at[jnp.where(inside, local, shard_rows)].add(
            arrived.astype(jnp.float32), mode="drop"
        )

    word_rows = word_rows_of(0, grid_ids, jnp.zeros((shard_rows, width), jnp.float32))

    def more_rows(carry):
        number, held = carry
        ids = gather_far_first(place, slot_ids_of(number).reshape(place.blk, room))
        ids = lax.dynamic_index_in_dim(ids, place.b, 2, keepdims=False)
        return (number + 1, word_rows_of(number, ids, held))

    _, word_rows = lax.while_loop(
        lambda carry: carry[0] < rounds, more_rows, (jnp.int32(1), word_rows)
    )

    vector_grads = jnp.stack(
        [
            first_gain_grad,
            first_shift_grad,
            qkv_bias_grad[:width],
            qkv_bias_grad[2 * width :],
            out_bias_grad,
            second_gain_grad,
            second_shift_grad,
            down_bias_grad,
            third_gain_grad,
            third_shift_grad,
        ]
    )
    small_grad = jnp.concatenate([position_grad, vector_grads, up_bias_grad.reshape(-1, width)], 0)
    small_flat = small_grad.reshape(-1, strip)
    small_piece = -(-small_flat.shape[0] // (16 * place.count)) * 16
    small_padded = jnp.concatenate(
        [
            small_flat,
            jnp.zeros((small_piece * place.count - small_flat.shape[0], strip), jnp.float32),
        ]
    ).astype(jnp.bfloat16)
    small_parts = small_padded.reshape(place.blk, place.xs, 2, small_piece, strip)
    group_two = reduce_group(
        place, [(normed_low, projected_grad), (attended, branch_grad)], [small_parts]
    )
    cut = group_two.shape[0] - small_piece
    small_own = group_two[cut:]
    matrix_own = jnp.concatenate([group_one, group_two[:cut]]).astype(jnp.bfloat16)
    gathered_grads = gather_stage(place, matrix_own, place.x_masks, place.x)
    gathered_grads = gather_stage(place, gathered_grads, place.core_masks, place.core)
    gathered_grads = jnp.swapaxes(gathered_grads, 0, 1)
    masters = (down_master, up_master, qkv_master, out_master)
    shards, at = [], 0
    for master in masters:
        rows, columns = master.shape[0] // place.xs, master.shape[1]
        length = rows * (columns // 2 // strip)
        shards.append(
            whole_rows(place, gathered_grads[:, :, at : at + length], rows, columns).astype(
                jnp.float32
            )
        )
        at += length

    matrix_floats = matrix_own.astype(jnp.float32)
    squares = (
        jnp.sum(matrix_floats * matrix_floats)
        + jnp.sum(small_own * small_own)
        + jnp.sum(word_rows * word_rows) / place.grp
    )
    late = jnp.concatenate([small_own, jnp.full((8, strip), squares)])
    late = gather_far_first(place, late).reshape(place.count, -1, strip)
    small_total = late[:, :small_piece].reshape(-1, strip)[: small_flat.shape[0]]
    small_total = small_total.reshape(small_grad.shape)
    grad_norm = jnp.sqrt(jnp.sum(late[:, small_piece, 0]))
    factor = clip_bound / jnp.maximum(grad_norm, clip_bound)
    down_shard, up_shard, qkv_shard, out_shard = shards
    grads = (word_rows, qkv_shard, out_shard, up_shard, down_shard, small_total)
    parameters = (word_master, qkv_master, out_master, up_master, down_master, small_rows)
    moments = (word_moments, qkv_moments, out_moments, up_moments, down_moments, small_moments)
    results = []
    for grad, moment, master, rate in zip(grads, moments, parameters, rate_table):
        results.extend(adam_update(grad * factor, moment, master, rate))
    return (loss_total, pair_count, grad_norm, *results)


def solution(mesh):
    in_specs = (
        P(both, None, None),
        P(both, None),
        P(both),
        P(both, None),
        P("grp", None),
        P(),
        P(),
        P(),
        P(),
        P("blk", None),
        P("blk", None),
        P("blk", None),
        P("blk", None),
        P("blk", None),
        P(None, "blk", None),
        P(None, "blk", None),
        P(None, "blk", None),
        P(None, "blk", None),
        P(None, "blk", None),
        P(),
        P(),
    )
    out_specs = (P(), P(), P()) + (P("blk", None),) * 15 + (P(), P(), P())
    return jax.shard_map(
        on_device, mesh=mesh, in_specs=in_specs, out_specs=out_specs, check_vma=False
    )
```

```python
import functools

import jax
import jax.numpy as jnp
from jax import lax
from jax.experimental import pallas as pl
from jax.experimental.pallas import tpu as pltpu
from jax.sharding import PartitionSpec as P

HEADS = 12
STEP = 5


logit_divisor_constant = 0.01
clip_bound = 0.001
beta_first = 0.5
beta_second = 0.5
decay_weight = 0.01
epsilon = 1e-08
rate_table = (0.1, 0.02, 0.1, 0.02, 0.01, 0.2)
finest_arithmetic = lax.Precision.HIGHEST
both = ("blk", "grp")
strip = 384


def contract_rows(left, right):
    return lax.dot_general(
        left, right, (((0,), (0,)), ((), ())), preferred_element_type=jnp.float32
    )


def contract_cols(left, right):
    return lax.dot_general(
        left, right, (((1,), (1,)), ((), ())), preferred_element_type=jnp.float32
    )


def adam_update(grad, moments, master, rate):
    first = beta_first * moments[0] + (1.0 - beta_first) * grad
    second = beta_second * moments[1] + (1.0 - beta_second) * grad * grad
    first_hat = first / (1.0 - beta_first**STEP)
    second_hat = second / (1.0 - beta_second**STEP)
    updated = master - rate * (first_hat / (jnp.sqrt(second_hat) + epsilon) + decay_weight * master)
    return (first, second, updated)


def masked_softmax(pairwise_affinity_matrix, allowed):
    masked = jnp.where(allowed, pairwise_affinity_matrix, -1000000000.0)
    top = jnp.max(masked, -1, keepdims=True)
    expo = jnp.where(allowed, jnp.exp(masked - top), 0.0)
    total = jnp.sum(expo, -1, keepdims=True)
    return (top[:, 0] + jnp.log(total[:, 0]), expo / total)


VMEM_ALLOWED = 56 * 1024 * 1024
low = jnp.bfloat16


def whole_block(shape):
    return pl.BlockSpec(shape, lambda *_: (0,) * len(shape), pipeline_mode=pl.Buffered(1))


def rows_block(rows, columns):
    return pl.BlockSpec((rows, columns), lambda i, *_: (i, 0))


def normalize(states):
    mean = jnp.mean(states, -1, keepdims=True)
    centered = states - mean
    inverse = lax.rsqrt(jnp.mean(centered * centered, -1, keepdims=True) + 1e-06)
    return centered * inverse, inverse


def normalize_back(grad, gain, unit_states, inverse):
    scaled = grad * gain
    inner = jnp.mean(scaled * unit_states, -1, keepdims=True)
    back = inverse * (scaled - jnp.mean(scaled, -1, keepdims=True) - unit_states * inner)
    return back, jnp.sum(grad * unit_states, 0, keepdims=True), jnp.sum(grad, 0, keepdims=True)


def gelu_and_slope(values):
    size = jnp.abs(values) * 0.7071067811865476
    t = 1.0 / (1.0 + 0.3275911 * size)
    series = t * (
        0.254829592
        + t * (-0.284496736 + t * (1.421413741 + t * (-1.453152027 + t * 1.061405429)))
    )
    bell = jnp.exp(-size * size)
    tail = 0.5 * series * bell
    below = jnp.where(values >= 0.0, 1.0 - tail, tail)
    return values * below, below + values * (0.3989422804014327 * bell)


def dot_rows(left, right):
    return lax.dot_general(
        left, right, (((0,), (0,)), ((), ())), preferred_element_type=jnp.float32
    )


def dot_cols(left, right):
    return lax.dot_general(
        left, right, (((1,), (1,)), ((), ())), preferred_element_type=jnp.float32
    )


def dot_plain(left, right):
    return jnp.dot(left, right, preferred_element_type=jnp.float32)


def head_masks(lanes, head_dim):
    even = (lax.broadcasted_iota(jnp.int32, (1, lanes), 1) < head_dim).astype(low)
    return even, (1.0 - even.astype(jnp.float32)).astype(low)


def forward_kernel(
    lengths_ref,
    slots_ref,
    found_ref,
    small_ref,
    qkv_ref,
    out_ref,
    up_ref,
    down_ref,
    unit1_ref,
    inverse1_ref,
    normed_ref,
    projected_ref,
    probs_ref,
    attended_ref,
    unit2_ref,
    inverse2_ref,
    middle_ref,
    activated_ref,
    slope_ref,
    unit3_ref,
    inverse3_ref,
    pooled_ref,
    embed_ref,
    *,
    seq_len,
    seqs,
    head_dim,
):
    step = pl.program_id(0)
    width = found_ref.shape[1]
    rows = seqs * seq_len
    slots = found_ref.shape[0]

    def vector(index):
        return small_ref[seq_len + index : seq_len + index + 1, :]

    pick = slots_ref[...] == lax.broadcasted_iota(jnp.int32, (rows, slots), 1)
    pick = jnp.where(pick, 1.0, 0.0).astype(low)
    embedded = dot_plain(pick, found_ref[...])
    positions = small_ref[:seq_len, :]
    embedded = embedded + jnp.concatenate([positions] * seqs, 0)
    unit1, inverse1 = normalize(embedded)
    unit1_ref[...] = unit1
    inverse1_ref[...] = inverse1
    normed = unit1 * vector(0) + vector(1)
    normed_low = normed.astype(low)
    normed_ref[...] = normed_low
    zeros = jnp.zeros((1, width), jnp.float32)
    for part, bias in enumerate((vector(2), zeros, vector(3))):
        at = slice(part * width, (part + 1) * width)
        projected_ref[:, at] = (dot_plain(normed_low, qkv_ref[:, at]) + bias).astype(low)
    lanes = 2 * head_dim
    even, odd = head_masks(lanes, head_dim)
    key_at = lax.broadcasted_iota(jnp.int32, (2 * seq_len, seq_len), 1)
    for s in range(seqs):
        at = slice(s * seq_len, (s + 1) * seq_len)
        live = key_at < lengths_ref[step * seqs + s]
        for p in range(width // lanes):
            query = projected_ref[at, p * lanes : (p + 1) * lanes]
            keys = projected_ref[at, width + p * lanes : width + (p + 1) * lanes]
            values = projected_ref[at, 2 * width + p * lanes : 2 * width + (p + 1) * lanes]
            query = jnp.concatenate([query * even, query * odd], 0)
            logits = dot_cols(query, keys) * head_dim ** (-0.5)
            logits = jnp.where(live, logits, -1000000000.0)
            expo = jnp.exp(logits - jnp.max(logits, -1, keepdims=True))
            probs = (expo / jnp.sum(expo, -1, keepdims=True)).astype(low)
            probs_ref[s, p] = probs
            both_probs = jnp.concatenate([probs[:seq_len], probs[seq_len:]], 1)
            both_values = jnp.concatenate([values * even, values * odd], 0)
            attended_ref[at, p * lanes : (p + 1) * lanes] = dot_plain(
                both_probs, both_values
            ).astype(low)
    branch = dot_plain(attended_ref[...], out_ref[...]) + vector(4)
    unit2, inverse2 = normalize(normed + branch)
    unit2_ref[...] = unit2
    inverse2_ref[...] = inverse2
    middle = unit2 * vector(5) + vector(6)
    middle_low = middle.astype(low)
    middle_ref[...] = middle_low
    lowered = middle + vector(7)
    for j in range(up_ref.shape[1] // width):
        at = slice(j * width, (j + 1) * width)
        lifted = dot_plain(middle_low, up_ref[:, at]) + vector(10 + j)
        activated, slope = gelu_and_slope(lifted)
        activated = activated.astype(low)
        activated_ref[:, at] = activated
        slope_ref[:, at] = slope.astype(low)
        lowered = lowered + dot_plain(activated, down_ref[at, :])
    unit3, inverse3 = normalize(lowered)
    unit3_ref[...] = unit3
    inverse3_ref[...] = inverse3
    final = unit3 * vector(8) + vector(9)
    row_at = lax.broadcasted_iota(jnp.int32, (seq_len, 1), 0)
    pooled = []
    for s in range(seqs):
        length = lengths_ref[step * seqs + s]
        weights = (row_at < length).astype(jnp.float32)
        total = jnp.sum(final[s * seq_len : (s + 1) * seq_len] * weights, 0, keepdims=True)
        pooled.append(total / length.astype(jnp.float32))
    pooled = jnp.concatenate(pooled, 0)
    pooled_ref[0] = pooled
    squares = jnp.sum(pooled * pooled, -1, keepdims=True)
    embed_ref[0] = (pooled * lax.rsqrt(squares + 1e-06)).astype(low)


def forward(lengths_flat, slot, found, small_rows, weights, seq_len, head_dim):
    tokens, width = slot.shape[0], found.shape[1]
    seqs = 2
    rows = seqs * seq_len
    steps = tokens // rows
    lifted = weights[2].shape[1]
    f32 = jnp.float32
    outs = [
        ((tokens, width), f32),
        ((tokens, 1), f32),
        ((tokens, width), low),
        ((tokens, 3 * width), low),
        ((steps * seqs, width // (2 * head_dim), 2 * seq_len, seq_len), low),
        ((tokens, width), low),
        ((tokens, width), f32),
        ((tokens, 1), f32),
        ((tokens, width), low),
        ((tokens, lifted), low),
        ((tokens, lifted), low),
        ((tokens, width), f32),
        ((tokens, 1), f32),
        ((steps, seqs, width), f32),
        ((steps, seqs, width), low),
    ]

    def spec(shape):
        if shape[0] == tokens:
            return rows_block(rows, shape[1])
        block = (shape[0] // steps,) + shape[1:]
        return pl.BlockSpec(block, lambda i, *_: (i,) + (0,) * (len(shape) - 1))

    return pl.pallas_call(
        functools.partial(forward_kernel, seq_len=seq_len, seqs=seqs, head_dim=head_dim),
        out_shape=[jax.ShapeDtypeStruct(*item) for item in outs],
        grid_spec=pltpu.PrefetchScalarGridSpec(
            num_scalar_prefetch=1,
            grid=(steps,),
            in_specs=[rows_block(rows, 1), whole_block(found.shape), whole_block(small_rows.shape)]
            + [whole_block(item.shape) for item in weights],
            out_specs=[spec(item[0]) for item in outs],
        ),
        compiler_params=pltpu.CompilerParams(vmem_limit_bytes=VMEM_ALLOWED),
        cost_estimate=pl.CostEstimate(
            flops=20 * 10**9, bytes_accessed=50 * 10**6, transcendentals=10**7
        ),
        name="encoder_forward",
    )(lengths_flat, slot, found, small_rows, *weights)


def feed_back_kernel(
    lengths_ref,
    embed_grad_ref,
    pooled_ref,
    small_ref,
    unit3_ref,
    inverse3_ref,
    slope_ref,
    unit2_ref,
    inverse2_ref,
    up_ref,
    down_ref,
    lowered_ref,
    lifted_ref,
    second_ref,
    sums_ref,
    *,
    seq_len,
    seqs,
):
    step = pl.program_id(0)
    width = unit3_ref.shape[1]

    @pl.when(step == 0)
    def _():
        sums_ref[...] = jnp.zeros_like(sums_ref)

    def vector(index):
        return small_ref[seq_len + index : seq_len + index + 1, :]

    pooled, grad = pooled_ref[0], embed_grad_ref[0]
    inverse = lax.rsqrt(jnp.sum(pooled * pooled, -1, keepdims=True) + 1e-06)
    inner = jnp.sum(pooled * grad, -1, keepdims=True)
    pooled_grad = inverse * (grad - pooled * (inverse * inverse * inner))
    row_at = lax.broadcasted_iota(jnp.int32, (seq_len, 1), 0)
    final_grad = []
    for s in range(seqs):
        length = lengths_ref[step * seqs + s]
        weights = (row_at < length).astype(jnp.float32)
        final_grad.append(weights * (pooled_grad[s : s + 1] / length.astype(jnp.float32)))
    final_grad = jnp.concatenate(final_grad, 0)
    third, gain3, shift3 = normalize_back(
        final_grad, vector(8), unit3_ref[...], inverse3_ref[...]
    )
    lowered_grad = third.astype(low)
    lowered_ref[...] = lowered_grad
    middle_grad = third
    up_sums = []
    for j in range(up_ref.shape[1] // width):
        at = slice(j * width, (j + 1) * width)
        grad = dot_cols(lowered_grad, down_ref[at, :]) * slope_ref[:, at].astype(jnp.float32)
        grad = grad.astype(low)
        lifted_ref[:, at] = grad
        up_sums.append(jnp.sum(grad.astype(jnp.float32), 0, keepdims=True))
        middle_grad = middle_grad + dot_cols(grad, up_ref[:, at])
    second, gain2, shift2 = normalize_back(
        middle_grad, vector(5), unit2_ref[...], inverse2_ref[...]
    )
    second_ref[...] = second
    branch_sum = jnp.sum(second.astype(low).astype(jnp.float32), 0, keepdims=True)
    lowered_sum = jnp.sum(lowered_grad.astype(jnp.float32), 0, keepdims=True)
    sums = [branch_sum, gain2, shift2, lowered_sum, gain3, shift3] + up_sums
    sums_ref[: len(sums), :] += jnp.concatenate(sums, 0)


def feed_back(lengths_flat, embed_grad, kept, small_rows, weights, seq_len):
    unit2, inverse2, slope, unit3, inverse3, pooled = kept
    tokens, width = unit2.shape
    lifted = slope.shape[1]
    seqs = 2
    rows = seqs * seq_len
    steps = tokens // rows
    pair = pl.BlockSpec((1, seqs, width), lambda i, *_: (i, 0, 0))
    return pl.pallas_call(
        functools.partial(feed_back_kernel, seq_len=seq_len, seqs=seqs),
        out_shape=[
            jax.ShapeDtypeStruct((tokens, width), low),
            jax.ShapeDtypeStruct((tokens, lifted), low),
            jax.ShapeDtypeStruct((tokens, width), jnp.float32),
            jax.ShapeDtypeStruct((16, width), jnp.float32),
        ],
        grid_spec=pltpu.PrefetchScalarGridSpec(
            num_scalar_prefetch=1,
            grid=(steps,),
            in_specs=[
                pair,
                pair,
                whole_block(small_rows.shape),
                rows_block(rows, width),
                rows_block(rows, 1),
                rows_block(rows, lifted),
                rows_block(rows, width),
                rows_block(rows, 1),
                whole_block(weights[0].shape),
                whole_block(weights[1].shape),
            ],
            out_specs=[
                rows_block(rows, width),
                rows_block(rows, lifted),
                rows_block(rows, width),
                pl.BlockSpec((16, width), lambda i, *_: (0, 0)),
            ],
        ),
        compiler_params=pltpu.CompilerParams(vmem_limit_bytes=VMEM_ALLOWED),
        cost_estimate=pl.CostEstimate(
            flops=10 * 10**9, bytes_accessed=40 * 10**6, transcendentals=0
        ),
        name="feed_back",
    )(
        lengths_flat,
        embed_grad,
        pooled,
        small_rows,
        unit3,
        inverse3,
        slope,
        unit2,
        inverse2,
        *weights,
    )


def attention_back_kernel(
    slots_ref,
    second_ref,
    projected_ref,
    probs_ref,
    unit1_ref,
    inverse1_ref,
    small_ref,
    qkv_ref,
    out_ref,
    branch_ref,
    projected_grad_ref,
    rows_ref,
    positions_ref,
    sums_ref,
    total_ref,
    *,
    seq_len,
    seqs,
    head_dim,
):
    step = pl.program_id(0)
    width = second_ref.shape[1]
    lanes = 2 * head_dim
    scale = head_dim ** (-0.5)

    @pl.when(step == 0)
    def _():
        sums_ref[...] = jnp.zeros_like(sums_ref)
        positions_ref[...] = jnp.zeros_like(positions_ref)
        total_ref[...] = jnp.zeros_like(total_ref)

    second = second_ref[...]
    branch = second.astype(low)
    branch_ref[...] = branch
    attended_grad = dot_cols(branch, out_ref[...]).astype(low)
    even, odd = head_masks(lanes, head_dim)
    for s in range(seqs):
        at = slice(s * seq_len, (s + 1) * seq_len)
        for p in range(width // lanes):
            here = slice(p * lanes, (p + 1) * lanes)
            there = slice(width + p * lanes, width + (p + 1) * lanes)
            yonder = slice(2 * width + p * lanes, 2 * width + (p + 1) * lanes)
            query = projected_ref[at, here]
            keys = projected_ref[at, there]
            values = projected_ref[at, yonder]
            grad = attended_grad[at, here]
            grad = jnp.concatenate([grad * even, grad * odd], 0)
            query = jnp.concatenate([query * even, query * odd], 0)
            keys = jnp.concatenate([keys * even, keys * odd], 0)
            probs_low = probs_ref[s, p]
            probs = probs_low.astype(jnp.float32)
            probs_grad = dot_cols(grad, values)
            weighted = probs * probs_grad
            inner = jnp.sum(weighted, -1, keepdims=True)
            logits_grad = ((weighted - probs * inner) * scale).astype(low)
            both_grads = jnp.concatenate([logits_grad[:seq_len], logits_grad[seq_len:]], 1)
            projected_grad_ref[at, here] = dot_plain(both_grads, keys).astype(low)
            projected_grad_ref[at, there] = dot_rows(logits_grad, query).astype(low)
            projected_grad_ref[at, yonder] = dot_rows(probs_low, grad).astype(low)
    projected_grad = projected_grad_ref[...]
    query_sum = jnp.sum(projected_grad[:, :width].astype(jnp.float32), 0, keepdims=True)
    value_sum = jnp.sum(projected_grad[:, 2 * width :].astype(jnp.float32), 0, keepdims=True)
    normed_grad = second + dot_cols(projected_grad, qkv_ref[...])
    gain = small_ref[seq_len : seq_len + 1, :]
    embedded_grad, gain1, shift1 = normalize_back(
        normed_grad, gain, unit1_ref[...], inverse1_ref[...]
    )
    for s in range(seqs):
        positions_ref[...] += embedded_grad[s * seq_len : (s + 1) * seq_len]
    sums_ref[:4, :] += jnp.concatenate([gain1, shift1, query_sum, value_sum], 0)
    slots, rows = total_ref.shape[0], seqs * seq_len
    hit = slots_ref[0] == lax.broadcasted_iota(jnp.int32, (slots, rows), 0)
    hit = jnp.where(hit, 1.0, 0.0).astype(low)
    total_ref[...] += dot_plain(hit, embedded_grad.astype(low))

    @pl.when(step == pl.num_programs(0) - 1)
    def _():
        rows_ref[...] = total_ref[...].astype(low)


def attention_back(slot, second, kept, small_rows, weights, seq_len, head_dim, slots):
    projected, probs, unit1, inverse1 = kept
    tokens, width = second.shape
    seqs = 2
    rows = seqs * seq_len
    steps = tokens // rows
    probs_block = (seqs,) + probs.shape[1:]

    def fixed(shape):
        return pl.BlockSpec(shape, lambda i, *_: (0, 0))

    return pl.pallas_call(
        functools.partial(
            attention_back_kernel, seq_len=seq_len, seqs=seqs, head_dim=head_dim
        ),
        out_shape=[
            jax.ShapeDtypeStruct((tokens, width), low),
            jax.ShapeDtypeStruct((tokens, 3 * width), low),
            jax.ShapeDtypeStruct((slots, width), low),
            jax.ShapeDtypeStruct((seq_len, width), jnp.float32),
            jax.ShapeDtypeStruct((8, width), jnp.float32),
        ],
        grid=(steps,),
        in_specs=[
            pl.BlockSpec((1, 1, rows), lambda i: (i, 0, 0)),
            rows_block(rows, width),
            rows_block(rows, 3 * width),
            pl.BlockSpec(probs_block, lambda i: (i, 0, 0, 0)),
            rows_block(rows, width),
            rows_block(rows, 1),
            whole_block(small_rows.shape),
            whole_block(weights[0].shape),
            whole_block(weights[1].shape),
        ],
        out_specs=[
            rows_block(rows, width),
            rows_block(rows, 3 * width),
            fixed((slots, width)),
            fixed((seq_len, width)),
            fixed((8, width)),
        ],
        scratch_shapes=[pltpu.VMEM((slots, width), jnp.float32)],
        compiler_params=pltpu.CompilerParams(vmem_limit_bytes=VMEM_ALLOWED),
        cost_estimate=pl.CostEstimate(
            flops=10 * 10**9, bytes_accessed=30 * 10**6, transcendentals=0
        ),
        name="attention_back",
    )(slot.reshape(steps, 1, rows), second, projected, probs, unit1, inverse1, small_rows, *weights)


def weight_grad_kernel(core_ref, *refs, jobs, xs):
    theirs_ref, mine_ref, turned_ref = refs[-3:]
    step = pl.program_id(0)
    start, base = 0, 0
    for n, (tiles, tall, piece, strips) in enumerate(jobs):
        left_ref, right_ref = refs[2 * n], refs[2 * n + 1]

        def work(start=start, base=base, left_ref=left_ref, right_ref=right_ref, job=jobs[n]):
            tiles, tall, piece, strips = job
            tile = step - start
            if tall or tiles == 1:
                grad = dot_rows(left_ref[...], right_ref[...])
            else:

                @pl.when(tile == 0)
                def _():
                    turned_ref[...] = left_ref[...].T

                grad = dot_plain(turned_ref[...], right_ref[...])
            count = grad.shape[0] // piece // xs
            for j in range(2):
                part = grad[:, j * strip : (j + 1) * strip]
                part = part.reshape(count, xs, piece, strip)
                if tall:
                    half = j
                    at = (pl.ds(tile * count, count), slice(None), pl.ds(base, piece))
                else:
                    number = 2 * tile + j
                    half = number // strips
                    row = pl.multiple_of(base + (number % strips) * piece, 16)
                    at = (slice(None), slice(None), pl.ds(row, piece))

                @pl.when(core_ref[0] == half)
                def _(at=at, part=part):
                    mine_ref[at] = part

                @pl.when(core_ref[0] != half)
                def _(at=at, part=part):
                    theirs_ref[at] = part.astype(low)

        pl.when((step >= start) & (step < start + tiles))(work)
        start += tiles
        base += piece * strips


def weight_grads(place, pairs):
    tile_rows = 2 * strip
    jobs, in_specs, operands = [], [], []
    start, rows = 0, 0
    tokens = pairs[0][0].shape[0]
    for left, right in pairs:
        strips = right.shape[1] // 2 // strip
        tall = left.shape[1] > tile_rows
        tiles = left.shape[1] // tile_rows if tall else strips
        piece = left.shape[1] // place.blk // place.xs

        def tile_of(i, start=start, tiles=tiles):
            return jnp.clip(i - start, 0, tiles - 1)

        def block(varies, f=tile_of):
            if varies:
                return pl.BlockSpec((tokens, tile_rows), lambda i, h: (0, f(i)))
            return whole_block((tokens, tile_rows))

        in_specs += [block(tall), block(not tall and tiles > 1)]
        jobs.append((tiles, tall, piece, strips))
        operands += [left, right]
        start += tiles
        rows += piece * strips
    shape = (place.blk, place.xs, rows, strip)
    return pl.pallas_call(
        functools.partial(weight_grad_kernel, jobs=jobs, xs=place.xs),
        out_shape=[
            jax.ShapeDtypeStruct(shape, low),
            jax.ShapeDtypeStruct(shape, jnp.float32),
        ],
        grid_spec=pltpu.PrefetchScalarGridSpec(
            num_scalar_prefetch=1,
            grid=(start,),
            in_specs=in_specs,
            out_specs=[whole_block(shape), whole_block(shape)],
            scratch_shapes=[pltpu.VMEM((tile_rows, tokens), low)],
        ),
        compiler_params=pltpu.CompilerParams(vmem_limit_bytes=VMEM_ALLOWED),
        cost_estimate=pl.CostEstimate(
            flops=start * 2 * tokens * tile_rows * tile_rows,
            bytes_accessed=16 * 10**6,
            transcendentals=0,
        ),
        name="weight_grads",
    )(place.core.reshape(1).astype(jnp.int32), *operands)


def word_sum_kernel(place_ref, count_ref, id_ref, *refs, grp, blk, room, span):
    sources = refs[:grp]
    out_ref, squares_ref, total_ref, rows_ref, chunk_ref, in_sems, out_sem = refs[grp:]
    batch = 8
    copies = [
        pltpu.make_async_copy(sources[k], rows_ref.at[k], in_sems.at[k]) for k in range(grp)
    ]
    for copy in copies:
        copy.start()
    zeros = jnp.zeros((batch, total_ref.shape[1]), jnp.float32)

    def clear(i, _):
        total_ref[pl.ds(pl.multiple_of(i * batch, batch), batch), :] = zeros
        return 0

    lax.fori_loop(0, total_ref.shape[0] // batch, clear, 0, unroll=4)
    for copy in copies:
        copy.wait()

    def one_source(n, _):
        slot = (n // blk) ^ place_ref[0]
        start = (n % blk) * room
        count = count_ref[n]

        def widen(i, _):
            at = pl.ds(pl.multiple_of(start + i * 16, 16), 16)
            to = pl.ds(pl.multiple_of(i * 16, 16), 16)
            chunk_ref[to, :] = rows_ref[slot, at, :].astype(jnp.float32)
            return 0

        lax.fori_loop(0, (count + 15) // 16, widen, 0)

        def add(i, _):
            at = [id_ref[n * room + i * batch + j] for j in range(batch)]
            sums = [
                total_ref[pl.ds(at[j], 1), :] + chunk_ref[pl.ds(i * batch + j, 1), :]
                for j in range(batch)
            ]
            for j in range(batch):
                total_ref[pl.ds(at[j], 1), :] = sums[j]
            return 0

        lax.fori_loop(0, (count + batch - 1) // batch, add, 0)
        return 0

    lax.fori_loop(0, grp * blk, one_source, 0)
    shard_rows = out_ref.shape[0]

    def finish(i, squares):
        at = pl.ds(pl.multiple_of(i * span, span), span)
        part = total_ref[at, :]
        pltpu.make_async_copy(total_ref.at[at], out_ref.at[at], out_sem).start()
        part = part * part
        return squares + jnp.sum(part.reshape(span // 8, 8, part.shape[1]), 0)

    squares = lax.fori_loop(
        0, shard_rows // span, finish, jnp.zeros((8, total_ref.shape[1]), jnp.float32)
    )
    squares_ref[...] = jnp.sum(squares, 0, keepdims=True)
    pltpu.make_async_copy(total_ref.at[pl.ds(0, shard_rows)], out_ref, out_sem).wait()


def word_sum(grp_index, counts, ids, sources, shard_rows, blk, room):
    grp, width = len(sources), sources[0].shape[1]
    span = next(size for size in (128, 64, 32, 16, 8) if shard_rows % size == 0)
    anywhere = pl.BlockSpec(memory_space=pl.ANY)
    return pl.pallas_call(
        functools.partial(word_sum_kernel, grp=grp, blk=blk, room=room, span=span),
        out_shape=[
            jax.ShapeDtypeStruct((shard_rows, width), jnp.float32),
            jax.ShapeDtypeStruct((1, width), jnp.float32),
        ],
        grid_spec=pltpu.PrefetchScalarGridSpec(
            num_scalar_prefetch=3,
            grid=(1,),
            in_specs=[anywhere] * grp,
            out_specs=[anywhere, whole_block((1, width))],
            scratch_shapes=[
                pltpu.VMEM((shard_rows + 32, width), jnp.float32),
                pltpu.VMEM((grp,) + sources[0].shape, low),
                pltpu.VMEM((room, width), jnp.float32),
                pltpu.SemaphoreType.DMA((grp,)),
                pltpu.SemaphoreType.DMA,
            ],
        ),
        compiler_params=pltpu.CompilerParams(vmem_limit_bytes=VMEM_ALLOWED),
        cost_estimate=pl.CostEstimate(
            flops=10**7, bytes_accessed=40 * 10**6, transcendentals=0
        ),
        name="word_sum",
    )(grp_index.reshape(1), counts, ids, *sources)


class Place:
    def __init__(self):
        self.blk, self.grp = lax.axis_size("blk"), lax.axis_size("grp")
        self.count = self.blk * self.grp
        self.b, self.g = lax.axis_index("blk"), lax.axis_index("grp")
        self.xs, self.far = self.grp // 2, self.blk // 2
        self.core, self.x = self.g % 2, self.g // 2
        self.y, self.z = self.b % 2, self.b // 2
        self.core_masks = [0, 1]
        self.x_masks = [2 * i for i in range(self.xs)]
        self.y_masks = [0, self.grp]
        self.z_masks = [2 * self.grp * i for i in range(self.far)]

    def send(self, value, mask):
        pairs = [(i, i ^ mask) for i in range(self.count)]
        return lax.ppermute(value, both, pairs)


def in_order(pieces, index):
    step = 1
    while step < len(pieces):
        odd = (index & step) != 0
        pieces = [jnp.where(odd, pieces[i ^ step], pieces[i]) for i in range(len(pieces))]
        step *= 2
    return pieces


def gather_stage(place, value, masks, index):
    pieces = [value] + [place.send(value, mask) for mask in masks[1:]]
    return jnp.stack(in_order(pieces, index))


def gather_far_first(place, value):
    shape = value.shape
    value = gather_stage(place, value, place.z_masks, place.z)
    middle = [a + b for a in place.y_masks for b in place.x_masks]
    value = gather_stage(place, value, middle, place.y * place.xs + place.x)
    value = gather_stage(place, value, place.core_masks, place.core)
    value = value.reshape((2, 2, place.xs, place.far) + shape)
    return jnp.transpose(value, (3, 1, 2, 0) + tuple(range(4, 4 + len(shape)))).reshape(
        (place.blk, place.grp) + shape
    )


def to_send(value, fine):
    high = value.astype(low)
    if not fine:
        return high
    rows = value.shape[-2]
    rest = value[..., rows - fine :, :] - high[..., rows - fine :, :].astype(jnp.float32)
    return jnp.concatenate([high, rest.astype(low)], -2)


def from_sent(value, fine):
    value = value.astype(jnp.float32)
    if not fine:
        return value
    rows = value.shape[-2] - fine
    tail = value[..., rows - fine : rows, :] + value[..., rows:, :]
    return jnp.concatenate([value[..., : rows - fine, :], tail], -2)


def reduce_stage(place, value, masks, index, fine):
    terms = [lax.dynamic_index_in_dim(value, index, 0, keepdims=False).astype(jnp.float32)]
    for k in range(1, len(masks)):
        part = lax.dynamic_index_in_dim(value, index ^ k, 0, keepdims=False)
        terms.append(from_sent(place.send(to_send(part, fine), masks[k]), fine))
    while len(terms) > 1:
        terms = [terms[i] + terms[i + 1] for i in range(0, len(terms), 2)]
    return terms[0]


def reduce_rest(place, value, x_first, fine):
    rows = value.shape[2]
    value = value.reshape(place.far, 2, place.xs, rows, value.shape[3])
    if x_first:
        value = jnp.moveaxis(value, 2, 0)
        value = reduce_stage(place, value, place.x_masks, place.x, fine)
        value = jnp.moveaxis(value, 1, 0)
        value = reduce_stage(place, value, place.y_masks, place.y, fine)
    else:
        value = jnp.moveaxis(value, 1, 0)
        value = reduce_stage(place, value, place.y_masks, place.y, fine)
        value = jnp.moveaxis(value, 1, 0)
        value = reduce_stage(place, value, place.x_masks, place.x, fine)
    return reduce_stage(place, value, place.z_masks, place.z, fine)


def half_gradient(place, left, right, core):
    width = right.shape[1] // 2
    part = lax.dynamic_slice_in_dim(right, core * width, width, 1)
    grad = contract_rows(left, part).astype(jnp.bfloat16)
    rows = grad.shape[0] // place.blk // place.xs
    strips = width // strip
    grad = grad.reshape(place.blk, place.xs, rows, strips, strip)
    return jnp.transpose(grad, (0, 1, 3, 2, 4)).reshape(
        place.blk, place.xs, strips * rows, strip
    )


def reduce_group(place, pairs, extra):
    if all(a.shape[1] % (16 * place.blk * place.xs) == 0 for a, _ in pairs):
        theirs, mine = weight_grads(place, pairs)
    else:
        mine = [half_gradient(place, a, b, place.core) for a, b in pairs]
        theirs = [half_gradient(place, a, b, 1 - place.core) for a, b in pairs]
        mine, theirs = jnp.concatenate(mine, 2), jnp.concatenate(theirs, 2)
    fine = 0
    if extra is not None:
        fine = extra.shape[3]
        own = lax.dynamic_index_in_dim(extra, place.core, 2, keepdims=False)
        mine = jnp.concatenate([mine.astype(jnp.float32), own], 2)
        other = lax.dynamic_index_in_dim(extra, 1 - place.core, 2, keepdims=False)
        theirs = jnp.concatenate([theirs, to_send(other, fine)], 2)
    arrived = from_sent(place.send(theirs, 1), fine)
    return mine.astype(jnp.float32) + arrived, fine


def reduce_group_rest(place, value, fine):
    cut = value.shape[2] // 32 * 16
    return jnp.concatenate(
        [
            reduce_rest(place, value[:, :, :cut], True, 0),
            reduce_rest(place, value[:, :, cut:], False, fine),
        ]
    )


def whole_rows(place, pieces, rows, width):
    strips = width // 2 // strip
    pieces = pieces.reshape(place.xs, 2, strips, rows, strip)
    return jnp.transpose(pieces, (0, 3, 1, 2, 4)).reshape(place.xs * rows, width)


def on_device(
    token_ids,
    lengths,
    valid,
    false_neg,
    word_table,
    qkv_weight,
    out_weight,
    up_weight,
    down_weight,
    word_master,
    qkv_master,
    out_master,
    up_master,
    down_master,
    word_moments,
    qkv_moments,
    out_moments,
    up_moments,
    down_moments,
    small_rows,
    small_moments,
):
    place = Place()
    pairs_here = token_ids.shape[0]
    total_pairs = pairs_here * place.count
    seq_count = 2 * pairs_here
    seq_len = token_ids.shape[2]
    width = word_table.shape[1]
    head_dim = width // HEADS
    flat_ids = token_ids.reshape(-1)
    tokens = flat_ids.shape[0]
    lengths_flat = lengths.reshape(-1)

    shard_rows = word_master.shape[0]
    table_rows = word_table.shape[0]
    per_owner = table_rows // shard_rows
    room = max(16, tokens // place.blk)
    shard = flat_ids // shard_rows
    same_id = flat_ids[:, None] == flat_ids[None, :]
    before = jnp.arange(tokens)[:, None] < jnp.arange(tokens)[None, :]
    first = ~jnp.any(same_id & before, 0)
    smaller = (
        (shard[:, None] == shard[None, :])
        & (flat_ids[None, :] < flat_ids[:, None])
        & first[None, :]
    )
    rank = jnp.sum(smaller.astype(jnp.int32), 1)
    slots = place.blk * room

    def slot_ids_of(round_number):
        at = rank - round_number * room
        slot = jnp.where((at >= 0) & (at < room), shard * room + at, slots)
        hit = slot[None, :] == jnp.arange(slots)[:, None]
        return jnp.max(jnp.where(hit, flat_ids[None, :], -1), 1)

    def lookup_slots(round_number):
        at = rank - round_number * room
        owner = shard // per_owner
        relative = ((owner ^ place.g) * per_owner + shard % per_owner) * room + at
        return jnp.where((at >= 0) & (at < room), relative, slots)

    def gradient_slots(round_number):
        at = rank - round_number * room
        relative = (shard ^ place.b) * room + at
        return jnp.where((at >= 0) & (at < room), relative, slots)

    def fetch(grp_ids, round_number):
        span = per_owner * room
        asked = [lax.dynamic_slice_in_dim(ids, place.g * span, span) for ids in grp_ids]
        local = jnp.concatenate(asked) - place.g * table_rows
        found = word_table.at[jnp.clip(local, 0, table_rows - 1)].get(mode="clip")
        parts = [found[k * span : (k + 1) * span] for k in range(place.grp)]
        rows = [parts[0]] + [place.send(parts[k], k) for k in range(1, place.grp)]
        return jnp.concatenate(rows)

    def pack(values, length):
        return jnp.concatenate([values, jnp.zeros((length - values.shape[0],), values.dtype)])

    slot_ids = slot_ids_of(0)
    early = jnp.concatenate(
        [slot_ids, false_neg.reshape(-1), valid, jnp.max(rank)[None]]
    )
    early = pack(early, -(-early.shape[0] // 1024) * 1024).reshape(-1, 128)
    grp_early = [early] + [place.send(early, k) for k in range(1, place.grp)]
    grp_ids = [item.reshape(-1)[:slots] for item in grp_early]
    looked_up = fetch(grp_ids, 0)
    early_all = jnp.stack(in_order(grp_early, place.g))
    early_all = gather_stage(place, early_all, place.y_masks, place.y)
    early_all = gather_stage(place, early_all, place.z_masks, place.z)
    early_all = early_all.reshape(place.count, -1)
    ids_all = early_all[:, :slots]
    at = slots
    false_neg_all = early_all[:, at : at + pairs_here * total_pairs].reshape(
        total_pairs, total_pairs
    )
    at += pairs_here * total_pairs
    valid_all = early_all[:, at : at + pairs_here].reshape(-1)
    at += pairs_here
    rounds = jnp.max(early_all[:, at]) // room + 1

    def look_up_all():
        whole = lax.all_gather(word_table, "grp", axis=0, tiled=True)
        return jnp.arange(tokens, dtype=jnp.int32), whole[flat_ids]

    slot, found = lax.cond(
        rounds > 1, look_up_all, lambda: (lookup_slots(0).astype(jnp.int32), looked_up)
    )
    (
        unit1,
        inverse1,
        normed_low,
        projected,
        probs,
        attended,
        unit2,
        inverse2,
        middle_low,
        activated_low,
        slope,
        unit3,
        inverse3,
        pooled,
        own_embed,
    ) = forward(
        lengths_flat,
        slot[:, None],
        found,
        small_rows,
        (qkv_weight, out_weight, up_weight, down_weight),
        seq_len,
        head_dim,
    )

    gathered = gather_far_first(place, own_embed).reshape(total_pairs, 2, width)
    queries, documents = gathered[:, 0], gathered[:, 1]
    diagonal = jnp.arange(total_pairs)[:, None] == jnp.arange(total_pairs)[None, :]
    allowed = (valid_all[None, :] > 0) & ((false_neg_all == 0) | diagonal)
    scores = contract_cols(queries, documents) / logit_divisor_constant
    query_lse, query_probs = masked_softmax(scores, allowed)
    doc_lse, doc_probs = masked_softmax(scores.T, allowed)
    diag = jnp.sum(jnp.where(diagonal, scores, 0.0), -1)
    valid_floats = valid_all.astype(jnp.float32)
    pair_count = jnp.maximum(jnp.sum(valid_floats), 1.0)
    loss_total = jnp.sum(valid_floats * (query_lse + doc_lse - 2.0 * diag)) / 2.0
    row_weight = valid_floats / (2.0 * pair_count)
    identity_mask = diagonal.astype(jnp.float32)
    score_grad = (
        row_weight[:, None] * (query_probs - identity_mask)
        + (row_weight[:, None] * (doc_probs - identity_mask)).T
    )
    row_start = (place.b * place.grp + place.g) * pairs_here
    query_grad_rows = lax.dynamic_slice_in_dim(score_grad, row_start, pairs_here, 0)
    doc_grad_rows = lax.dynamic_slice_in_dim(score_grad, row_start, pairs_here, 1).T
    embed_grad = (
        jnp.stack(
            [
                jnp.dot(
                    query_grad_rows, documents.astype(jnp.float32), precision=finest_arithmetic
                ),
                jnp.dot(doc_grad_rows, queries.astype(jnp.float32), precision=finest_arithmetic),
            ],
            1,
        )
        / logit_divisor_constant
    )

    lowered_grad, lifted_low, second, feed_sums = feed_back(
        lengths_flat,
        embed_grad,
        (unit2, inverse2, slope, unit3, inverse3, pooled),
        small_rows,
        (up_weight, down_weight),
        seq_len,
    )
    group_one, _ = reduce_group(
        place, [(activated_low, lowered_grad), (middle_low, lifted_low)], None
    )
    second, group_one = lax.optimization_barrier((second, group_one))
    group_one = reduce_group_rest(place, group_one, 0)
    branch_grad, projected_grad, own_rows, position_grad, attention_sums = attention_back(
        gradient_slots(0),
        second,
        (projected, probs, unit1, inverse1),
        small_rows,
        (qkv_weight, out_weight),
        seq_len,
        head_dim,
        slots,
    )

    grid_ids = lax.dynamic_slice_in_dim(
        ids_all.reshape(place.blk, place.grp, place.blk, room), place.b, 1, 2
    )[:, :, 0]

    rows = own_rows.reshape(place.blk, room, width)
    arrived = [rows[0]] + [place.send(rows[k], k * place.grp) for k in range(1, place.blk)]
    halves = [jnp.concatenate(arrived[: place.far]), jnp.concatenate(arrived[place.far :])]
    over_x = [
        jnp.concatenate([halves[0], halves[1]])
        if mask == 0
        else jnp.concatenate([place.send(half, mask) for half in halves])
        for mask in place.x_masks
    ]
    over_core = [place.send(item, 1) for item in over_x]
    sources = [item for pair in zip(over_x, over_core) for item in pair]
    ids = jnp.stack(in_order([grid_ids[i] for i in range(place.blk)], place.b), 1)
    local = ids - place.b * shard_rows
    inside = ids >= 0
    counts = jnp.sum(inside.astype(jnp.int32), -1).reshape(-1)
    local = jnp.where(inside, local, shard_rows).reshape(-1)
    word_rows, word_squares = word_sum(
        place.g, counts, local, sources, shard_rows, place.blk, room
    )
    word_squares = jnp.sum(word_squares)

    def all_rows(carry):
        token_grads = attention_back(
            jnp.arange(tokens, dtype=jnp.int32) + carry[0],
            second,
            (projected, probs, unit1, inverse1),
            small_rows,
            (qkv_weight, out_weight),
            seq_len,
            head_dim,
            slots,
        )[2]
        every_id = lax.all_gather(flat_ids + carry[0], "blk", axis=0, tiled=True) - place.b * shard_rows
        every_row = lax.all_gather(token_grads, "blk", axis=0, tiled=True)
        inside = (every_id >= 0) & (every_id < shard_rows)
        total = (
            jnp.zeros((shard_rows, width), jnp.float32)
            .at[jnp.where(inside, every_id, shard_rows)]
            .add(every_row.astype(jnp.float32), mode="drop")
        )
        total = lax.psum(total, "grp")
        return (carry[0] + 1, total, jnp.sum(total * total))

    _, word_rows, word_squares = lax.while_loop(
        lambda carry: (carry[0] < 1) & (rounds > 1),
        all_rows,
        (jnp.int32(0), word_rows, word_squares),
    )

    small_grad = jnp.concatenate([position_grad, attention_sums[:4], feed_sums[:10]], 0)
    small_flat = small_grad.reshape(-1, strip)
    small_piece = -(-small_flat.shape[0] // (16 * place.count)) * 16
    small_padded = jnp.concatenate(
        [
            small_flat,
            jnp.zeros((small_piece * place.count - small_flat.shape[0], strip), jnp.float32),
        ]
    )
    small_parts = small_padded.reshape(place.blk, place.xs, 2, small_piece, strip)
    group_two, fine = reduce_group(
        place, [(normed_low, projected_grad), (attended, branch_grad)], small_parts
    )
    group_two = reduce_group_rest(place, group_two, fine)
    cut = group_two.shape[0] - small_piece
    small_own = group_two[cut:]
    matrix_own = jnp.concatenate([group_one, group_two[:cut]]).astype(jnp.bfloat16)
    gathered_grads = gather_stage(place, matrix_own, place.x_masks, place.x)
    gathered_grads = gather_stage(place, gathered_grads, place.core_masks, place.core)
    gathered_grads = jnp.swapaxes(gathered_grads, 0, 1)
    masters = (down_master, up_master, qkv_master, out_master)
    shards, at = [], 0
    for master in masters:
        rows, columns = master.shape[0] // place.xs, master.shape[1]
        length = rows * (columns // 2 // strip)
        shards.append(
            whole_rows(place, gathered_grads[:, :, at : at + length], rows, columns).astype(
                jnp.float32
            )
        )
        at += length

    matrix_floats = matrix_own.astype(jnp.float32)
    squares = (
        jnp.sum(matrix_floats * matrix_floats)
        + jnp.sum(small_own * small_own)
        + word_squares / place.grp
    )
    late = jnp.concatenate([small_own, jnp.full((8, strip), squares)])
    late = gather_far_first(place, late).reshape(place.count, -1, strip)
    small_total = late[:, :small_piece].reshape(-1, strip)[: small_flat.shape[0]]
    small_total = small_total.reshape(small_grad.shape)
    grad_norm = jnp.sqrt(jnp.sum(late[:, small_piece, 0]))
    factor = clip_bound / jnp.maximum(grad_norm, clip_bound)
    down_shard, up_shard, qkv_shard, out_shard = shards
    grads = (word_rows, qkv_shard, out_shard, up_shard, down_shard, small_total)
    parameters = (word_master, qkv_master, out_master, up_master, down_master, small_rows)
    moments = (word_moments, qkv_moments, out_moments, up_moments, down_moments, small_moments)
    results = []
    for grad, moment, master, rate in zip(grads, moments, parameters, rate_table):
        results.extend(adam_update(grad * factor, moment, master, rate))
    return (loss_total, pair_count, grad_norm, *results)


def solution(mesh):
    in_specs = (
        P(both, None, None),
        P(both, None),
        P(both),
        P(both, None),
        P("grp", None),
        P(),
        P(),
        P(),
        P(),
        P("blk", None),
        P("blk", None),
        P("blk", None),
        P("blk", None),
        P("blk", None),
        P(None, "blk", None),
        P(None, "blk", None),
        P(None, "blk", None),
        P(None, "blk", None),
        P(None, "blk", None),
        P(),
        P(),
    )
    out_specs = (P(), P(), P()) + (P("blk", None),) * 15 + (P(), P(), P())
    return jax.shard_map(
        on_device, mesh=mesh, in_specs=in_specs, out_specs=out_specs, check_vma=False
    )
```

```python
import functools

import jax
import jax.numpy as jnp
from jax import lax
from jax.experimental import pallas as pl
from jax.experimental.pallas import tpu as pltpu
from jax.sharding import PartitionSpec as P

HEADS = 12
STEP = 5


logit_divisor_constant = 0.01
clip_bound = 0.001
beta_first = 0.5
beta_second = 0.5
decay_weight = 0.01
epsilon = 1e-08
rate_table = (0.1, 0.02, 0.1, 0.02, 0.01, 0.2)
finest_arithmetic = lax.Precision.HIGHEST
both = ("blk", "grp")
strip = 384


def contract_rows(left, right):
    return lax.dot_general(
        left, right, (((0,), (0,)), ((), ())), preferred_element_type=jnp.float32
    )


def contract_cols(left, right):
    return lax.dot_general(
        left, right, (((1,), (1,)), ((), ())), preferred_element_type=jnp.float32
    )


def adam_update(grad, moments, master, rate):
    first = beta_first * moments[0] + (1.0 - beta_first) * grad
    second = beta_second * moments[1] + (1.0 - beta_second) * grad * grad
    first_hat = first / (1.0 - beta_first**STEP)
    second_hat = second / (1.0 - beta_second**STEP)
    updated = master - rate * (first_hat / (jnp.sqrt(second_hat) + epsilon) + decay_weight * master)
    return (first, second, updated)


def masked_softmax(pairwise_affinity_matrix, allowed):
    masked = jnp.where(allowed, pairwise_affinity_matrix, -1000000000.0)
    top = jnp.max(masked, -1, keepdims=True)
    expo = jnp.where(allowed, jnp.exp(masked - top), 0.0)
    total = jnp.sum(expo, -1, keepdims=True)
    return (top[:, 0] + jnp.log(total[:, 0]), expo / total)


VMEM_ALLOWED = 56 * 1024 * 1024
low = jnp.bfloat16


def whole_block(shape):
    return pl.BlockSpec(shape, lambda *_: (0,) * len(shape), pipeline_mode=pl.Buffered(1))


def rows_block(rows, columns):
    return pl.BlockSpec((rows, columns), lambda i, *_: (i, 0))


def normalize(states):
    mean = jnp.mean(states, -1, keepdims=True)
    centered = states - mean
    inverse = lax.rsqrt(jnp.mean(centered * centered, -1, keepdims=True) + 1e-06)
    return centered * inverse, inverse


def normalize_back(grad, gain, unit_states, inverse):
    scaled = grad * gain
    inner = jnp.mean(scaled * unit_states, -1, keepdims=True)
    back = inverse * (scaled - jnp.mean(scaled, -1, keepdims=True) - unit_states * inner)
    return back, jnp.sum(grad * unit_states, 0, keepdims=True), jnp.sum(grad, 0, keepdims=True)


def gelu_and_slope(values):
    size = jnp.abs(values) * 0.7071067811865476
    t = 1.0 / (1.0 + 0.3275911 * size)
    series = t * (
        0.254829592
        + t * (-0.284496736 + t * (1.421413741 + t * (-1.453152027 + t * 1.061405429)))
    )
    bell = jnp.exp(-size * size)
    tail = 0.5 * series * bell
    below = jnp.where(values >= 0.0, 1.0 - tail, tail)
    return values * below, below + values * (0.3989422804014327 * bell)


def dot_rows(left, right):
    return lax.dot_general(
        left, right, (((0,), (0,)), ((), ())), preferred_element_type=jnp.float32
    )


def dot_cols(left, right):
    return lax.dot_general(
        left, right, (((1,), (1,)), ((), ())), preferred_element_type=jnp.float32
    )


def dot_plain(left, right):
    return jnp.dot(left, right, preferred_element_type=jnp.float32)


def head_masks(lanes, head_dim):
    even = (lax.broadcasted_iota(jnp.int32, (1, lanes), 1) < head_dim).astype(low)
    return even, (1.0 - even.astype(jnp.float32)).astype(low)


def forward_kernel(
    lengths_ref,
    slots_ref,
    found_ref,
    small_ref,
    qkv_ref,
    out_ref,
    up_ref,
    down_ref,
    unit1_ref,
    inverse1_ref,
    normed_ref,
    projected_ref,
    probs_ref,
    attended_ref,
    unit2_ref,
    inverse2_ref,
    middle_ref,
    activated_ref,
    slope_ref,
    unit3_ref,
    inverse3_ref,
    pooled_ref,
    embed_ref,
    *,
    seq_len,
    seqs,
    head_dim,
):
    step = pl.program_id(0)
    width = found_ref.shape[1]
    rows = seqs * seq_len
    slots = found_ref.shape[0]

    def vector(index):
        return small_ref[seq_len + index : seq_len + index + 1, :]

    pick = slots_ref[...] == lax.broadcasted_iota(jnp.int32, (rows, slots), 1)
    pick = jnp.where(pick, 1.0, 0.0).astype(low)
    embedded = dot_plain(pick, found_ref[...])
    positions = small_ref[:seq_len, :]
    embedded = embedded + jnp.concatenate([positions] * seqs, 0)
    unit1, inverse1 = normalize(embedded)
    unit1_ref[...] = unit1
    inverse1_ref[...] = inverse1
    normed = unit1 * vector(0) + vector(1)
    normed_low = normed.astype(low)
    normed_ref[...] = normed_low
    zeros = jnp.zeros((1, width), jnp.float32)
    for part, bias in enumerate((vector(2), zeros, vector(3))):
        at = slice(part * width, (part + 1) * width)
        projected_ref[:, at] = (dot_plain(normed_low, qkv_ref[:, at]) + bias).astype(low)
    lanes = 2 * head_dim
    even, odd = head_masks(lanes, head_dim)
    key_at = lax.broadcasted_iota(jnp.int32, (2 * seq_len, seq_len), 1)
    for s in range(seqs):
        at = slice(s * seq_len, (s + 1) * seq_len)
        live = key_at < lengths_ref[step * seqs + s]
        for p in range(width // lanes):
            query = projected_ref[at, p * lanes : (p + 1) * lanes]
            keys = projected_ref[at, width + p * lanes : width + (p + 1) * lanes]
            values = projected_ref[at, 2 * width + p * lanes : 2 * width + (p + 1) * lanes]
            query = jnp.concatenate([query * even, query * odd], 0)
            logits = dot_cols(query, keys) * head_dim ** (-0.5)
            logits = jnp.where(live, logits, -1000000000.0)
            expo = jnp.exp(logits - jnp.max(logits, -1, keepdims=True))
            probs = (expo / jnp.sum(expo, -1, keepdims=True)).astype(low)
            probs_ref[s, p] = probs
            both_probs = jnp.concatenate([probs[:seq_len], probs[seq_len:]], 1)
            both_values = jnp.concatenate([values * even, values * odd], 0)
            attended_ref[at, p * lanes : (p + 1) * lanes] = dot_plain(
                both_probs, both_values
            ).astype(low)
    branch = dot_plain(attended_ref[...], out_ref[...]) + vector(4)
    unit2, inverse2 = normalize(normed + branch)
    unit2_ref[...] = unit2
    inverse2_ref[...] = inverse2
    middle = unit2 * vector(5) + vector(6)
    middle_low = middle.astype(low)
    middle_ref[...] = middle_low
    lowered = middle + vector(7)
    for j in range(up_ref.shape[1] // width):
        at = slice(j * width, (j + 1) * width)
        lifted = dot_plain(middle_low, up_ref[:, at]) + vector(10 + j)
        activated, slope = gelu_and_slope(lifted)
        activated = activated.astype(low)
        activated_ref[:, at] = activated
        slope_ref[:, at] = slope.astype(low)
        lowered = lowered + dot_plain(activated, down_ref[at, :])
    unit3, inverse3 = normalize(lowered)
    unit3_ref[...] = unit3
    inverse3_ref[...] = inverse3
    final = unit3 * vector(8) + vector(9)
    row_at = lax.broadcasted_iota(jnp.int32, (seq_len, 1), 0)
    pooled = []
    for s in range(seqs):
        length = lengths_ref[step * seqs + s]
        weights = (row_at < length).astype(jnp.float32)
        total = jnp.sum(final[s * seq_len : (s + 1) * seq_len] * weights, 0, keepdims=True)
        pooled.append(total / length.astype(jnp.float32))
    pooled = jnp.concatenate(pooled, 0)
    pooled_ref[0] = pooled
    squares = jnp.sum(pooled * pooled, -1, keepdims=True)
    embed_ref[0] = (pooled * lax.rsqrt(squares + 1e-06)).astype(low)


def forward(lengths_flat, slot, found, small_rows, weights, seq_len, head_dim):
    tokens, width = slot.shape[0], found.shape[1]
    seqs = 2
    rows = seqs * seq_len
    steps = tokens // rows
    lifted = weights[2].shape[1]
    f32 = jnp.float32
    outs = [
        ((tokens, width), f32),
        ((tokens, 1), f32),
        ((tokens, width), low),
        ((tokens, 3 * width), low),
        ((steps * seqs, width // (2 * head_dim), 2 * seq_len, seq_len), low),
        ((tokens, width), low),
        ((tokens, width), f32),
        ((tokens, 1), f32),
        ((tokens, width), low),
        ((tokens, lifted), low),
        ((tokens, lifted), low),
        ((tokens, width), f32),
        ((tokens, 1), f32),
        ((steps, seqs, width), f32),
        ((steps, seqs, width), low),
    ]

    def spec(shape):
        if shape[0] == tokens:
            return rows_block(rows, shape[1])
        block = (shape[0] // steps,) + shape[1:]
        return pl.BlockSpec(block, lambda i, *_: (i,) + (0,) * (len(shape) - 1))

    return pl.pallas_call(
        functools.partial(forward_kernel, seq_len=seq_len, seqs=seqs, head_dim=head_dim),
        out_shape=[jax.ShapeDtypeStruct(*item) for item in outs],
        grid_spec=pltpu.PrefetchScalarGridSpec(
            num_scalar_prefetch=1,
            grid=(steps,),
            in_specs=[rows_block(rows, 1), whole_block(found.shape), whole_block(small_rows.shape)]
            + [whole_block(item.shape) for item in weights],
            out_specs=[spec(item[0]) for item in outs],
        ),
        compiler_params=pltpu.CompilerParams(vmem_limit_bytes=VMEM_ALLOWED),
        cost_estimate=pl.CostEstimate(
            flops=20 * 10**9, bytes_accessed=50 * 10**6, transcendentals=10**7
        ),
        name="encoder_forward",
    )(lengths_flat, slot, found, small_rows, *weights)


def feed_back_kernel(
    lengths_ref,
    embed_grad_ref,
    pooled_ref,
    small_ref,
    unit3_ref,
    inverse3_ref,
    slope_ref,
    unit2_ref,
    inverse2_ref,
    up_ref,
    down_ref,
    lowered_ref,
    lifted_ref,
    second_ref,
    sums_ref,
    *,
    seq_len,
    seqs,
):
    step = pl.program_id(0)
    width = unit3_ref.shape[1]

    @pl.when(step == 0)
    def _():
        sums_ref[...] = jnp.zeros_like(sums_ref)

    def vector(index):
        return small_ref[seq_len + index : seq_len + index + 1, :]

    pooled, grad = pooled_ref[0], embed_grad_ref[0]
    inverse = lax.rsqrt(jnp.sum(pooled * pooled, -1, keepdims=True) + 1e-06)
    inner = jnp.sum(pooled * grad, -1, keepdims=True)
    pooled_grad = inverse * (grad - pooled * (inverse * inverse * inner))
    row_at = lax.broadcasted_iota(jnp.int32, (seq_len, 1), 0)
    final_grad = []
    for s in range(seqs):
        length = lengths_ref[step * seqs + s]
        weights = (row_at < length).astype(jnp.float32)
        final_grad.append(weights * (pooled_grad[s : s + 1] / length.astype(jnp.float32)))
    final_grad = jnp.concatenate(final_grad, 0)
    third, gain3, shift3 = normalize_back(
        final_grad, vector(8), unit3_ref[...], inverse3_ref[...]
    )
    lowered_grad = third.astype(low)
    lowered_ref[...] = lowered_grad
    middle_grad = third
    up_sums = []
    for j in range(up_ref.shape[1] // width):
        at = slice(j * width, (j + 1) * width)
        grad = dot_cols(lowered_grad, down_ref[at, :]) * slope_ref[:, at].astype(jnp.float32)
        grad = grad.astype(low)
        lifted_ref[:, at] = grad
        up_sums.append(jnp.sum(grad.astype(jnp.float32), 0, keepdims=True))
        middle_grad = middle_grad + dot_cols(grad, up_ref[:, at])
    second, gain2, shift2 = normalize_back(
        middle_grad, vector(5), unit2_ref[...], inverse2_ref[...]
    )
    second_ref[...] = second
    branch_sum = jnp.sum(second.astype(low).astype(jnp.float32), 0, keepdims=True)
    lowered_sum = jnp.sum(lowered_grad.astype(jnp.float32), 0, keepdims=True)
    sums = [branch_sum, gain2, shift2, lowered_sum, gain3, shift3] + up_sums
    sums_ref[: len(sums), :] += jnp.concatenate(sums, 0)


def feed_back(lengths_flat, embed_grad, kept, small_rows, weights, seq_len):
    unit2, inverse2, slope, unit3, inverse3, pooled = kept
    tokens, width = unit2.shape
    lifted = slope.shape[1]
    seqs = 2
    rows = seqs * seq_len
    steps = tokens // rows
    pair = pl.BlockSpec((1, seqs, width), lambda i, *_: (i, 0, 0))
    return pl.pallas_call(
        functools.partial(feed_back_kernel, seq_len=seq_len, seqs=seqs),
        out_shape=[
            jax.ShapeDtypeStruct((tokens, width), low),
            jax.ShapeDtypeStruct((tokens, lifted), low),
            jax.ShapeDtypeStruct((tokens, width), jnp.float32),
            jax.ShapeDtypeStruct((16, width), jnp.float32),
        ],
        grid_spec=pltpu.PrefetchScalarGridSpec(
            num_scalar_prefetch=1,
            grid=(steps,),
            in_specs=[
                pair,
                pair,
                whole_block(small_rows.shape),
                rows_block(rows, width),
                rows_block(rows, 1),
                rows_block(rows, lifted),
                rows_block(rows, width),
                rows_block(rows, 1),
                whole_block(weights[0].shape),
                whole_block(weights[1].shape),
            ],
            out_specs=[
                rows_block(rows, width),
                rows_block(rows, lifted),
                rows_block(rows, width),
                pl.BlockSpec((16, width), lambda i, *_: (0, 0)),
            ],
        ),
        compiler_params=pltpu.CompilerParams(vmem_limit_bytes=VMEM_ALLOWED),
        cost_estimate=pl.CostEstimate(
            flops=10 * 10**9, bytes_accessed=40 * 10**6, transcendentals=0
        ),
        name="feed_back",
    )(
        lengths_flat,
        embed_grad,
        pooled,
        small_rows,
        unit3,
        inverse3,
        slope,
        unit2,
        inverse2,
        *weights,
    )


def attention_back_kernel(
    slots_ref,
    second_ref,
    projected_ref,
    probs_ref,
    unit1_ref,
    inverse1_ref,
    small_ref,
    qkv_ref,
    out_ref,
    branch_ref,
    projected_grad_ref,
    mine_ref,
    theirs_ref,
    positions_ref,
    sums_ref,
    total_ref,
    *,
    seq_len,
    seqs,
    head_dim,
):
    step = pl.program_id(0)
    width = second_ref.shape[1]
    lanes = 2 * head_dim
    scale = head_dim ** (-0.5)

    @pl.when(step == 0)
    def _():
        sums_ref[...] = jnp.zeros_like(sums_ref)
        positions_ref[...] = jnp.zeros_like(positions_ref)
        total_ref[...] = jnp.zeros_like(total_ref)

    second = second_ref[...]
    branch = second.astype(low)
    branch_ref[...] = branch
    attended_grad = dot_cols(branch, out_ref[...]).astype(low)
    even, odd = head_masks(lanes, head_dim)
    for s in range(seqs):
        at = slice(s * seq_len, (s + 1) * seq_len)
        for p in range(width // lanes):
            here = slice(p * lanes, (p + 1) * lanes)
            there = slice(width + p * lanes, width + (p + 1) * lanes)
            yonder = slice(2 * width + p * lanes, 2 * width + (p + 1) * lanes)
            query = projected_ref[at, here]
            keys = projected_ref[at, there]
            values = projected_ref[at, yonder]
            grad = attended_grad[at, here]
            grad = jnp.concatenate([grad * even, grad * odd], 0)
            query = jnp.concatenate([query * even, query * odd], 0)
            keys = jnp.concatenate([keys * even, keys * odd], 0)
            probs_low = probs_ref[s, p]
            probs = probs_low.astype(jnp.float32)
            probs_grad = dot_cols(grad, values)
            weighted = probs * probs_grad
            inner = jnp.sum(weighted, -1, keepdims=True)
            logits_grad = ((weighted - probs * inner) * scale).astype(low)
            both_grads = jnp.concatenate([logits_grad[:seq_len], logits_grad[seq_len:]], 1)
            projected_grad_ref[at, here] = dot_plain(both_grads, keys).astype(low)
            projected_grad_ref[at, there] = dot_rows(logits_grad, query).astype(low)
            projected_grad_ref[at, yonder] = dot_rows(probs_low, grad).astype(low)
    projected_grad = projected_grad_ref[...]
    query_sum = jnp.sum(projected_grad[:, :width].astype(jnp.float32), 0, keepdims=True)
    value_sum = jnp.sum(projected_grad[:, 2 * width :].astype(jnp.float32), 0, keepdims=True)
    normed_grad = second + dot_cols(projected_grad, qkv_ref[...])
    gain = small_ref[seq_len : seq_len + 1, :]
    embedded_grad, gain1, shift1 = normalize_back(
        normed_grad, gain, unit1_ref[...], inverse1_ref[...]
    )
    for s in range(seqs):
        positions_ref[...] += embedded_grad[s * seq_len : (s + 1) * seq_len]
    sums_ref[:4, :] += jnp.concatenate([gain1, shift1, query_sum, value_sum], 0)
    slots, rows = total_ref.shape[0], seqs * seq_len
    hit = slots_ref[0] == lax.broadcasted_iota(jnp.int32, (slots, rows), 0)
    hit = jnp.where(hit, 1.0, 0.0).astype(low)
    total_ref[...] += dot_plain(hit, embedded_grad.astype(low))

    @pl.when(step == pl.num_programs(0) - 1)
    def _():
        half = total_ref.shape[0] // 2
        mine_ref[...] = total_ref[:half]
        theirs_ref[...] = total_ref[half:].astype(low)


def attention_back(slot, second, kept, small_rows, weights, seq_len, head_dim, slots):
    projected, probs, unit1, inverse1 = kept
    tokens, width = second.shape
    seqs = 2
    rows = seqs * seq_len
    steps = tokens // rows
    probs_block = (seqs,) + probs.shape[1:]

    def fixed(shape):
        return pl.BlockSpec(shape, lambda i, *_: (0, 0))

    return pl.pallas_call(
        functools.partial(
            attention_back_kernel, seq_len=seq_len, seqs=seqs, head_dim=head_dim
        ),
        out_shape=[
            jax.ShapeDtypeStruct((tokens, width), low),
            jax.ShapeDtypeStruct((tokens, 3 * width), low),
            jax.ShapeDtypeStruct((slots // 2, width), jnp.float32),
            jax.ShapeDtypeStruct((slots // 2, width), low),
            jax.ShapeDtypeStruct((seq_len, width), jnp.float32),
            jax.ShapeDtypeStruct((8, width), jnp.float32),
        ],
        grid=(steps,),
        in_specs=[
            pl.BlockSpec((1, 1, rows), lambda i: (i, 0, 0)),
            rows_block(rows, width),
            rows_block(rows, 3 * width),
            pl.BlockSpec(probs_block, lambda i: (i, 0, 0, 0)),
            rows_block(rows, width),
            rows_block(rows, 1),
            whole_block(small_rows.shape),
            whole_block(weights[0].shape),
            whole_block(weights[1].shape),
        ],
        out_specs=[
            rows_block(rows, width),
            rows_block(rows, 3 * width),
            fixed((slots // 2, width)),
            fixed((slots // 2, width)),
            fixed((seq_len, width)),
            fixed((8, width)),
        ],
        scratch_shapes=[pltpu.VMEM((slots, width), jnp.float32)],
        compiler_params=pltpu.CompilerParams(vmem_limit_bytes=VMEM_ALLOWED),
        cost_estimate=pl.CostEstimate(
            flops=10 * 10**9, bytes_accessed=30 * 10**6, transcendentals=0
        ),
        name="attention_back",
    )(slot.reshape(steps, 1, rows), second, projected, probs, unit1, inverse1, small_rows, *weights)


def weight_grad_kernel(core_ref, *refs, jobs, xs):
    theirs_ref, mine_ref, turned_ref = refs[-3:]
    step = pl.program_id(0)
    start, base = 0, 0
    for n, (tiles, tall, piece, strips) in enumerate(jobs):
        left_ref, right_ref = refs[2 * n], refs[2 * n + 1]

        def work(start=start, base=base, left_ref=left_ref, right_ref=right_ref, job=jobs[n]):
            tiles, tall, piece, strips = job
            tile = step - start
            if tall or tiles == 1:
                grad = dot_rows(left_ref[...], right_ref[...])
            else:

                @pl.when(tile == 0)
                def _():
                    turned_ref[...] = left_ref[...].T

                grad = dot_plain(turned_ref[...], right_ref[...])
            count = grad.shape[0] // piece // xs
            for j in range(2):
                part = grad[:, j * strip : (j + 1) * strip]
                part = part.reshape(count, xs, piece, strip)
                if tall:
                    half = j
                    at = (pl.ds(tile * count, count), slice(None), pl.ds(base, piece))
                else:
                    number = 2 * tile + j
                    half = number // strips
                    row = pl.multiple_of(base + (number % strips) * piece, 16)
                    at = (slice(None), slice(None), pl.ds(row, piece))

                @pl.when(core_ref[0] == half)
                def _(at=at, part=part):
                    mine_ref[at] = part

                @pl.when(core_ref[0] != half)
                def _(at=at, part=part):
                    theirs_ref[at] = part.astype(low)

        pl.when((step >= start) & (step < start + tiles))(work)
        start += tiles
        base += piece * strips


def weight_grads(place, pairs):
    tile_rows = 2 * strip
    jobs, in_specs, operands = [], [], []
    start, rows = 0, 0
    tokens = pairs[0][0].shape[0]
    for left, right in pairs:
        strips = right.shape[1] // 2 // strip
        tall = left.shape[1] > tile_rows
        tiles = left.shape[1] // tile_rows if tall else strips
        piece = left.shape[1] // place.blk // place.xs

        def tile_of(i, start=start, tiles=tiles):
            return jnp.clip(i - start, 0, tiles - 1)

        def block(varies, f=tile_of):
            if varies:
                return pl.BlockSpec((tokens, tile_rows), lambda i, h: (0, f(i)))
            return whole_block((tokens, tile_rows))

        in_specs += [block(tall), block(not tall and tiles > 1)]
        jobs.append((tiles, tall, piece, strips))
        operands += [left, right]
        start += tiles
        rows += piece * strips
    shape = (place.blk, place.xs, rows, strip)
    return pl.pallas_call(
        functools.partial(weight_grad_kernel, jobs=jobs, xs=place.xs),
        out_shape=[
            jax.ShapeDtypeStruct(shape, low),
            jax.ShapeDtypeStruct(shape, jnp.float32),
        ],
        grid_spec=pltpu.PrefetchScalarGridSpec(
            num_scalar_prefetch=1,
            grid=(start,),
            in_specs=in_specs,
            out_specs=[whole_block(shape), whole_block(shape)],
            scratch_shapes=[pltpu.VMEM((tile_rows, tokens), low)],
        ),
        compiler_params=pltpu.CompilerParams(vmem_limit_bytes=VMEM_ALLOWED),
        cost_estimate=pl.CostEstimate(
            flops=start * 2 * tokens * tile_rows * tile_rows,
            bytes_accessed=16 * 10**6,
            transcendentals=0,
        ),
        name="weight_grads",
    )(place.core.reshape(1).astype(jnp.int32), *operands)


def word_sum_kernel(place_ref, count_ref, id_ref, *refs, grp, chunks, room, span):
    sources = refs[:grp]
    out_ref, squares_ref, total_ref, rows_ref, chunk_ref, in_sems, out_sem = refs[grp:]
    batch = 8
    copies = [
        pltpu.make_async_copy(sources[k], rows_ref.at[k], in_sems.at[k]) for k in range(grp)
    ]
    for copy in copies:
        copy.start()
    zeros = jnp.zeros((batch, total_ref.shape[1]), jnp.float32)

    def clear(i, _):
        total_ref[pl.ds(pl.multiple_of(i * batch, batch), batch), :] = zeros
        return 0

    lax.fori_loop(0, total_ref.shape[0] // batch, clear, 0, unroll=4)
    for copy in copies:
        copy.wait()

    def one_source(n, _):
        slot = (n // chunks) ^ place_ref[0]
        start = (n % chunks) * room
        count = count_ref[n]

        def widen(i, _):
            at = pl.ds(pl.multiple_of(start + i * 16, 16), 16)
            to = pl.ds(pl.multiple_of(i * 16, 16), 16)
            chunk_ref[to, :] = rows_ref[slot, at, :].astype(jnp.float32)
            return 0

        lax.fori_loop(0, (count + 15) // 16, widen, 0)

        def add(i, _):
            at = [id_ref[n * room + i * batch + j] for j in range(batch)]
            sums = [
                total_ref[pl.ds(at[j], 1), :] + chunk_ref[pl.ds(i * batch + j, 1), :]
                for j in range(batch)
            ]
            for j in range(batch):
                total_ref[pl.ds(at[j], 1), :] = sums[j]
            return 0

        lax.fori_loop(0, (count + batch - 1) // batch, add, 0)
        return 0

    lax.fori_loop(0, grp * chunks, one_source, 0)
    shard_rows = out_ref.shape[0]

    def finish(i, squares):
        at = pl.ds(pl.multiple_of(i * span, span), span)
        part = total_ref[at, :]
        pltpu.make_async_copy(total_ref.at[at], out_ref.at[at], out_sem).start()
        part = part * part
        return squares + jnp.sum(part.reshape(span // 8, 8, part.shape[1]), 0)

    squares = lax.fori_loop(
        0, shard_rows // span, finish, jnp.zeros((8, total_ref.shape[1]), jnp.float32)
    )
    squares_ref[...] = jnp.sum(squares, 0, keepdims=True)
    pltpu.make_async_copy(total_ref.at[pl.ds(0, shard_rows)], out_ref, out_sem).wait()


def word_sum(grp_index, counts, ids, sources, shard_rows, chunks, room):
    grp, width = len(sources), sources[0].shape[1]
    span = next(size for size in (128, 64, 32, 16, 8) if shard_rows % size == 0)
    anywhere = pl.BlockSpec(memory_space=pl.ANY)
    return pl.pallas_call(
        functools.partial(word_sum_kernel, grp=grp, chunks=chunks, room=room, span=span),
        out_shape=[
            jax.ShapeDtypeStruct((shard_rows, width), jnp.float32),
            jax.ShapeDtypeStruct((1, width), jnp.float32),
        ],
        grid_spec=pltpu.PrefetchScalarGridSpec(
            num_scalar_prefetch=3,
            grid=(1,),
            in_specs=[anywhere] * grp,
            out_specs=[anywhere, whole_block((1, width))],
            scratch_shapes=[
                pltpu.VMEM((shard_rows + 32, width), jnp.float32),
                pltpu.VMEM((grp,) + sources[0].shape, low),
                pltpu.VMEM((room, width), jnp.float32),
                pltpu.SemaphoreType.DMA((grp,)),
                pltpu.SemaphoreType.DMA,
            ],
        ),
        compiler_params=pltpu.CompilerParams(vmem_limit_bytes=VMEM_ALLOWED),
        cost_estimate=pl.CostEstimate(
            flops=10**7, bytes_accessed=40 * 10**6, transcendentals=0
        ),
        name="word_sum",
    )(grp_index.reshape(1), counts, ids, *sources)


def adam_kernel(factor_ref, grad_ref, master_ref, moments_ref, first_ref, second_ref, new_ref, *, rate):
    results = adam_update(
        grad_ref[...] * factor_ref[0], (moments_ref[0], moments_ref[1]), master_ref[...], rate
    )
    first_ref[...], second_ref[...], new_ref[...] = results


def adam_rows(factor, grad, master, moments, rate):
    rows, width = master.shape
    span = next(size for size in (256, 240, 192, 128, 96, 64, 32, 16, 8) if rows % size == 0)
    block = rows_block(span, width)
    return pl.pallas_call(
        functools.partial(adam_kernel, rate=rate),
        out_shape=[jax.ShapeDtypeStruct((rows, width), jnp.float32)] * 3,
        grid=(rows // span,),
        in_specs=[
            pl.BlockSpec(memory_space=pltpu.SMEM),
            block,
            block,
            pl.BlockSpec((2, span, width), lambda i: (0, i, 0)),
        ],
        out_specs=[block] * 3,
        compiler_params=pltpu.CompilerParams(vmem_limit_bytes=VMEM_ALLOWED),
        cost_estimate=pl.CostEstimate(
            flops=20 * rows * width, bytes_accessed=28 * rows * width, transcendentals=0
        ),
        name="adam_rows",
    )(factor, grad, master, moments)


def adam_matrices_kernel(place_ref, factor_ref, *refs, grp, shapes, rates):
    count = len(shapes)
    pieces, rest = (refs[:grp], refs[grp : 2 * grp]), refs[2 * grp :]
    small_ref, rest = rest[0], rest[1:]
    masters, rest = rest[: count + 1], rest[count + 1 :]
    moments, rest = rest[: count + 1], rest[count + 1 :]
    outs, scratch = rest[: 3 * count + 3], rest[3 * count + 3 :]
    factor = factor_ref[0]
    base = 0
    for n, (rows, width) in enumerate(shapes):
        strips = width // 2 // strip
        piece = rows // (grp // 2)
        group = pieces[n // 2]
        base = 0 if n % 2 == 0 else base
        for k in range(grp):
            source = place_ref[0] ^ k
            x, core = source // 2, source % 2
            for s in range(strips):
                part = group[k][base + s * piece : base + (s + 1) * piece, :]
                to_row = pl.multiple_of(x * piece, 16)
                to_column = pl.multiple_of((core * strips + s) * strip, 128)
                scratch[n][pl.ds(to_row, piece), pl.ds(to_column, strip)] = part.astype(
                    jnp.float32
                )
        base += strips * piece
    for n in range(count + 1):
        grad = small_ref[...] if n == count else scratch[n][...]
        results = adam_update(
            grad * factor, (moments[n][0], moments[n][1]), masters[n][...], rates[n]
        )
        for m in range(3):
            outs[3 * n + m][...] = results[m]


def adam_matrices(grp_index, factor, pieces_one, pieces_two, small, masters, moments, rates):
    shapes = [item.shape for item in masters]
    count = len(shapes) - 1
    operands = [*pieces_one, *pieces_two, small, *masters, *moments]
    return pl.pallas_call(
        functools.partial(
            adam_matrices_kernel, grp=len(pieces_one), shapes=shapes[:count], rates=rates
        ),
        out_shape=[jax.ShapeDtypeStruct(s, jnp.float32) for s in shapes for _ in range(3)],
        grid_spec=pltpu.PrefetchScalarGridSpec(
            num_scalar_prefetch=1,
            grid=(1,),
            in_specs=[pl.BlockSpec(memory_space=pltpu.SMEM)]
            + [whole_block(item.shape) for item in operands],
            out_specs=[whole_block(s) for s in shapes for _ in range(3)],
            scratch_shapes=[pltpu.VMEM(s, jnp.float32) for s in shapes[:count]],
        ),
        compiler_params=pltpu.CompilerParams(vmem_limit_bytes=VMEM_ALLOWED),
        cost_estimate=pl.CostEstimate(
            flops=10**8, bytes_accessed=30 * 10**6, transcendentals=0
        ),
        name="adam_matrices",
    )(grp_index.reshape(1), factor, *operands)


class Place:
    def __init__(self):
        self.blk, self.grp = lax.axis_size("blk"), lax.axis_size("grp")
        self.count = self.blk * self.grp
        self.b, self.g = lax.axis_index("blk"), lax.axis_index("grp")
        self.xs, self.far = self.grp // 2, self.blk // 2
        self.core, self.x = self.g % 2, self.g // 2
        self.y, self.z = self.b % 2, self.b // 2
        self.core_masks = [0, 1]
        self.x_masks = [2 * i for i in range(self.xs)]
        self.y_masks = [0, self.grp]
        self.z_masks = [2 * self.grp * i for i in range(self.far)]

    def send_swapped(self, value, far_mask):
        pairs = []
        for i in range(self.count):
            core, x, y = i % 2, i // 2 % self.xs, i // self.grp % 2
            z = i // (2 * self.grp) ^ far_mask
            pairs.append((i, ((z * 2 + core) * self.xs + x) * 2 + y))
        return lax.ppermute(value, both, pairs)

    def send(self, value, mask):
        pairs = [(i, i ^ mask) for i in range(self.count)]
        return lax.ppermute(value, both, pairs)


def in_order(pieces, index):
    step = 1
    while step < len(pieces):
        odd = (index & step) != 0
        pieces = [jnp.where(odd, pieces[i ^ step], pieces[i]) for i in range(len(pieces))]
        step *= 2
    return pieces


def gather_stage(place, value, masks, index):
    pieces = [value] + [place.send(value, mask) for mask in masks[1:]]
    return jnp.stack(in_order(pieces, index))


def gather_far_first(place, value):
    shape = value.shape
    value = gather_stage(place, value, place.z_masks, place.z)
    middle = [a + b for a in place.y_masks for b in place.x_masks]
    value = gather_stage(place, value, middle, place.y * place.xs + place.x)
    value = gather_stage(place, value, place.core_masks, place.core)
    value = value.reshape((2, 2, place.xs, place.far) + shape)
    return jnp.transpose(value, (3, 1, 2, 0) + tuple(range(4, 4 + len(shape)))).reshape(
        (place.blk, place.grp) + shape
    )


def to_send(value, fine):
    high = value.astype(low)
    if not fine:
        return high
    rows = value.shape[-2]
    rest = value[..., rows - fine :, :] - high[..., rows - fine :, :].astype(jnp.float32)
    return jnp.concatenate([high, rest.astype(low)], -2)


def from_sent(value, fine):
    value = value.astype(jnp.float32)
    if not fine:
        return value
    rows = value.shape[-2] - fine
    tail = value[..., rows - fine : rows, :] + value[..., rows:, :]
    return jnp.concatenate([value[..., : rows - fine, :], tail], -2)


def stage_parts(value, masks, index, fine):
    keep = lax.dynamic_index_in_dim(value, index, 0, keepdims=False)
    parts = [
        to_send(lax.dynamic_index_in_dim(value, index ^ k, 0, keepdims=False), fine)
        for k in range(1, len(masks))
    ]
    return keep, parts


def stage_sum(keep, arrived, fine):
    terms = [keep.astype(jnp.float32)] + [from_sent(item, fine) for item in arrived]
    while len(terms) > 1:
        terms = [terms[i] + terms[i + 1] for i in range(0, len(terms), 2)]
    return terms[0]


class Reduction:
    def __init__(self, place, value, x_first, fine=0):
        rows, columns = value.shape[2:]
        value = value.reshape(place.far, 2, place.xs, rows, columns)
        x_stage = (place.x_masks, place.x)
        y_stage = (place.y_masks, place.y)
        self.place, self.fine = place, fine
        if x_first:
            self.stages = [(*x_stage, 2), (*y_stage, 1)]
        else:
            self.stages = [(*y_stage, 1), (*x_stage, 1)]
        self.stages.append((place.z_masks, place.z, 0))
        self.value = value

    def prepare(self):
        self.masks, index, axis = self.stages.pop(0)
        self.keep, self.parts = stage_parts(
            jnp.moveaxis(self.value, axis, 0), self.masks, index, self.fine
        )

    def send(self):
        self.arrived = [
            self.place.send(part, mask) for part, mask in zip(self.parts, self.masks[1:])
        ]

    def add(self):
        self.value = stage_sum(self.keep, self.arrived, self.fine)


def tie(*items):
    return lax.optimization_barrier(items)


def half_gradient(place, left, right, core):
    width = right.shape[1] // 2
    part = lax.dynamic_slice_in_dim(right, core * width, width, 1)
    grad = contract_rows(left, part).astype(jnp.bfloat16)
    rows = grad.shape[0] // place.blk // place.xs
    strips = width // strip
    grad = grad.reshape(place.blk, place.xs, rows, strips, strip)
    return jnp.transpose(grad, (0, 1, 3, 2, 4)).reshape(
        place.blk, place.xs, strips * rows, strip
    )


def group_products(place, pairs):
    if all(a.shape[1] % (16 * place.blk * place.xs) == 0 for a, _ in pairs):
        return weight_grads(place, pairs)
    mine = [half_gradient(place, a, b, place.core) for a, b in pairs]
    theirs = [half_gradient(place, a, b, 1 - place.core) for a, b in pairs]
    return jnp.concatenate(theirs, 2), jnp.concatenate(mine, 2).astype(jnp.float32)


def merge_ids(left, right, length):
    hits = []
    for own, other in ((left, right), (right, left)):
        repeated = jnp.any(other[..., :, None] == own[..., None, :], -1)
        lower = (
            (other >= 0)[..., None, :]
            & ~repeated[..., None, :]
            & (other[..., None, :] < own[..., :, None])
        )
        rank = jnp.arange(own.shape[-1]) + jnp.sum(lower.astype(jnp.int32), -1)
        hit = rank[..., None, :] == jnp.arange(length)[:, None]
        hits.append(jnp.max(jnp.where(hit, own[..., None, :], -1), -1))
    return jnp.maximum(*hits)


def whole_rows(place, pieces, rows, width):
    strips = width // 2 // strip
    pieces = pieces.reshape(place.xs, 2, strips, rows, strip)
    return jnp.transpose(pieces, (0, 3, 1, 2, 4)).reshape(place.xs * rows, width)


def on_device(
    token_ids,
    lengths,
    valid,
    false_neg,
    word_table,
    qkv_weight,
    out_weight,
    up_weight,
    down_weight,
    word_master,
    qkv_master,
    out_master,
    up_master,
    down_master,
    word_moments,
    qkv_moments,
    out_moments,
    up_moments,
    down_moments,
    small_rows,
    small_moments,
):
    place = Place()
    pairs_here = token_ids.shape[0]
    total_pairs = pairs_here * place.count
    seq_count = 2 * pairs_here
    seq_len = token_ids.shape[2]
    width = word_table.shape[1]
    head_dim = width // HEADS
    flat_ids = token_ids.reshape(-1)
    tokens = flat_ids.shape[0]
    lengths_flat = lengths.reshape(-1)

    shard_rows = word_master.shape[0]
    table_rows = word_table.shape[0]
    per_owner = table_rows // shard_rows
    room = max(16, tokens // place.blk)
    shard = flat_ids // shard_rows
    same_id = flat_ids[:, None] == flat_ids[None, :]
    before = jnp.arange(tokens)[:, None] < jnp.arange(tokens)[None, :]
    first = ~jnp.any(same_id & before, 0)
    smaller = (
        (shard[:, None] == shard[None, :])
        & (flat_ids[None, :] < flat_ids[:, None])
        & first[None, :]
    )
    rank = jnp.sum(smaller.astype(jnp.int32), 1)
    slots = place.blk * room

    owner = shard // per_owner
    relative = ((owner ^ place.g) * per_owner + shard % per_owner) * room + rank
    lookup_slots = jnp.where(rank < room, relative, slots)

    def fetch(grp_ids):
        span = per_owner * room
        asked = [lax.dynamic_slice_in_dim(ids, place.g * span, span) for ids in grp_ids]
        local = jnp.concatenate(asked) - place.g * table_rows
        found = word_table.at[jnp.clip(local, 0, table_rows - 1)].get(mode="clip")
        found, sibling = tie(found, grp_ids[1])
        parts = [found[k * span : (k + 1) * span] for k in range(place.grp)]
        rows = [parts[0]] + [place.send(parts[k], k) for k in range(1, place.grp)]
        return jnp.concatenate(rows), sibling

    def pack(values, length):
        return jnp.concatenate([values, jnp.zeros((length - values.shape[0],), values.dtype)])

    slot = jnp.where(rank < room, shard * room + rank, slots)
    hit = slot[None, :] == jnp.arange(slots)[:, None]
    slot_ids = jnp.max(jnp.where(hit, flat_ids[None, :], -1), 1)
    early = jnp.concatenate(
        [
            slot_ids,
            false_neg.reshape(-1),
            valid,
            (jnp.max(rank) >= room).astype(jnp.int32)[None],
        ]
    )
    early = pack(early, -(-early.shape[0] // 1024) * 1024).reshape(-1, 128)
    grp_early = [early] + [place.send(early, k) for k in range(1, place.grp)]
    looked_up, sibling = fetch([item.reshape(-1)[:slots] for item in grp_early])
    early_all = jnp.stack(in_order(grp_early, place.g))
    early_all = gather_stage(place, early_all, place.y_masks, place.y)
    early_all = gather_stage(place, early_all, place.z_masks, place.z)
    early_all = early_all.reshape(place.count, -1)
    ids_all = early_all[:, :slots].reshape(place.blk, place.xs, 2, place.blk, room)
    at = slots
    false_neg_all = early_all[:, at : at + pairs_here * total_pairs].reshape(
        total_pairs, total_pairs
    )
    at += pairs_here * total_pairs
    valid_all = early_all[:, at : at + pairs_here].reshape(-1)
    at += pairs_here
    crowded = jnp.max(early_all[:, at]) > 0

    chip_room = max(16, tokens * 3 // 2 // place.blk // 16 * 16)
    chip_slots = place.blk * chip_room
    known = jnp.any(sibling[:, None] == flat_ids[None, :], 1)
    extra = (
        (sibling[None, :] >= 0)
        & ~known[None, :]
        & (sibling[None, :] // shard_rows == shard[:, None])
        & (sibling[None, :] < flat_ids[:, None])
    )
    chip_rank = rank + jnp.sum(extra.astype(jnp.int32), 1)
    shard_y, shard_z = shard % 2, shard // 2
    order = jnp.where(shard_y == place.core, 0, place.far) + (shard_z ^ place.z)
    gradient_slot = jnp.where(
        chip_rank < chip_room, order * chip_room + chip_rank, chip_slots
    )
    weights = (qkv_weight, out_weight, up_weight, down_weight)

    def encode(slot, found):
        return forward(
            lengths_flat, slot[:, None], found, small_rows, weights, seq_len, head_dim
        )

    def look_up_all():
        whole = lax.all_gather(word_table, "grp", axis=0, tiled=True)
        return jnp.arange(tokens, dtype=jnp.int32), whole[flat_ids]

    slot, found = lax.cond(
        crowded, look_up_all, lambda: (lookup_slots.astype(jnp.int32), looked_up)
    )
    (
        unit1,
        inverse1,
        normed_low,
        projected,
        probs,
        attended,
        unit2,
        inverse2,
        middle_low,
        activated_low,
        slope,
        unit3,
        inverse3,
        pooled,
        own_embed,
    ) = encode(slot, found)

    chip_crowded = (jnp.max(rank) >= room) | (jnp.max(chip_rank) >= chip_room)
    embed_rows = jnp.concatenate(
        [own_embed.reshape(-1, width), jnp.full((8, width), chip_crowded, low)]
    )
    gathered = gather_far_first(place, embed_rows).reshape(place.count, -1, width)
    rows_crowded = jnp.max(gathered[:, -1, 0].astype(jnp.float32)) > 0.5
    gathered = gathered[:, : 2 * pairs_here].reshape(total_pairs, 2, width)
    queries, documents = gathered[:, 0], gathered[:, 1]
    diagonal = jnp.arange(total_pairs)[:, None] == jnp.arange(total_pairs)[None, :]
    allowed = (valid_all[None, :] > 0) & ((false_neg_all == 0) | diagonal)
    scores = contract_cols(queries, documents) / logit_divisor_constant
    query_lse, query_probs = masked_softmax(scores, allowed)
    doc_lse, doc_probs = masked_softmax(scores.T, allowed)
    diag = jnp.sum(jnp.where(diagonal, scores, 0.0), -1)
    valid_floats = valid_all.astype(jnp.float32)
    pair_count = jnp.maximum(jnp.sum(valid_floats), 1.0)
    loss_total = jnp.sum(valid_floats * (query_lse + doc_lse - 2.0 * diag)) / 2.0
    row_weight = valid_floats / (2.0 * pair_count)
    identity_mask = diagonal.astype(jnp.float32)
    score_grad = (
        row_weight[:, None] * (query_probs - identity_mask)
        + (row_weight[:, None] * (doc_probs - identity_mask)).T
    )
    row_start = (place.b * place.grp + place.g) * pairs_here
    query_grad_rows = lax.dynamic_slice_in_dim(score_grad, row_start, pairs_here, 0)
    doc_grad_rows = lax.dynamic_slice_in_dim(score_grad, row_start, pairs_here, 1).T
    embed_grad = (
        jnp.stack(
            [
                jnp.dot(
                    query_grad_rows, documents.astype(jnp.float32), precision=finest_arithmetic
                ),
                jnp.dot(doc_grad_rows, queries.astype(jnp.float32), precision=finest_arithmetic),
            ],
            1,
        )
        / logit_divisor_constant
    )

    lowered_grad, lifted_low, second, feed_sums = feed_back(
        lengths_flat,
        embed_grad,
        (unit2, inverse2, slope, unit3, inverse3, pooled),
        small_rows,
        (up_weight, down_weight),
        seq_len,
    )
    theirs_down, mine_down = group_products(place, [(activated_low, lowered_grad)])
    lifted_low, theirs_down, mine_down = tie(lifted_low, theirs_down, mine_down)
    core_down = place.send(theirs_down, 1)
    theirs_up, mine_up = group_products(place, [(middle_low, lifted_low)])
    down = Reduction(place, mine_down + core_down.astype(jnp.float32), False)
    down.prepare()
    theirs_up, mine_up, down.parts = tie(theirs_up, mine_up, down.parts)
    down.send()
    core_up = place.send(theirs_up, 1)
    up = Reduction(place, mine_up + core_up.astype(jnp.float32), True)
    up.prepare()
    second, up.parts = tie(second, up.parts)
    up.send()
    branch_grad, projected_grad, mine_rows, theirs_rows, position_grad, attention_sums = attention_back(
        gradient_slot,
        second,
        (projected, probs, unit1, inverse1),
        small_rows,
        (qkv_weight, out_weight),
        seq_len,
        head_dim,
        chip_slots,
    )

    theirs_rows, down.arrived, up.arrived = tie(theirs_rows, down.arrived, up.arrived)
    rows = mine_rows + place.send(theirs_rows, 1).astype(jnp.float32)
    rows = rows.astype(low).reshape(place.far, chip_room, width)
    arrived = [place.send_swapped(rows[k], k) for k in range(place.far)]
    down.add()
    down.prepare()
    up.add()
    up.prepare()
    projected_grad, branch_grad, down.parts, up.parts = tie(
        projected_grad, branch_grad, down.parts, up.parts
    )
    down.send()
    theirs_two, mine_two = group_products(
        place, [(normed_low, projected_grad), (attended, branch_grad)]
    )
    arrived, down.arrived, up.parts, theirs_two, mine_two = tie(
        arrived, down.arrived, up.parts, theirs_two, mine_two
    )
    core_two = place.send(theirs_two, 1)
    up.send()
    arrived = jnp.concatenate(arrived)
    over_x = [arrived] + [place.send(arrived, mask) for mask in place.x_masks[1:]]

    small_grad = jnp.concatenate([position_grad, attention_sums[:4], feed_sums[:10]], 0)
    small_flat = small_grad.reshape(-1, strip)
    small_piece = -(-small_flat.shape[0] // (16 * place.count)) * 16
    small_padded = jnp.concatenate(
        [
            small_flat,
            jnp.zeros((small_piece * place.count - small_flat.shape[0], strip), jnp.float32),
        ]
    )
    small_parts = small_padded.reshape(place.blk, place.xs, 2, small_piece, strip)
    fine = small_piece
    small_mine = lax.dynamic_index_in_dim(small_parts, place.core, 2, keepdims=False)
    small_theirs = lax.dynamic_index_in_dim(small_parts, 1 - place.core, 2, keepdims=False)
    small_theirs = place.send(to_send(small_theirs, fine), 1)
    value_two = jnp.concatenate(
        [mine_two + core_two.astype(jnp.float32), small_mine + from_sent(small_theirs, fine)], 2
    )
    two = Reduction(place, value_two, False, fine)
    two.prepare()
    over_x, up.arrived, two.parts = tie(over_x, up.arrived, two.parts)
    two.send()
    down.add()
    up.add()
    one = Reduction(place, jnp.zeros((place.blk, place.xs, 16, strip), low), False)
    one.stages = one.stages[-1:]
    one.value = jnp.concatenate([down.value, up.value], 1)
    one.prepare()
    over_x, one.parts = tie(over_x, one.parts)
    one.send()
    sources = [item for value in over_x for item in (value, place.send(value, 1))]
    ids = lax.dynamic_index_in_dim(ids_all, place.b, 3, keepdims=False)
    ids = merge_ids(ids[:, :, 0], ids[:, :, 1], chip_room)
    ids = ids.reshape(place.far, 2, place.xs, chip_room)
    ids = jnp.stack(in_order([ids[i] for i in range(place.far)], place.z))
    ids = jnp.transpose(ids, (2, 1, 0, 3))
    local = ids - place.b * shard_rows
    inside = ids >= 0
    counts = jnp.sum(inside.astype(jnp.int32), -1).reshape(-1)
    local = jnp.where(inside, local, shard_rows).reshape(-1)
    def few_rows():
        return word_sum(place.g, counts, local, sources, shard_rows, place.far, chip_room)

    def all_rows():
        token_halves = attention_back(
            jnp.arange(tokens, dtype=jnp.int32),
            second,
            (projected, probs, unit1, inverse1),
            small_rows,
            (qkv_weight, out_weight),
            seq_len,
            head_dim,
            slots,
        )[2:4]
        token_grads = jnp.concatenate([token_halves[0].astype(low), token_halves[1]])
        every_id = lax.all_gather(flat_ids, "blk", axis=0, tiled=True) - place.b * shard_rows
        every_row = lax.all_gather(token_grads, "blk", axis=0, tiled=True)
        inside = (every_id >= 0) & (every_id < shard_rows)
        total = (
            jnp.zeros((shard_rows, width), jnp.float32)
            .at[jnp.where(inside, every_id, shard_rows)]
            .add(every_row.astype(jnp.float32), mode="drop")
        )
        total = lax.psum(total, "grp")
        return total, jnp.sum(total * total, 0, keepdims=True)

    word_rows, word_squares = lax.cond(rows_crowded, all_rows, few_rows)
    word_rows, word_squares, two.arrived, one.arrived = tie(
        word_rows, word_squares, two.arrived, one.arrived
    )
    two.add()
    two.prepare()
    two.send()
    one.add()
    two.add()
    two.prepare()
    one.value, two.parts = tie(one.value, two.parts)
    two.send()
    piece_one = one.value.astype(low)
    one_x = [piece_one] + [place.send(piece_one, mask) for mask in place.x_masks[1:]]
    two.add()
    cut = two.value.shape[0] - small_piece
    piece_two, small_own = two.value[:cut].astype(low), two.value[cut:]
    squares = jnp.sum(small_own * small_own, 0, keepdims=True)
    for item in (piece_one, piece_two):
        item = item.astype(jnp.float32)
        squares = squares + jnp.sum(item * item, 0, keepdims=True)
    squares = squares + jnp.sum(word_squares.reshape(-1, 1, strip), 0) / place.grp
    late = jnp.concatenate([small_own, jnp.broadcast_to(squares, (8, strip))])
    late, one_x = tie(late, one_x)
    late = gather_stage(place, late, place.z_masks, place.z)
    two_x = [piece_two] + [place.send(piece_two, mask) for mask in place.x_masks[1:]]
    late, two_x = tie(late, two_x)
    middle = [a + b for a in place.y_masks for b in place.x_masks]
    late = gather_stage(place, late, middle, place.y * place.xs + place.x)
    pieces_one = [item for value in one_x for item in (value, place.send(value, 1))]
    late, pieces_one = tie(late, pieces_one)
    late = gather_stage(place, late, place.core_masks, place.core)
    pieces_two = [item for value in two_x for item in (value, place.send(value, 1))]
    late = late.reshape((2, 2, place.xs, place.far) + late.shape[3:])
    late = jnp.transpose(late, (3, 1, 2, 0, 4, 5)).reshape(place.count, -1, strip)
    small_total = late[:, :small_piece].reshape(-1, strip)[: small_flat.shape[0]]
    small_total = small_total.reshape(small_grad.shape)
    grad_norm = jnp.sqrt(jnp.sum(late[:, small_piece]))
    factor = (clip_bound / jnp.maximum(grad_norm, clip_bound)).reshape(1)
    word_results = adam_rows(factor, word_rows, word_master, word_moments, rate_table[0])
    masters = (down_master, up_master, qkv_master, out_master, small_rows)
    moments = (down_moments, up_moments, qkv_moments, out_moments, small_moments)
    rates = tuple(rate_table[i] for i in (4, 3, 1, 2, 5))
    if all(item.shape[0] % (16 * place.xs) == 0 for item in masters[:4]):
        results = adam_matrices(
            place.g, factor, pieces_one, pieces_two, small_total, masters, moments, rates
        )
    else:
        ordered = [
            jnp.concatenate(pair)
            for pair in zip(in_order(pieces_one, place.g), in_order(pieces_two, place.g))
        ]
        ordered = jnp.stack(ordered).reshape((place.xs, 2) + ordered[0].shape)
        grads, at = [], 0
        for master in masters[:4]:
            rows, columns = master.shape[0] // place.xs, master.shape[1]
            length = rows * (columns // 2 // strip)
            part = ordered[:, :, at : at + length]
            grads.append(whole_rows(place, part, rows, columns).astype(jnp.float32))
            at += length
        grads.append(small_total)
        results = []
        for grad, moment, master, rate in zip(grads, moments, masters, rates):
            results.extend(adam_update(grad * factor[0], moment, master, rate))
    down, up, qkv, out, small = (results[3 * n : 3 * n + 3] for n in range(5))
    results = [*word_results, *qkv, *out, *up, *down, *small]
    return (loss_total, pair_count, grad_norm, *results)


def solution(mesh):
    in_specs = (
        P(both, None, None),
        P(both, None),
        P(both),
        P(both, None),
        P("grp", None),
        P(),
        P(),
        P(),
        P(),
        P("blk", None),
        P("blk", None),
        P("blk", None),
        P("blk", None),
        P("blk", None),
        P(None, "blk", None),
        P(None, "blk", None),
        P(None, "blk", None),
        P(None, "blk", None),
        P(None, "blk", None),
        P(),
        P(),
    )
    out_specs = (P(), P(), P()) + (P("blk", None),) * 15 + (P(), P(), P())
    return jax.shard_map(
        on_device, mesh=mesh, in_specs=in_specs, out_specs=out_specs, check_vma=False
    )
```

```python
import functools

import jax
import jax.numpy as jnp
from jax import lax
from jax.experimental import pallas as pl
from jax.experimental.pallas import tpu as pltpu
from jax.sharding import PartitionSpec as P

HEADS = 12
STEP = 5


logit_divisor_constant = 0.01
clip_bound = 0.001
beta_first = 0.5
beta_second = 0.5
decay_weight = 0.01
epsilon = 1e-08
rate_table = (0.1, 0.02, 0.1, 0.02, 0.01, 0.2)
finest_arithmetic = lax.Precision.HIGHEST
both = ("blk", "grp")
strip = 384


def contract_rows(left, right):
    return lax.dot_general(
        left, right, (((0,), (0,)), ((), ())), preferred_element_type=jnp.float32
    )


def contract_cols(left, right):
    return lax.dot_general(
        left, right, (((1,), (1,)), ((), ())), preferred_element_type=jnp.float32
    )


def adam_update(grad, moments, master, rate):
    first = beta_first * moments[0] + (1.0 - beta_first) * grad
    second = beta_second * moments[1] + (1.0 - beta_second) * grad * grad
    first_hat = first / (1.0 - beta_first**STEP)
    second_hat = second / (1.0 - beta_second**STEP)
    updated = master - rate * (first_hat / (jnp.sqrt(second_hat) + epsilon) + decay_weight * master)
    return (first, second, updated)


def masked_softmax(pairwise_affinity_matrix, allowed):
    masked = jnp.where(allowed, pairwise_affinity_matrix, -1000000000.0)
    top = jnp.max(masked, -1, keepdims=True)
    expo = jnp.where(allowed, jnp.exp(masked - top), 0.0)
    total = jnp.sum(expo, -1, keepdims=True)
    return (top[:, 0] + jnp.log(total[:, 0]), expo / total)


VMEM_ALLOWED = 56 * 1024 * 1024
low = jnp.bfloat16


def whole_block(shape):
    return pl.BlockSpec(shape, lambda *_: (0,) * len(shape), pipeline_mode=pl.Buffered(1))


def rows_block(rows, columns):
    return pl.BlockSpec((rows, columns), lambda i, *_: (i, 0))


def normalize(states):
    mean = jnp.mean(states, -1, keepdims=True)
    centered = states - mean
    inverse = lax.rsqrt(jnp.mean(centered * centered, -1, keepdims=True) + 1e-06)
    return centered * inverse, inverse


def normalize_back(grad, gain, unit_states, inverse):
    unit_states = unit_states.astype(jnp.float32)
    scaled = grad * gain
    inner = jnp.mean(scaled * unit_states, -1, keepdims=True)
    back = inverse * (scaled - jnp.mean(scaled, -1, keepdims=True) - unit_states * inner)
    return back, jnp.sum(grad * unit_states, 0, keepdims=True), jnp.sum(grad, 0, keepdims=True)


def gelu_and_slope(values):
    size = jnp.abs(values) * 0.7071067811865476
    t = 1.0 / (1.0 + 0.3275911 * size)
    series = t * (
        0.254829592
        + t * (-0.284496736 + t * (1.421413741 + t * (-1.453152027 + t * 1.061405429)))
    )
    bell = jnp.exp(-size * size)
    tail = 0.5 * series * bell
    below = jnp.where(values >= 0.0, 1.0 - tail, tail)
    return values * below, below + values * (0.3989422804014327 * bell)


def dot_rows(left, right):
    return lax.dot_general(
        left, right, (((0,), (0,)), ((), ())), preferred_element_type=jnp.float32
    )


def dot_cols(left, right):
    return lax.dot_general(
        left, right, (((1,), (1,)), ((), ())), preferred_element_type=jnp.float32
    )


def dot_plain(left, right):
    return jnp.dot(left, right, preferred_element_type=jnp.float32)


def head_masks(lanes, head_dim):
    even = (lax.broadcasted_iota(jnp.int32, (1, lanes), 1) < head_dim).astype(low)
    return even, (1.0 - even.astype(jnp.float32)).astype(low)


def forward_kernel(
    lengths_ref,
    slots_ref,
    found_ref,
    small_ref,
    qkv_ref,
    out_ref,
    up_ref,
    down_ref,
    unit1_ref,
    inverse1_ref,
    normed_ref,
    projected_ref,
    probs_ref,
    attended_ref,
    unit2_ref,
    inverse2_ref,
    middle_ref,
    activated_ref,
    slope_ref,
    unit3_ref,
    inverse3_ref,
    pooled_ref,
    embed_ref,
    *,
    seq_len,
    seqs,
    head_dim,
):
    step = pl.program_id(0)
    width = found_ref.shape[1]
    rows = seqs * seq_len
    slots = found_ref.shape[0]

    def vector(index):
        return small_ref[seq_len + index : seq_len + index + 1, :]

    pick = slots_ref[...] == lax.broadcasted_iota(jnp.int32, (rows, slots), 1)
    pick = jnp.where(pick, 1.0, 0.0).astype(low)
    embedded = dot_plain(pick, found_ref[...])
    positions = small_ref[:seq_len, :]
    embedded = embedded + jnp.concatenate([positions] * seqs, 0)
    unit1, inverse1 = normalize(embedded)
    unit1_ref[...] = unit1.astype(low)
    inverse1_ref[...] = inverse1
    normed = unit1 * vector(0) + vector(1)
    normed_low = normed.astype(low)
    normed_ref[...] = normed_low
    zeros = jnp.zeros((1, width), jnp.float32)
    for part, bias in enumerate((vector(2), zeros, vector(3))):
        at = slice(part * width, (part + 1) * width)
        projected_ref[:, at] = (dot_plain(normed_low, qkv_ref[:, at]) + bias).astype(low)
    lanes = 2 * head_dim
    even, odd = head_masks(lanes, head_dim)
    key_at = lax.broadcasted_iota(jnp.int32, (2 * seq_len, seq_len), 1)
    for s in range(seqs):
        at = slice(s * seq_len, (s + 1) * seq_len)
        live = key_at < lengths_ref[step * seqs + s]
        for p in range(width // lanes):
            query = projected_ref[at, p * lanes : (p + 1) * lanes]
            keys = projected_ref[at, width + p * lanes : width + (p + 1) * lanes]
            values = projected_ref[at, 2 * width + p * lanes : 2 * width + (p + 1) * lanes]
            query = jnp.concatenate([query * even, query * odd], 0)
            logits = dot_cols(query, keys) * head_dim ** (-0.5)
            logits = jnp.where(live, logits, -1000000000.0)
            expo = jnp.exp(logits - jnp.max(logits, -1, keepdims=True))
            probs = (expo / jnp.sum(expo, -1, keepdims=True)).astype(low)
            probs_ref[s, p] = probs
            both_probs = jnp.concatenate([probs[:seq_len], probs[seq_len:]], 1)
            both_values = jnp.concatenate([values * even, values * odd], 0)
            attended_ref[at, p * lanes : (p + 1) * lanes] = dot_plain(
                both_probs, both_values
            ).astype(low)
    branch = dot_plain(attended_ref[...], out_ref[...]) + vector(4)
    unit2, inverse2 = normalize(normed + branch)
    unit2_ref[...] = unit2.astype(low)
    inverse2_ref[...] = inverse2
    middle = unit2 * vector(5) + vector(6)
    middle_low = middle.astype(low)
    middle_ref[...] = middle_low
    lowered = middle + vector(7)
    for j in range(up_ref.shape[1] // width):
        at = slice(j * width, (j + 1) * width)
        lifted = dot_plain(middle_low, up_ref[:, at]) + vector(10 + j)
        activated, slope = gelu_and_slope(lifted)
        activated = activated.astype(low)
        activated_ref[:, at] = activated
        slope_ref[:, at] = slope.astype(low)
        lowered = lowered + dot_plain(activated, down_ref[at, :])
    unit3, inverse3 = normalize(lowered)
    unit3_ref[...] = unit3.astype(low)
    inverse3_ref[...] = inverse3
    final = unit3 * vector(8) + vector(9)
    row_at = lax.broadcasted_iota(jnp.int32, (seq_len, 1), 0)
    pooled = []
    for s in range(seqs):
        length = lengths_ref[step * seqs + s]
        weights = (row_at < length).astype(jnp.float32)
        total = jnp.sum(final[s * seq_len : (s + 1) * seq_len] * weights, 0, keepdims=True)
        pooled.append(total / length.astype(jnp.float32))
    pooled = jnp.concatenate(pooled, 0)
    pooled_ref[0] = pooled
    squares = jnp.sum(pooled * pooled, -1, keepdims=True)
    embed_ref[0] = (pooled * lax.rsqrt(squares + 1e-06)).astype(low)


def forward(lengths_flat, slot, found, small_rows, weights, seq_len, head_dim):
    tokens, width = slot.shape[0], found.shape[1]
    seqs = 2
    rows = seqs * seq_len
    steps = tokens // rows
    lifted = weights[2].shape[1]
    f32 = jnp.float32
    outs = [
        ((tokens, width), low),
        ((tokens, 1), f32),
        ((tokens, width), low),
        ((tokens, 3 * width), low),
        ((steps * seqs, width // (2 * head_dim), 2 * seq_len, seq_len), low),
        ((tokens, width), low),
        ((tokens, width), low),
        ((tokens, 1), f32),
        ((tokens, width), low),
        ((tokens, lifted), low),
        ((tokens, lifted), low),
        ((tokens, width), low),
        ((tokens, 1), f32),
        ((steps, seqs, width), f32),
        ((steps, seqs, width), low),
    ]

    def spec(shape):
        if shape[0] == tokens:
            return rows_block(rows, shape[1])
        block = (shape[0] // steps,) + shape[1:]
        return pl.BlockSpec(block, lambda i, *_: (i,) + (0,) * (len(shape) - 1))

    return pl.pallas_call(
        functools.partial(forward_kernel, seq_len=seq_len, seqs=seqs, head_dim=head_dim),
        out_shape=[jax.ShapeDtypeStruct(*item) for item in outs],
        grid_spec=pltpu.PrefetchScalarGridSpec(
            num_scalar_prefetch=1,
            grid=(steps,),
            in_specs=[rows_block(rows, 1), whole_block(found.shape), whole_block(small_rows.shape)]
            + [whole_block(item.shape) for item in weights],
            out_specs=[spec(item[0]) for item in outs],
        ),
        compiler_params=pltpu.CompilerParams(vmem_limit_bytes=VMEM_ALLOWED),
        cost_estimate=pl.CostEstimate(
            flops=20 * 10**9, bytes_accessed=50 * 10**6, transcendentals=10**7
        ),
        name="encoder_forward",
    )(lengths_flat, slot, found, small_rows, *weights)


def feed_back_kernel(
    lengths_ref,
    embed_grad_ref,
    pooled_ref,
    small_ref,
    unit3_ref,
    inverse3_ref,
    slope_ref,
    unit2_ref,
    inverse2_ref,
    up_ref,
    down_ref,
    lowered_ref,
    lifted_ref,
    second_ref,
    branch_ref,
    sums_ref,
    *,
    seq_len,
    seqs,
):
    step = pl.program_id(0)
    width = unit3_ref.shape[1]

    @pl.when(step == 0)
    def _():
        sums_ref[...] = jnp.zeros_like(sums_ref)

    def vector(index):
        return small_ref[seq_len + index : seq_len + index + 1, :]

    pooled, grad = pooled_ref[0], embed_grad_ref[0]
    inverse = lax.rsqrt(jnp.sum(pooled * pooled, -1, keepdims=True) + 1e-06)
    inner = jnp.sum(pooled * grad, -1, keepdims=True)
    pooled_grad = inverse * (grad - pooled * (inverse * inverse * inner))
    row_at = lax.broadcasted_iota(jnp.int32, (seq_len, 1), 0)
    final_grad = []
    for s in range(seqs):
        length = lengths_ref[step * seqs + s]
        weights = (row_at < length).astype(jnp.float32)
        final_grad.append(weights * (pooled_grad[s : s + 1] / length.astype(jnp.float32)))
    final_grad = jnp.concatenate(final_grad, 0)
    third, gain3, shift3 = normalize_back(
        final_grad, vector(8), unit3_ref[...], inverse3_ref[...]
    )
    lowered_grad = third.astype(low)
    lowered_ref[...] = lowered_grad
    middle_grad = third
    up_sums = []
    for j in range(up_ref.shape[1] // width):
        at = slice(j * width, (j + 1) * width)
        grad = dot_cols(lowered_grad, down_ref[at, :]) * slope_ref[:, at].astype(jnp.float32)
        grad = grad.astype(low)
        lifted_ref[:, at] = grad
        up_sums.append(jnp.sum(grad.astype(jnp.float32), 0, keepdims=True))
        middle_grad = middle_grad + dot_cols(grad, up_ref[:, at])
    second, gain2, shift2 = normalize_back(
        middle_grad, vector(5), unit2_ref[...], inverse2_ref[...]
    )
    second_ref[...] = second
    branch = second.astype(low)
    branch_ref[...] = branch
    branch_sum = jnp.sum(branch.astype(jnp.float32), 0, keepdims=True)
    lowered_sum = jnp.sum(lowered_grad.astype(jnp.float32), 0, keepdims=True)
    sums = [branch_sum, gain2, shift2, lowered_sum, gain3, shift3] + up_sums
    sums_ref[: len(sums), :] += jnp.concatenate(sums, 0)


def feed_back(lengths_flat, embed_grad, kept, small_rows, weights, seq_len):
    unit2, inverse2, slope, unit3, inverse3, pooled = kept
    tokens, width = unit2.shape
    lifted = slope.shape[1]
    seqs = 2
    rows = seqs * seq_len
    steps = tokens // rows
    pair = pl.BlockSpec((1, seqs, width), lambda i, *_: (i, 0, 0))
    return pl.pallas_call(
        functools.partial(feed_back_kernel, seq_len=seq_len, seqs=seqs),
        out_shape=[
            jax.ShapeDtypeStruct((tokens, width), low),
            jax.ShapeDtypeStruct((tokens, lifted), low),
            jax.ShapeDtypeStruct((tokens, width), jnp.float32),
            jax.ShapeDtypeStruct((tokens, width), low),
            jax.ShapeDtypeStruct((16, width), jnp.float32),
        ],
        grid_spec=pltpu.PrefetchScalarGridSpec(
            num_scalar_prefetch=1,
            grid=(steps,),
            in_specs=[
                pair,
                pair,
                whole_block(small_rows.shape),
                rows_block(rows, width),
                rows_block(rows, 1),
                rows_block(rows, lifted),
                rows_block(rows, width),
                rows_block(rows, 1),
                whole_block(weights[0].shape),
                whole_block(weights[1].shape),
            ],
            out_specs=[
                rows_block(rows, width),
                rows_block(rows, lifted),
                rows_block(rows, width),
                rows_block(rows, width),
                pl.BlockSpec((16, width), lambda i, *_: (0, 0)),
            ],
        ),
        compiler_params=pltpu.CompilerParams(vmem_limit_bytes=VMEM_ALLOWED),
        cost_estimate=pl.CostEstimate(
            flops=10 * 10**9, bytes_accessed=40 * 10**6, transcendentals=0
        ),
        name="feed_back",
    )(
        lengths_flat,
        embed_grad,
        pooled,
        small_rows,
        unit3,
        inverse3,
        slope,
        unit2,
        inverse2,
        *weights,
    )


def attention_back_kernel(
    slots_ref,
    second_ref,
    projected_ref,
    probs_ref,
    unit1_ref,
    inverse1_ref,
    small_ref,
    qkv_ref,
    out_ref,
    projected_grad_ref,
    mine_ref,
    theirs_ref,
    positions_ref,
    sums_ref,
    tokens_ref,
    *,
    seq_len,
    seqs,
    head_dim,
):
    step = pl.program_id(0)
    width = second_ref.shape[1]
    rows = seqs * seq_len
    lanes = 2 * head_dim
    scale = head_dim ** (-0.5)

    @pl.when(step == 0)
    def _():
        sums_ref[...] = jnp.zeros_like(sums_ref)
        positions_ref[...] = jnp.zeros_like(positions_ref)

    second = second_ref[...]
    attended_grad = dot_cols(second.astype(low), out_ref[...]).astype(low)
    even, odd = head_masks(lanes, head_dim)
    for s in range(seqs):
        at = slice(s * seq_len, (s + 1) * seq_len)
        for p in range(width // lanes):
            here = slice(p * lanes, (p + 1) * lanes)
            there = slice(width + p * lanes, width + (p + 1) * lanes)
            yonder = slice(2 * width + p * lanes, 2 * width + (p + 1) * lanes)
            query = projected_ref[at, here]
            keys = projected_ref[at, there]
            values = projected_ref[at, yonder]
            grad = attended_grad[at, here]
            grad = jnp.concatenate([grad * even, grad * odd], 0)
            query = jnp.concatenate([query * even, query * odd], 0)
            keys = jnp.concatenate([keys * even, keys * odd], 0)
            probs_low = probs_ref[s, p]
            probs = probs_low.astype(jnp.float32)
            probs_grad = dot_cols(grad, values)
            weighted = probs * probs_grad
            inner = jnp.sum(weighted, -1, keepdims=True)
            logits_grad = ((weighted - probs * inner) * scale).astype(low)
            both_grads = jnp.concatenate([logits_grad[:seq_len], logits_grad[seq_len:]], 1)
            projected_grad_ref[at, here] = dot_plain(both_grads, keys).astype(low)
            projected_grad_ref[at, there] = dot_rows(logits_grad, query).astype(low)
            projected_grad_ref[at, yonder] = dot_rows(probs_low, grad).astype(low)
    projected_grad = projected_grad_ref[...]
    query_sum = jnp.sum(projected_grad[:, :width].astype(jnp.float32), 0, keepdims=True)
    value_sum = jnp.sum(projected_grad[:, 2 * width :].astype(jnp.float32), 0, keepdims=True)
    normed_grad = second + dot_cols(projected_grad, qkv_ref[...])
    gain = small_ref[seq_len : seq_len + 1, :]
    embedded_grad, gain1, shift1 = normalize_back(
        normed_grad, gain, unit1_ref[...], inverse1_ref[...]
    )
    for s in range(seqs):
        positions_ref[...] += embedded_grad[s * seq_len : (s + 1) * seq_len]
    sums_ref[:4, :] += jnp.concatenate([gain1, shift1, query_sum, value_sum], 0)
    tokens_ref[pl.ds(step * rows, rows), :] = embedded_grad.astype(low)

    @pl.when(step == pl.num_programs(0) - 1)
    def _():
        half, tokens = mine_ref.shape[0], tokens_ref.shape[0]
        block = next(size for size in (256, 128, 64, 32, 16) if half % size == 0)
        for out_ref, base in ((mine_ref, 0), (theirs_ref, half)):
            for n in range(half // block):
                slot_at = lax.broadcasted_iota(jnp.int32, (block, tokens), 0)
                hit = slots_ref[...] == slot_at + (base + n * block)
                hit = jnp.where(hit, 1.0, 0.0).astype(low)
                out_ref[n * block : (n + 1) * block, :] = dot_plain(hit, tokens_ref[...]).astype(
                    out_ref.dtype
                )


def attention_back(slot, second, kept, small_rows, weights, seq_len, head_dim, slots):
    projected, probs, unit1, inverse1 = kept
    tokens, width = second.shape
    seqs = 2
    rows = seqs * seq_len
    steps = tokens // rows
    probs_block = (seqs,) + probs.shape[1:]

    def fixed(shape):
        return pl.BlockSpec(shape, lambda i, *_: (0, 0))

    return pl.pallas_call(
        functools.partial(
            attention_back_kernel, seq_len=seq_len, seqs=seqs, head_dim=head_dim
        ),
        out_shape=[
            jax.ShapeDtypeStruct((tokens, 3 * width), low),
            jax.ShapeDtypeStruct((slots // 2, width), jnp.float32),
            jax.ShapeDtypeStruct((slots // 2, width), low),
            jax.ShapeDtypeStruct((seq_len, width), jnp.float32),
            jax.ShapeDtypeStruct((8, width), jnp.float32),
        ],
        grid=(steps,),
        in_specs=[
            whole_block((1, tokens)),
            rows_block(rows, width),
            rows_block(rows, 3 * width),
            pl.BlockSpec(probs_block, lambda i: (i, 0, 0, 0)),
            rows_block(rows, width),
            rows_block(rows, 1),
            whole_block(small_rows.shape),
            whole_block(weights[0].shape),
            whole_block(weights[1].shape),
        ],
        out_specs=[
            rows_block(rows, 3 * width),
            fixed((slots // 2, width)),
            fixed((slots // 2, width)),
            fixed((seq_len, width)),
            fixed((8, width)),
        ],
        scratch_shapes=[pltpu.VMEM((tokens, width), low)],
        compiler_params=pltpu.CompilerParams(vmem_limit_bytes=VMEM_ALLOWED),
        cost_estimate=pl.CostEstimate(
            flops=10 * 10**9, bytes_accessed=30 * 10**6, transcendentals=0
        ),
        name="attention_back",
    )(slot.reshape(1, tokens), second, projected, probs, unit1, inverse1, small_rows, *weights)


def weight_grad_kernel(core_ref, *refs, jobs, xs):
    theirs_ref, mine_ref, turned_ref = refs[-3:]
    step = pl.program_id(0)
    start, base = 0, 0
    for n, (tiles, tall, piece, strips) in enumerate(jobs):
        left_ref, right_ref = refs[2 * n], refs[2 * n + 1]

        def work(start=start, base=base, left_ref=left_ref, right_ref=right_ref, job=jobs[n]):
            tiles, tall, piece, strips = job
            tile = step - start
            if tall or tiles == 1:
                grad = dot_rows(left_ref[...], right_ref[...])
            else:

                @pl.when(tile == 0)
                def _():
                    turned_ref[...] = left_ref[...].T

                grad = dot_plain(turned_ref[...], right_ref[...])
            count = grad.shape[0] // piece // xs
            for j in range(2):
                part = grad[:, j * strip : (j + 1) * strip]
                part = part.reshape(count, xs, piece, strip)
                if tall:
                    half = j
                    at = (pl.ds(tile * count, count), slice(None), pl.ds(base, piece))
                else:
                    number = 2 * tile + j
                    half = number // strips
                    row = pl.multiple_of(base + (number % strips) * piece, 16)
                    at = (slice(None), slice(None), pl.ds(row, piece))

                @pl.when(core_ref[0] == half)
                def _(at=at, part=part):
                    mine_ref[at] = part.astype(low)

                @pl.when(core_ref[0] != half)
                def _(at=at, part=part):
                    theirs_ref[at] = part.astype(low)

        pl.when((step >= start) & (step < start + tiles))(work)
        start += tiles
        base += piece * strips


def weight_grads(place, pairs):
    tile_rows = 2 * strip
    jobs, in_specs, operands = [], [], []
    start, rows = 0, 0
    tokens = pairs[0][0].shape[0]
    for left, right in pairs:
        strips = right.shape[1] // 2 // strip
        tall = left.shape[1] > tile_rows
        tiles = left.shape[1] // tile_rows if tall else strips
        piece = left.shape[1] // place.blk // place.xs

        def tile_of(i, start=start, tiles=tiles):
            return jnp.clip(i - start, 0, tiles - 1)

        def block(varies, f=tile_of):
            if varies:
                return pl.BlockSpec((tokens, tile_rows), lambda i, h: (0, f(i)))
            return whole_block((tokens, tile_rows))

        in_specs += [block(tall), block(not tall and tiles > 1)]
        jobs.append((tiles, tall, piece, strips))
        operands += [left, right]
        start += tiles
        rows += piece * strips
    shape = (place.blk, place.xs, rows, strip)
    return pl.pallas_call(
        functools.partial(weight_grad_kernel, jobs=jobs, xs=place.xs),
        out_shape=[
            jax.ShapeDtypeStruct(shape, low),
            jax.ShapeDtypeStruct(shape, low),
        ],
        grid_spec=pltpu.PrefetchScalarGridSpec(
            num_scalar_prefetch=1,
            grid=(start,),
            in_specs=in_specs,
            out_specs=[whole_block(shape), whole_block(shape)],
            scratch_shapes=[pltpu.VMEM((tile_rows, tokens), low)],
        ),
        compiler_params=pltpu.CompilerParams(vmem_limit_bytes=VMEM_ALLOWED),
        cost_estimate=pl.CostEstimate(flops=1000, bytes_accessed=1000, transcendentals=0),
        name="weight_grads",
    )(place.core.reshape(1).astype(jnp.int32), *operands)


def word_sum_kernel(
    place_ref, count_ref, id_ref, *refs, sources, chunks, room, span, own, finishing
):
    inputs, rest = refs[:sources], refs[sources:]
    if finishing:
        base_ref, out_ref, squares_ref, total_ref, rows_ref, chunk_ref = rest[:6]
        in_sems, out_sem, base_total_ref, base_sem = rest[6:]
        base_copy = pltpu.make_async_copy(base_ref, base_total_ref, base_sem)
        base_copy.start()
    else:
        out_ref, total_ref, rows_ref, chunk_ref, in_sems, out_sem = rest
    batch = 8
    copies = [
        pltpu.make_async_copy(inputs[k], rows_ref.at[k], in_sems.at[k]) for k in range(sources)
    ]
    for copy in copies:
        copy.start()
    zeros = jnp.zeros((batch, total_ref.shape[1]), jnp.float32)

    def clear(i, _):
        total_ref[pl.ds(pl.multiple_of(i * batch, batch), batch), :] = zeros
        return 0

    lax.fori_loop(0, total_ref.shape[0] // batch, clear, 0, unroll=4)
    for copy in copies:
        copy.wait()

    def one_source(m, _):
        me = place_ref[0]
        place = m // chunks
        if sources == 2:
            x = (me // 2) ^ (own // 2)
            source = x * 2 + place
        else:
            x = place // 2
            x = x + jnp.where(x >= me // 2, 1, 0)
            source = x * 2 + place % 2
        slot = (source ^ me) - own
        n = source * chunks + m % chunks
        start = (m % chunks) * room
        count = count_ref[n]

        def widen(i, _):
            at = pl.ds(pl.multiple_of(start + i * 16, 16), 16)
            to = pl.ds(pl.multiple_of(i * 16, 16), 16)
            chunk_ref[to, :] = rows_ref[slot, at, :].astype(jnp.float32)
            return 0

        lax.fori_loop(0, (count + 15) // 16, widen, 0)

        def add(i, _):
            at = [id_ref[n * room + i * batch + j] for j in range(batch)]
            sums = [
                total_ref[pl.ds(at[j], 1), :] + chunk_ref[pl.ds(i * batch + j, 1), :]
                for j in range(batch)
            ]
            for j in range(batch):
                total_ref[pl.ds(at[j], 1), :] = sums[j]
            return 0

        lax.fori_loop(0, (count + batch - 1) // batch, add, 0)
        return 0

    lax.fori_loop(0, sources * chunks, one_source, 0)
    shard_rows = out_ref.shape[0]
    if not finishing:
        copy = pltpu.make_async_copy(total_ref.at[pl.ds(0, shard_rows)], out_ref, out_sem)
        copy.start()
        copy.wait()
        return
    base_copy.wait()

    def finish(i, squares):
        at = pl.ds(pl.multiple_of(i * span, span), span)
        part = total_ref[at, :] + base_total_ref[at, :]
        total_ref[at, :] = part
        pltpu.make_async_copy(total_ref.at[at], out_ref.at[at], out_sem).start()
        part = part * part
        return squares + jnp.sum(part.reshape(span // 8, 8, part.shape[1]), 0)

    squares = lax.fori_loop(
        0, shard_rows // span, finish, jnp.zeros((8, total_ref.shape[1]), jnp.float32)
    )
    squares_ref[...] = jnp.sum(squares, 0, keepdims=True)
    pltpu.make_async_copy(total_ref.at[pl.ds(0, shard_rows)], out_ref, out_sem).wait()


def word_sum(grp_index, counts, ids, sources, shard_rows, chunks, room, base=None):
    count, width = len(sources), sources[0].shape[1]
    span = next(size for size in (128, 64, 32, 16, 8) if shard_rows % size == 0)
    anywhere = pl.BlockSpec(memory_space=pl.ANY)
    finishing = base is not None
    out_shape = [jax.ShapeDtypeStruct((shard_rows, width), jnp.float32)]
    out_specs = [anywhere]
    scratch = [
        pltpu.VMEM((shard_rows + 32, width), jnp.float32),
        pltpu.VMEM((count,) + sources[0].shape, low),
        pltpu.VMEM((room, width), jnp.float32),
        pltpu.SemaphoreType.DMA((count,)),
        pltpu.SemaphoreType.DMA,
    ]
    operands = list(sources)
    if finishing:
        out_shape.append(jax.ShapeDtypeStruct((1, width), jnp.float32))
        out_specs.append(whole_block((1, width)))
        scratch += [pltpu.VMEM((shard_rows, width), jnp.float32), pltpu.SemaphoreType.DMA]
        operands.append(base)
    results = pl.pallas_call(
        functools.partial(
            word_sum_kernel,
            sources=count,
            chunks=chunks,
            room=room,
            span=span,
            own=2 if finishing else 0,
            finishing=finishing,
        ),
        out_shape=out_shape,
        grid_spec=pltpu.PrefetchScalarGridSpec(
            num_scalar_prefetch=3,
            grid=(1,),
            in_specs=[anywhere] * len(operands),
            out_specs=out_specs,
            scratch_shapes=scratch,
        ),
        compiler_params=pltpu.CompilerParams(vmem_limit_bytes=VMEM_ALLOWED),
        cost_estimate=pl.CostEstimate(flops=1000, bytes_accessed=1000, transcendentals=0),
        name="word_sum",
    )(grp_index.reshape(1), counts, ids, *operands)
    return results if finishing else results[0]


def adam_kernel(factor_ref, grad_ref, master_ref, moments_ref, first_ref, second_ref, new_ref, *, rate):
    results = adam_update(
        grad_ref[...] * factor_ref[0], (moments_ref[0], moments_ref[1]), master_ref[...], rate
    )
    first_ref[...], second_ref[...], new_ref[...] = results


def adam_rows(factor, grad, master, moments, rate):
    rows, width = master.shape
    span = next(size for size in (384, 320, 240, 192, 128, 96, 64, 32, 16, 8) if rows % size == 0)
    block = rows_block(span, width)
    return pl.pallas_call(
        functools.partial(adam_kernel, rate=rate),
        out_shape=[jax.ShapeDtypeStruct((rows, width), jnp.float32)] * 3,
        grid=(rows // span,),
        in_specs=[
            pl.BlockSpec(memory_space=pltpu.SMEM),
            block,
            block,
            pl.BlockSpec((2, span, width), lambda i: (0, i, 0)),
        ],
        out_specs=[block] * 3,
        compiler_params=pltpu.CompilerParams(vmem_limit_bytes=VMEM_ALLOWED),
        cost_estimate=pl.CostEstimate(
            flops=20 * rows * width, bytes_accessed=28 * rows * width, transcendentals=0
        ),
        name="adam_rows",
    )(factor, grad, master, moments)


def adam_matrices_kernel(place_ref, factor_ref, *refs, grp, shapes, rates):
    count = len(shapes)
    pieces, rest = (refs[:grp], refs[grp : 2 * grp]), refs[2 * grp :]
    small_ref, rest = rest[0], rest[1:]
    masters, rest = rest[: count + 1], rest[count + 1 :]
    moments, rest = rest[: count + 1], rest[count + 1 :]
    outs, scratch = rest[: 3 * count + 3], rest[3 * count + 3 :]
    factor = factor_ref[0]
    base = 0
    for n, (rows, width) in enumerate(shapes):
        strips = width // 2 // strip
        piece = rows // (grp // 2)
        group = pieces[n // 3]
        base = 0 if n % 3 == 0 else base
        for k in range(grp):
            source = place_ref[0] ^ k
            x, core = source // 2, source % 2
            for s in range(strips):
                part = group[k][base + s * piece : base + (s + 1) * piece, :]
                to_row = pl.multiple_of(x * piece, 16)
                to_column = pl.multiple_of((core * strips + s) * strip, 128)
                scratch[n][pl.ds(to_row, piece), pl.ds(to_column, strip)] = part.astype(
                    jnp.float32
                )
        base += strips * piece
    for n in range(count + 1):
        grad = small_ref[...] if n == count else scratch[n][...]
        results = adam_update(
            grad * factor, (moments[n][0], moments[n][1]), masters[n][...], rates[n]
        )
        for m in range(3):
            outs[3 * n + m][...] = results[m]


def adam_matrices(grp_index, factor, pieces_one, pieces_two, small, masters, moments, rates):
    shapes = [item.shape for item in masters]
    count = len(shapes) - 1
    operands = [*pieces_one, *pieces_two, small, *masters, *moments]
    return pl.pallas_call(
        functools.partial(
            adam_matrices_kernel, grp=len(pieces_one), shapes=shapes[:count], rates=rates
        ),
        out_shape=[jax.ShapeDtypeStruct(s, jnp.float32) for s in shapes for _ in range(3)],
        grid_spec=pltpu.PrefetchScalarGridSpec(
            num_scalar_prefetch=1,
            grid=(1,),
            in_specs=[pl.BlockSpec(memory_space=pltpu.SMEM)]
            + [whole_block(item.shape) for item in operands],
            out_specs=[whole_block(s) for s in shapes for _ in range(3)],
            scratch_shapes=[pltpu.VMEM(s, jnp.float32) for s in shapes[:count]],
        ),
        compiler_params=pltpu.CompilerParams(vmem_limit_bytes=VMEM_ALLOWED),
        cost_estimate=pl.CostEstimate(
            flops=10**8, bytes_accessed=30 * 10**6, transcendentals=0
        ),
        name="adam_matrices",
    )(grp_index.reshape(1), factor, *operands)


class Place:
    def __init__(self):
        self.blk, self.grp = lax.axis_size("blk"), lax.axis_size("grp")
        self.count = self.blk * self.grp
        self.b, self.g = lax.axis_index("blk"), lax.axis_index("grp")
        self.xs, self.far = self.grp // 2, self.blk // 2
        self.core, self.x = self.g % 2, self.g // 2
        self.y, self.z = self.b % 2, self.b // 2
        self.core_masks = [0, 1]
        self.x_masks = [2 * i for i in range(self.xs)]
        self.y_masks = [0, self.grp]
        self.z_masks = [2 * self.grp * i for i in range(self.far)]

    def send_split(self, value, far_mask):
        masks = [2 * self.grp * far_mask + self.grp * core for core in range(2)]
        return lax.ppermute(value, both, [(i, i ^ masks[i % 2]) for i in range(self.count)])

    def send(self, value, mask):
        pairs = [(i, i ^ mask) for i in range(self.count)]
        return lax.ppermute(value, both, pairs)


def in_order(pieces, index):
    step = 1
    while step < len(pieces):
        odd = (index & step) != 0
        pieces = [jnp.where(odd, pieces[i ^ step], pieces[i]) for i in range(len(pieces))]
        step *= 2
    return pieces


def gather_stage(place, value, masks, index):
    pieces = [value] + [place.send(value, mask) for mask in masks[1:]]
    return jnp.stack(in_order(pieces, index))


def gather_far_first(place, value):
    shape = value.shape
    value = gather_stage(place, value, place.z_masks, place.z)
    middle = [a + b for a in place.y_masks for b in place.x_masks]
    value = gather_stage(place, value, middle, place.y * place.xs + place.x)
    value = gather_stage(place, value, place.core_masks, place.core)
    value = value.reshape((2, 2, place.xs, place.far) + shape)
    return jnp.transpose(value, (3, 1, 2, 0) + tuple(range(4, 4 + len(shape)))).reshape(
        (place.blk, place.grp) + shape
    )


def two_terms(value):
    high = lax.reduce_precision(value, 8, 7)
    return jnp.concatenate([high, value - high], -2).astype(low)


def one_term(value):
    value = value.astype(jnp.float32)
    rows = value.shape[-2] // 2
    return value[..., :rows, :] + value[..., rows:, :]


def add_up(terms):
    while len(terms) > 1:
        terms = [terms[i] + terms[i + 1] for i in range(0, len(terms), 2)]
    return terms[0]


class Reduction:
    def __init__(self, place, value, x_first, small=None):
        self.place = place
        self.value, self.small = self.shaped(value), self.shaped(small)
        x_stage = (place.x_masks, place.x)
        y_stage = (place.y_masks, place.y)
        if x_first:
            self.stages = [(*x_stage, 2), (*y_stage, 1)]
        else:
            self.stages = [(*y_stage, 1), (*x_stage, 1)]
        self.stages.append((place.z_masks, place.z, 0))

    def shaped(self, value):
        if value is None:
            return None
        place = self.place
        return value.reshape((place.far, 2, place.xs) + value.shape[2:])

    def prepare(self):
        self.masks, self.index, axis = self.stages.pop(0)
        self.value = jnp.moveaxis(self.value, axis, 0)
        if self.small is not None:
            self.small = jnp.moveaxis(self.small, axis, 0)
        self.parts = []
        for k in range(1, len(self.masks)):
            at = self.index ^ k
            part = lax.dynamic_index_in_dim(self.value, at, 0, keepdims=False).astype(low)
            if self.small is not None:
                small = lax.dynamic_index_in_dim(self.small, at, 0, keepdims=False)
                part = jnp.concatenate([part, two_terms(small)], -2)
            self.parts.append(part)

    def send(self):
        self.arrived = [
            self.place.send(part, mask) for part, mask in zip(self.parts, self.masks[1:])
        ]

    def add(self):
        rows = self.value.shape[-2]
        own = lax.dynamic_index_in_dim(self.value, self.index, 0, keepdims=False)
        arrived = [item[..., :rows, :].astype(jnp.float32) for item in self.arrived]
        self.value = add_up([own.astype(jnp.float32)] + arrived)
        if self.small is not None:
            own = lax.dynamic_index_in_dim(self.small, self.index, 0, keepdims=False)
            self.small = add_up([own] + [one_term(item[..., rows:, :]) for item in self.arrived])


def tie(*items):
    return lax.optimization_barrier(items)


def half_gradient(place, left, right, core):
    width = right.shape[1] // 2
    part = lax.dynamic_slice_in_dim(right, core * width, width, 1)
    grad = contract_rows(left, part).astype(jnp.bfloat16)
    rows = grad.shape[0] // place.blk // place.xs
    strips = width // strip
    grad = grad.reshape(place.blk, place.xs, rows, strips, strip)
    return jnp.transpose(grad, (0, 1, 3, 2, 4)).reshape(
        place.blk, place.xs, strips * rows, strip
    )


def group_products(place, pairs):
    if all(a.shape[1] % (16 * place.blk * place.xs) == 0 for a, _ in pairs):
        return weight_grads(place, pairs)
    mine = [half_gradient(place, a, b, place.core) for a, b in pairs]
    theirs = [half_gradient(place, a, b, 1 - place.core) for a, b in pairs]
    return jnp.concatenate(theirs, 2), jnp.concatenate(mine, 2)


def merge_ids(left, right, length):
    hits = []
    for own, other in ((left, right), (right, left)):
        repeated = jnp.any(other[..., :, None] == own[..., None, :], -1)
        lower = (
            (other >= 0)[..., None, :]
            & ~repeated[..., None, :]
            & (other[..., None, :] < own[..., :, None])
        )
        rank = jnp.arange(own.shape[-1]) + jnp.sum(lower.astype(jnp.int32), -1)
        hit = rank[..., None, :] == jnp.arange(length)[:, None]
        hits.append(jnp.max(jnp.where(hit, own[..., None, :], -1), -1))
    return jnp.maximum(*hits)


def whole_rows(place, pieces, rows, width):
    strips = width // 2 // strip
    pieces = pieces.reshape(place.xs, 2, strips, rows, strip)
    return jnp.transpose(pieces, (0, 3, 1, 2, 4)).reshape(place.xs * rows, width)


def on_device(
    token_ids,
    lengths,
    valid,
    false_neg,
    word_table,
    qkv_weight,
    out_weight,
    up_weight,
    down_weight,
    word_master,
    qkv_master,
    out_master,
    up_master,
    down_master,
    word_moments,
    qkv_moments,
    out_moments,
    up_moments,
    down_moments,
    small_rows,
    small_moments,
):
    place = Place()
    pairs_here = token_ids.shape[0]
    total_pairs = pairs_here * place.count
    seq_count = 2 * pairs_here
    seq_len = token_ids.shape[2]
    width = word_table.shape[1]
    head_dim = width // HEADS
    flat_ids = token_ids.reshape(-1)
    tokens = flat_ids.shape[0]
    lengths_flat = lengths.reshape(-1)

    shard_rows = word_master.shape[0]
    table_rows = word_table.shape[0]
    per_owner = table_rows // shard_rows
    room = max(16, tokens * 7 // 8 // place.blk)
    shard = flat_ids // shard_rows
    same_id = flat_ids[:, None] == flat_ids[None, :]
    before = jnp.arange(tokens)[:, None] < jnp.arange(tokens)[None, :]
    first = ~jnp.any(same_id & before, 0)
    smaller = (
        (shard[:, None] == shard[None, :])
        & (flat_ids[None, :] < flat_ids[:, None])
        & first[None, :]
    )
    rank = jnp.sum(smaller.astype(jnp.int32), 1)
    slots = place.blk * room

    owner = shard // per_owner
    relative = ((owner ^ place.g) * per_owner + shard % per_owner) * room + rank
    lookup_slots = jnp.where(rank < room, relative, slots)

    def fetch(grp_ids):
        span = per_owner * room
        asked = [lax.dynamic_slice_in_dim(ids, place.g * span, span) for ids in grp_ids]
        local = jnp.concatenate(asked) - place.g * table_rows
        found = word_table.at[jnp.clip(local, 0, table_rows - 1)].get(mode="clip")
        found, sibling = tie(found, grp_ids[1])
        parts = [found[k * span : (k + 1) * span] for k in range(place.grp)]
        rows = [parts[0]] + [place.send(parts[k], k) for k in range(1, place.grp)]
        rows.append(jnp.zeros((tokens - slots, width), low))
        return jnp.concatenate(rows), sibling

    def pack(values, length):
        return jnp.concatenate([values, jnp.zeros((length - values.shape[0],), values.dtype)])

    slot = jnp.where(rank < room, shard * room + rank, slots)
    hit = slot[None, :] == jnp.arange(slots)[:, None]
    slot_ids = jnp.max(jnp.where(hit, flat_ids[None, :], -1), 1)
    early = jnp.concatenate(
        [
            slot_ids,
            false_neg.reshape(-1),
            valid,
            (jnp.max(rank) >= room).astype(jnp.int32)[None],
        ]
    )
    early = pack(early, -(-early.shape[0] // 1024) * 1024).reshape(-1, 128)
    grp_early = [early] + [place.send(early, k) for k in range(1, place.grp)]
    looked_up, sibling = fetch([item.reshape(-1)[:slots] for item in grp_early])
    early_all = jnp.stack(in_order(grp_early, place.g))
    early_all = gather_stage(place, early_all, place.y_masks, place.y)
    early_all = gather_stage(place, early_all, place.z_masks, place.z)
    early_all = early_all.reshape(place.count, -1)
    ids_all = early_all[:, :slots].reshape(place.blk, place.xs, 2, place.blk, room)
    at = slots
    false_neg_all = early_all[:, at : at + pairs_here * total_pairs].reshape(
        total_pairs, total_pairs
    )
    at += pairs_here * total_pairs
    valid_all = early_all[:, at : at + pairs_here].reshape(-1)
    at += pairs_here
    crowded = jnp.max(early_all[:, at]) > 0

    chip_room = max(16, tokens * 3 // 2 // place.blk // 16 * 16)
    chip_slots = place.blk * chip_room
    known = jnp.any(sibling[:, None] == flat_ids[None, :], 1)
    extra = (
        (sibling[None, :] >= 0)
        & ~known[None, :]
        & (sibling[None, :] // shard_rows == shard[:, None])
        & (sibling[None, :] < flat_ids[:, None])
    )
    chip_rank = rank + jnp.sum(extra.astype(jnp.int32), 1)
    shard_y, shard_z = shard % 2, shard // 2
    order = jnp.where(shard_y ^ place.y == place.core, 0, place.far) + (shard_z ^ place.z)
    gradient_slot = jnp.where(
        chip_rank < chip_room, order * chip_room + chip_rank, chip_slots
    )
    weights = (qkv_weight, out_weight, up_weight, down_weight)

    def encode(slot, found):
        return forward(
            lengths_flat, slot[:, None], found, small_rows, weights, seq_len, head_dim
        )

    def look_up_all():
        whole = lax.all_gather(word_table, "grp", axis=0, tiled=True)
        return jnp.arange(tokens, dtype=jnp.int32), whole[flat_ids]

    slot, found = lax.cond(
        crowded, look_up_all, lambda: (lookup_slots.astype(jnp.int32), looked_up)
    )
    (
        unit1,
        inverse1,
        normed_low,
        projected,
        probs,
        attended,
        unit2,
        inverse2,
        middle_low,
        activated_low,
        slope,
        unit3,
        inverse3,
        pooled,
        own_embed,
    ) = encode(slot, found)

    chip_crowded = (jnp.max(rank) >= room) | (jnp.max(chip_rank) >= chip_room)
    embed_rows = jnp.concatenate(
        [own_embed.reshape(-1, width), jnp.full((8, width), chip_crowded, low)]
    )
    gathered = gather_far_first(place, embed_rows).reshape(place.count, -1, width)
    rows_crowded = jnp.max(gathered[:, -1, 0].astype(jnp.float32)) > 0.5
    gathered = gathered[:, : 2 * pairs_here].reshape(total_pairs, 2, width)
    queries, documents = gathered[:, 0], gathered[:, 1]
    diagonal = jnp.arange(total_pairs)[:, None] == jnp.arange(total_pairs)[None, :]
    allowed = (valid_all[None, :] > 0) & ((false_neg_all == 0) | diagonal)
    scores = contract_cols(queries, documents) / logit_divisor_constant
    query_lse, query_probs = masked_softmax(scores, allowed)
    doc_lse, doc_probs = masked_softmax(scores.T, allowed)
    diag = jnp.sum(jnp.where(diagonal, scores, 0.0), -1)
    valid_floats = valid_all.astype(jnp.float32)
    pair_count = jnp.maximum(jnp.sum(valid_floats), 1.0)
    loss_total = jnp.sum(valid_floats * (query_lse + doc_lse - 2.0 * diag)) / 2.0
    row_weight = valid_floats / (2.0 * pair_count)
    identity_mask = diagonal.astype(jnp.float32)
    score_grad = (
        row_weight[:, None] * (query_probs - identity_mask)
        + (row_weight[:, None] * (doc_probs - identity_mask)).T
    )
    row_start = (place.b * place.grp + place.g) * pairs_here
    query_grad_rows = lax.dynamic_slice_in_dim(score_grad, row_start, pairs_here, 0)
    doc_grad_rows = lax.dynamic_slice_in_dim(score_grad, row_start, pairs_here, 1).T
    embed_grad = (
        jnp.stack(
            [
                jnp.dot(
                    query_grad_rows, documents.astype(jnp.float32), precision=finest_arithmetic
                ),
                jnp.dot(doc_grad_rows, queries.astype(jnp.float32), precision=finest_arithmetic),
            ],
            1,
        )
        / logit_divisor_constant
    )

    lowered_grad, lifted_low, second, branch_grad, feed_sums = feed_back(
        lengths_flat,
        embed_grad,
        (unit2, inverse2, slope, unit3, inverse3, pooled),
        small_rows,
        (up_weight, down_weight),
        seq_len,
    )
    theirs_down, mine_down = group_products(place, [(activated_low, lowered_grad)])
    lifted_low, theirs_down, mine_down = tie(lifted_low, theirs_down, mine_down)
    core_down = place.send(theirs_down, 1)
    theirs_up, mine_up = group_products(
        place, [(middle_low, lifted_low), (attended, branch_grad)]
    )
    down = Reduction(place, mine_down.astype(jnp.float32) + core_down.astype(jnp.float32), False)
    down.prepare()
    theirs_up, mine_up, down.parts = tie(theirs_up, mine_up, down.parts)
    down.send()
    core_up = place.send(theirs_up, 1)
    up = Reduction(place, mine_up.astype(jnp.float32) + core_up.astype(jnp.float32), True)
    up.prepare()
    second, up.parts = tie(second, up.parts)
    up.send()
    projected_grad, mine_rows, theirs_rows, position_grad, attention_sums = attention_back(
        gradient_slot,
        second,
        (projected, probs, unit1, inverse1),
        small_rows,
        (qkv_weight, out_weight),
        seq_len,
        head_dim,
        chip_slots,
    )

    theirs_rows, position_grad, down.arrived, up.arrived = tie(
        theirs_rows, position_grad, down.arrived, up.arrived
    )
    ids = lax.dynamic_index_in_dim(ids_all, place.b, 3, keepdims=False)
    ids = merge_ids(ids[:, :, 0], ids[:, :, 1], chip_room)
    ids = ids.reshape(place.far, 2, place.xs, chip_room)
    ids = jnp.stack(in_order([ids[i] for i in range(place.far)], place.z))
    ids = jnp.stack(in_order([ids[:, 0], ids[:, 1]], place.y), 1)
    ids = jnp.transpose(ids, (2, 1, 0, 3))
    local = ids - place.b * shard_rows
    inside = ids >= 0
    counts = jnp.sum(inside.astype(jnp.int32), -1).reshape(-1)
    local = jnp.where(inside, local, shard_rows).reshape(-1)
    small_grad = jnp.concatenate([position_grad, attention_sums[:4], feed_sums[:10]], 0)
    small_flat = small_grad.reshape(-1, strip)
    small_piece = -(-small_flat.shape[0] // (16 * place.count)) * 16
    small_padded = jnp.concatenate(
        [
            small_flat,
            jnp.zeros((small_piece * place.count - small_flat.shape[0], strip), jnp.float32),
        ]
    )
    small_parts = small_padded.reshape(place.blk, place.xs, 2, small_piece, strip)
    small_mine = lax.dynamic_index_in_dim(small_parts, place.core, 2, keepdims=False)
    small_theirs = lax.dynamic_index_in_dim(small_parts, 1 - place.core, 2, keepdims=False)
    rows = mine_rows + place.send(theirs_rows, 1).astype(jnp.float32)
    small_value = small_mine + one_term(place.send(two_terms(small_theirs), 1))
    rows = rows.astype(low).reshape(place.far, chip_room, width)
    down.add()
    down.prepare()
    up.add()
    up.prepare()
    first_rows = jnp.concatenate([rows[0, :, :strip], rows[0, :, strip:]])
    rows, first_rows, small_value, projected_grad, down.parts, up.parts, counts, local = tie(
        rows, first_rows, small_value, projected_grad, down.parts, up.parts, counts, local
    )
    arrived = [place.send_split(rows[k], k) for k in range(1, place.far)]
    down.send()
    up_shape = up.parts[0].shape
    up_y = place.send(jnp.concatenate([up.parts[0].reshape(-1, strip), first_rows]), place.grp)
    theirs_two, mine_two = group_products(place, [(normed_low, projected_grad)])
    arrived, down.arrived, up_y, theirs_two, mine_two = tie(
        arrived, down.arrived, up_y, theirs_two, mine_two
    )
    cut = up_y.shape[0] - first_rows.shape[0]
    up.arrived = [up_y[:cut].reshape(up_shape)]
    other_y = jnp.concatenate([up_y[cut : cut + chip_room], up_y[cut + chip_room :]], 1)
    arrived = jnp.concatenate([jnp.where(place.core == 0, rows[0], other_y)] + arrived)
    over_x = [arrived] + [place.send(arrived, mask) for mask in place.x_masks[1:]]
    core_two = place.send(theirs_two, 1)
    near = [arrived, place.send(arrived, 1)]
    two = Reduction(
        place, mine_two.astype(jnp.float32) + core_two.astype(jnp.float32), False, small_value
    )
    two.prepare()
    down.add()
    up.add()
    one = Reduction(place, jnp.zeros((place.blk, place.xs, 16, strip), low), False)
    one.stages = one.stages[-1:]
    one.value = jnp.concatenate([down.value, up.value], 1)
    one.prepare()
    near, two.parts, one.parts = tie(near, two.parts, one.parts)
    two.send()
    one.send()
    own_total = word_sum(
        place.g, counts, local, near, shard_rows, place.far, chip_room
    )
    own_total, two.arrived, over_x = tie(own_total, two.arrived, over_x)
    others = [item for value in over_x[1:] for item in (value, place.send(value, 1))]
    two.add()
    two.prepare()
    others, two.parts = tie(others, two.parts)
    two.send()

    def few_rows():
        return word_sum(
            place.g, counts, local, others, shard_rows, place.far, chip_room, own_total
        )

    def all_rows():
        token_halves = attention_back(
            jnp.arange(tokens, dtype=jnp.int32),
            second,
            (projected, probs, unit1, inverse1),
            small_rows,
            (qkv_weight, out_weight),
            seq_len,
            head_dim,
            tokens,
        )[1:3]
        token_grads = jnp.concatenate([token_halves[0].astype(low), token_halves[1]])
        every_id = lax.all_gather(flat_ids, "blk", axis=0, tiled=True) - place.b * shard_rows
        every_row = lax.all_gather(token_grads, "blk", axis=0, tiled=True)
        inside = (every_id >= 0) & (every_id < shard_rows)
        total = (
            jnp.zeros((shard_rows, width), jnp.float32)
            .at[jnp.where(inside, every_id, shard_rows)]
            .add(every_row.astype(jnp.float32), mode="drop")
        )
        total = lax.psum(total, "grp")
        return total, jnp.sum(total * total, 0, keepdims=True)

    word_rows, word_squares = lax.cond(rows_crowded, all_rows, few_rows)
    word_rows, word_squares, two.arrived, one.arrived = tie(
        word_rows, word_squares, two.arrived, one.arrived
    )
    two.add()
    two.prepare()
    two.send()
    one.add()
    two.add()
    piece_one = one.value.astype(low)
    one_x = [piece_one] + [place.send(piece_one, mask) for mask in place.x_masks[1:]]
    piece_two, small_own = two.value.astype(low), two.small
    squares = jnp.sum(small_own * small_own, 0, keepdims=True)
    for item in (piece_one, piece_two):
        item = item.astype(jnp.float32)
        squares = squares + jnp.sum(item * item, 0, keepdims=True)
    squares = squares + jnp.sum(word_squares.reshape(-1, 1, strip), 0) / place.grp
    late = jnp.concatenate([small_own, jnp.broadcast_to(squares, (8, strip))])
    late, one_x = tie(late, one_x)
    late = gather_stage(place, late, place.z_masks, place.z)
    two_x = [piece_two] + [place.send(piece_two, mask) for mask in place.x_masks[1:]]
    late, two_x = tie(late, two_x)
    middle = [a + b for a in place.y_masks for b in place.x_masks]
    late = gather_stage(place, late, middle, place.y * place.xs + place.x)
    late = gather_stage(place, late, place.core_masks, place.core)
    late, one_x, two_x = tie(late, one_x, two_x)
    pieces_one = [item for value in one_x for item in (value, place.send(value, 1))]
    pieces_two = [item for value in two_x for item in (value, place.send(value, 1))]
    late = late.reshape((2, 2, place.xs, place.far) + late.shape[3:])
    late = jnp.transpose(late, (3, 1, 2, 0, 4, 5)).reshape(place.count, -1, strip)
    small_total = late[:, :small_piece].reshape(-1, strip)[: small_flat.shape[0]]
    small_total = small_total.reshape(small_grad.shape)
    grad_norm = jnp.sqrt(jnp.sum(late[:, small_piece]))
    factor = (clip_bound / jnp.maximum(grad_norm, clip_bound)).reshape(1)
    word_results = adam_rows(factor, word_rows, word_master, word_moments, rate_table[0])
    masters = (down_master, up_master, out_master, qkv_master, small_rows)
    moments = (down_moments, up_moments, out_moments, qkv_moments, small_moments)
    rates = tuple(rate_table[i] for i in (4, 3, 2, 1, 5))
    if all(item.shape[0] % (16 * place.xs) == 0 for item in masters[:4]):
        results = adam_matrices(
            place.g, factor, pieces_one, pieces_two, small_total, masters, moments, rates
        )
    else:
        ordered = [
            jnp.concatenate(pair)
            for pair in zip(in_order(pieces_one, place.g), in_order(pieces_two, place.g))
        ]
        ordered = jnp.stack(ordered).reshape((place.xs, 2) + ordered[0].shape)
        grads, at = [], 0
        for master in masters[:4]:
            rows, columns = master.shape[0] // place.xs, master.shape[1]
            length = rows * (columns // 2 // strip)
            part = ordered[:, :, at : at + length]
            grads.append(whole_rows(place, part, rows, columns).astype(jnp.float32))
            at += length
        grads.append(small_total)
        results = []
        for grad, moment, master, rate in zip(grads, moments, masters, rates):
            results.extend(adam_update(grad * factor[0], moment, master, rate))
    down, up, out, qkv, small = (results[3 * n : 3 * n + 3] for n in range(5))
    results = [*word_results, *qkv, *out, *up, *down, *small]
    return (loss_total, pair_count, grad_norm, *results)


def solution(mesh):
    in_specs = (
        P(both, None, None),
        P(both, None),
        P(both),
        P(both, None),
        P("grp", None),
        P(),
        P(),
        P(),
        P(),
        P("blk", None),
        P("blk", None),
        P("blk", None),
        P("blk", None),
        P("blk", None),
        P(None, "blk", None),
        P(None, "blk", None),
        P(None, "blk", None),
        P(None, "blk", None),
        P(None, "blk", None),
        P(),
        P(),
    )
    out_specs = (P(), P(), P()) + (P("blk", None),) * 15 + (P(), P(), P())
    return jax.shard_map(
        on_device, mesh=mesh, in_specs=in_specs, out_specs=out_specs, check_vma=False
    )
```

```python
import functools

import jax
import jax.numpy as jnp
from jax import lax
from jax.experimental import pallas as pl
from jax.experimental.pallas import tpu as pltpu
from jax.sharding import PartitionSpec as P

HEADS = 12
STEP = 5


logit_divisor_constant = 0.01
clip_bound = 0.001
beta_first = 0.5
beta_second = 0.5
decay_weight = 0.01
epsilon = 1e-08
rate_table = (0.1, 0.02, 0.1, 0.02, 0.01, 0.2)
finest_arithmetic = lax.Precision.HIGHEST
both = ("blk", "grp")
strip = 384


def contract_rows(left, right):
    return lax.dot_general(
        left, right, (((0,), (0,)), ((), ())), preferred_element_type=jnp.float32
    )


def contract_cols(left, right):
    return lax.dot_general(
        left, right, (((1,), (1,)), ((), ())), preferred_element_type=jnp.float32
    )


def adam_update(grad, moments, master, rate):
    first = beta_first * moments[0] + (1.0 - beta_first) * grad
    second = beta_second * moments[1] + (1.0 - beta_second) * grad * grad
    first_hat = first / (1.0 - beta_first**STEP)
    second_hat = second / (1.0 - beta_second**STEP)
    updated = master - rate * (first_hat / (jnp.sqrt(second_hat) + epsilon) + decay_weight * master)
    return (first, second, updated)


def masked_softmax(pairwise_affinity_matrix, allowed):
    masked = jnp.where(allowed, pairwise_affinity_matrix, -1000000000.0)
    top = jnp.max(masked, -1, keepdims=True)
    expo = jnp.where(allowed, jnp.exp(masked - top), 0.0)
    total = jnp.sum(expo, -1, keepdims=True)
    return (top[:, 0] + jnp.log(total[:, 0]), expo / total)


VMEM_ALLOWED = 56 * 1024 * 1024
low = jnp.bfloat16


def whole_block(shape):
    return pl.BlockSpec(shape, lambda *_: (0,) * len(shape), pipeline_mode=pl.Buffered(1))


def rows_block(rows, columns):
    return pl.BlockSpec((rows, columns), lambda i, *_: (i, 0))


def normalize(states):
    mean = jnp.mean(states, -1, keepdims=True)
    centered = states - mean
    inverse = lax.rsqrt(jnp.mean(centered * centered, -1, keepdims=True) + 1e-06)
    return centered * inverse, inverse


def normalize_back(grad, gain, unit_states, inverse):
    unit_states = unit_states.astype(jnp.float32)
    scaled = grad * gain
    inner = jnp.mean(scaled * unit_states, -1, keepdims=True)
    back = inverse * (scaled - jnp.mean(scaled, -1, keepdims=True) - unit_states * inner)
    return back, jnp.sum(grad * unit_states, 0, keepdims=True), jnp.sum(grad, 0, keepdims=True)


def gelu_and_slope(values):
    size = jnp.abs(values) * 0.7071067811865476
    t = 1.0 / (1.0 + 0.3275911 * size)
    series = t * (
        0.254829592
        + t * (-0.284496736 + t * (1.421413741 + t * (-1.453152027 + t * 1.061405429)))
    )
    bell = jnp.exp(-size * size)
    tail = 0.5 * series * bell
    below = jnp.where(values >= 0.0, 1.0 - tail, tail)
    return values * below, below + values * (0.3989422804014327 * bell)


def dot_rows(left, right):
    return lax.dot_general(
        left, right, (((0,), (0,)), ((), ())), preferred_element_type=jnp.float32
    )


def dot_cols(left, right):
    return lax.dot_general(
        left, right, (((1,), (1,)), ((), ())), preferred_element_type=jnp.float32
    )


def dot_plain(left, right):
    return jnp.dot(left, right, preferred_element_type=jnp.float32)


def head_masks(lanes, head_dim):
    even = (lax.broadcasted_iota(jnp.int32, (1, lanes), 1) < head_dim).astype(low)
    return even, (1.0 - even.astype(jnp.float32)).astype(low)


def forward_kernel(
    lengths_ref,
    slots_ref,
    found_ref,
    small_ref,
    qkv_ref,
    out_ref,
    up_ref,
    down_ref,
    unit1_ref,
    inverse1_ref,
    normed_ref,
    projected_ref,
    probs_ref,
    attended_ref,
    unit2_ref,
    inverse2_ref,
    middle_ref,
    activated_ref,
    slope_ref,
    unit3_ref,
    inverse3_ref,
    pooled_ref,
    embed_ref,
    *,
    seq_len,
    seqs,
    head_dim,
):
    step = pl.program_id(0)
    width = found_ref.shape[1]
    rows = seqs * seq_len
    slots = found_ref.shape[0]

    def vector(index):
        return small_ref[seq_len + index : seq_len + index + 1, :]

    pick = slots_ref[...] == lax.broadcasted_iota(jnp.int32, (rows, slots), 1)
    pick = jnp.where(pick, 1.0, 0.0).astype(low)
    embedded = dot_plain(pick, found_ref[...])
    positions = small_ref[:seq_len, :]
    embedded = embedded + jnp.concatenate([positions] * seqs, 0)
    unit1, inverse1 = normalize(embedded)
    unit1_ref[...] = unit1.astype(low)
    inverse1_ref[...] = inverse1
    normed = unit1 * vector(0) + vector(1)
    normed_low = normed.astype(low)
    normed_ref[...] = normed_low
    zeros = jnp.zeros((1, width), jnp.float32)
    for part, bias in enumerate((vector(2), zeros, vector(3))):
        at = slice(part * width, (part + 1) * width)
        projected_ref[:, at] = (dot_plain(normed_low, qkv_ref[:, at]) + bias).astype(low)
    lanes = 2 * head_dim
    even, odd = head_masks(lanes, head_dim)
    key_at = lax.broadcasted_iota(jnp.int32, (2 * seq_len, seq_len), 1)
    for s in range(seqs):
        at = slice(s * seq_len, (s + 1) * seq_len)
        live = key_at < lengths_ref[step * seqs + s]
        for p in range(width // lanes):
            query = projected_ref[at, p * lanes : (p + 1) * lanes]
            keys = projected_ref[at, width + p * lanes : width + (p + 1) * lanes]
            values = projected_ref[at, 2 * width + p * lanes : 2 * width + (p + 1) * lanes]
            query = jnp.concatenate([query * even, query * odd], 0)
            logits = dot_cols(query, keys) * head_dim ** (-0.5)
            logits = jnp.where(live, logits, -1000000000.0)
            expo = jnp.exp(logits - jnp.max(logits, -1, keepdims=True))
            probs = (expo / jnp.sum(expo, -1, keepdims=True)).astype(low)
            probs_ref[s, p] = probs
            both_probs = jnp.concatenate([probs[:seq_len], probs[seq_len:]], 1)
            both_values = jnp.concatenate([values * even, values * odd], 0)
            attended_ref[at, p * lanes : (p + 1) * lanes] = dot_plain(
                both_probs, both_values
            ).astype(low)
    branch = dot_plain(attended_ref[...], out_ref[...]) + vector(4)
    unit2, inverse2 = normalize(normed + branch)
    unit2_ref[...] = unit2.astype(low)
    inverse2_ref[...] = inverse2
    middle = unit2 * vector(5) + vector(6)
    middle_low = middle.astype(low)
    middle_ref[...] = middle_low
    lowered = middle + vector(7)
    for j in range(up_ref.shape[1] // width):
        at = slice(j * width, (j + 1) * width)
        lifted = dot_plain(middle_low, up_ref[:, at]) + vector(10 + j)
        activated, slope = gelu_and_slope(lifted)
        activated = activated.astype(low)
        activated_ref[:, at] = activated
        slope_ref[:, at] = slope.astype(low)
        lowered = lowered + dot_plain(activated, down_ref[at, :])
    unit3, inverse3 = normalize(lowered)
    unit3_ref[...] = unit3.astype(low)
    inverse3_ref[...] = inverse3
    final = unit3 * vector(8) + vector(9)
    row_at = lax.broadcasted_iota(jnp.int32, (seq_len, 1), 0)
    pooled = []
    for s in range(seqs):
        length = lengths_ref[step * seqs + s]
        weights = (row_at < length).astype(jnp.float32)
        total = jnp.sum(final[s * seq_len : (s + 1) * seq_len] * weights, 0, keepdims=True)
        pooled.append(total / length.astype(jnp.float32))
    pooled = jnp.concatenate(pooled, 0)
    pooled_ref[0] = pooled
    squares = jnp.sum(pooled * pooled, -1, keepdims=True)
    embed_ref[0] = (pooled * lax.rsqrt(squares + 1e-06)).astype(low)


def forward(lengths_flat, slot, found, small_rows, weights, seq_len, head_dim):
    tokens, width = slot.shape[0], found.shape[1]
    seqs = 2
    rows = seqs * seq_len
    steps = tokens // rows
    lifted = weights[2].shape[1]
    f32 = jnp.float32
    outs = [
        ((tokens, width), low),
        ((tokens, 1), f32),
        ((tokens, width), low),
        ((tokens, 3 * width), low),
        ((steps * seqs, width // (2 * head_dim), 2 * seq_len, seq_len), low),
        ((tokens, width), low),
        ((tokens, width), low),
        ((tokens, 1), f32),
        ((tokens, width), low),
        ((tokens, lifted), low),
        ((tokens, lifted), low),
        ((tokens, width), low),
        ((tokens, 1), f32),
        ((steps, seqs, width), f32),
        ((steps, seqs, width), low),
    ]

    def spec(shape):
        if shape[0] == tokens:
            return rows_block(rows, shape[1])
        block = (shape[0] // steps,) + shape[1:]
        return pl.BlockSpec(block, lambda i, *_: (i,) + (0,) * (len(shape) - 1))

    return pl.pallas_call(
        functools.partial(forward_kernel, seq_len=seq_len, seqs=seqs, head_dim=head_dim),
        out_shape=[jax.ShapeDtypeStruct(*item) for item in outs],
        grid_spec=pltpu.PrefetchScalarGridSpec(
            num_scalar_prefetch=1,
            grid=(steps,),
            in_specs=[rows_block(rows, 1), whole_block(found.shape), whole_block(small_rows.shape)]
            + [whole_block(item.shape) for item in weights],
            out_specs=[spec(item[0]) for item in outs],
        ),
        compiler_params=pltpu.CompilerParams(vmem_limit_bytes=VMEM_ALLOWED),
        cost_estimate=pl.CostEstimate(
            flops=20 * 10**9, bytes_accessed=50 * 10**6, transcendentals=10**7
        ),
        name="encoder_forward",
    )(lengths_flat, slot, found, small_rows, *weights)


def feed_back_kernel(
    lengths_ref,
    embed_grad_ref,
    pooled_ref,
    small_ref,
    unit3_ref,
    inverse3_ref,
    slope_ref,
    unit2_ref,
    inverse2_ref,
    up_ref,
    down_ref,
    lowered_ref,
    lifted_ref,
    second_ref,
    branch_ref,
    sums_ref,
    *,
    seq_len,
    seqs,
):
    step = pl.program_id(0)
    width = unit3_ref.shape[1]

    @pl.when(step == 0)
    def _():
        sums_ref[...] = jnp.zeros_like(sums_ref)

    def vector(index):
        return small_ref[seq_len + index : seq_len + index + 1, :]

    pooled, grad = pooled_ref[0], embed_grad_ref[0]
    inverse = lax.rsqrt(jnp.sum(pooled * pooled, -1, keepdims=True) + 1e-06)
    inner = jnp.sum(pooled * grad, -1, keepdims=True)
    pooled_grad = inverse * (grad - pooled * (inverse * inverse * inner))
    row_at = lax.broadcasted_iota(jnp.int32, (seq_len, 1), 0)
    final_grad = []
    for s in range(seqs):
        length = lengths_ref[step * seqs + s]
        weights = (row_at < length).astype(jnp.float32)
        final_grad.append(weights * (pooled_grad[s : s + 1] / length.astype(jnp.float32)))
    final_grad = jnp.concatenate(final_grad, 0)
    third, gain3, shift3 = normalize_back(
        final_grad, vector(8), unit3_ref[...], inverse3_ref[...]
    )
    lowered_grad = third.astype(low)
    lowered_ref[...] = lowered_grad
    middle_grad = third
    up_sums = []
    for j in range(up_ref.shape[1] // width):
        at = slice(j * width, (j + 1) * width)
        grad = dot_cols(lowered_grad, down_ref[at, :]) * slope_ref[:, at].astype(jnp.float32)
        grad = grad.astype(low)
        lifted_ref[:, at] = grad
        up_sums.append(jnp.sum(grad.astype(jnp.float32), 0, keepdims=True))
        middle_grad = middle_grad + dot_cols(grad, up_ref[:, at])
    second, gain2, shift2 = normalize_back(
        middle_grad, vector(5), unit2_ref[...], inverse2_ref[...]
    )
    second_ref[...] = second
    branch = second.astype(low)
    branch_ref[...] = branch
    branch_sum = jnp.sum(branch.astype(jnp.float32), 0, keepdims=True)
    lowered_sum = jnp.sum(lowered_grad.astype(jnp.float32), 0, keepdims=True)
    sums = [branch_sum, gain2, shift2, lowered_sum, gain3, shift3] + up_sums
    sums_ref[: len(sums), :] += jnp.concatenate(sums, 0)


def feed_back(lengths_flat, embed_grad, kept, small_rows, weights, seq_len):
    unit2, inverse2, slope, unit3, inverse3, pooled = kept
    tokens, width = unit2.shape
    lifted = slope.shape[1]
    seqs = 2
    rows = seqs * seq_len
    steps = tokens // rows
    pair = pl.BlockSpec((1, seqs, width), lambda i, *_: (i, 0, 0))
    return pl.pallas_call(
        functools.partial(feed_back_kernel, seq_len=seq_len, seqs=seqs),
        out_shape=[
            jax.ShapeDtypeStruct((tokens, width), low),
            jax.ShapeDtypeStruct((tokens, lifted), low),
            jax.ShapeDtypeStruct((tokens, width), jnp.float32),
            jax.ShapeDtypeStruct((tokens, width), low),
            jax.ShapeDtypeStruct((16, width), jnp.float32),
        ],
        grid_spec=pltpu.PrefetchScalarGridSpec(
            num_scalar_prefetch=1,
            grid=(steps,),
            in_specs=[
                pair,
                pair,
                whole_block(small_rows.shape),
                rows_block(rows, width),
                rows_block(rows, 1),
                rows_block(rows, lifted),
                rows_block(rows, width),
                rows_block(rows, 1),
                whole_block(weights[0].shape),
                whole_block(weights[1].shape),
            ],
            out_specs=[
                rows_block(rows, width),
                rows_block(rows, lifted),
                rows_block(rows, width),
                rows_block(rows, width),
                pl.BlockSpec((16, width), lambda i, *_: (0, 0)),
            ],
        ),
        compiler_params=pltpu.CompilerParams(vmem_limit_bytes=VMEM_ALLOWED),
        cost_estimate=pl.CostEstimate(
            flops=10 * 10**9, bytes_accessed=40 * 10**6, transcendentals=0
        ),
        name="feed_back",
    )(
        lengths_flat,
        embed_grad,
        pooled,
        small_rows,
        unit3,
        inverse3,
        slope,
        unit2,
        inverse2,
        *weights,
    )


def attention_back_kernel(
    slots_ref,
    second_ref,
    projected_ref,
    probs_ref,
    unit1_ref,
    inverse1_ref,
    small_ref,
    qkv_ref,
    out_ref,
    projected_grad_ref,
    mine_ref,
    theirs_ref,
    positions_ref,
    sums_ref,
    tokens_ref,
    *,
    seq_len,
    seqs,
    head_dim,
):
    step = pl.program_id(0)
    width = second_ref.shape[1]
    rows = seqs * seq_len
    lanes = 2 * head_dim
    scale = head_dim ** (-0.5)

    @pl.when(step == 0)
    def _():
        sums_ref[...] = jnp.zeros_like(sums_ref)
        positions_ref[...] = jnp.zeros_like(positions_ref)

    second = second_ref[...]
    attended_grad = dot_cols(second.astype(low), out_ref[...]).astype(low)
    even, odd = head_masks(lanes, head_dim)
    for s in range(seqs):
        at = slice(s * seq_len, (s + 1) * seq_len)
        for p in range(width // lanes):
            here = slice(p * lanes, (p + 1) * lanes)
            there = slice(width + p * lanes, width + (p + 1) * lanes)
            yonder = slice(2 * width + p * lanes, 2 * width + (p + 1) * lanes)
            query = projected_ref[at, here]
            keys = projected_ref[at, there]
            values = projected_ref[at, yonder]
            grad = attended_grad[at, here]
            grad = jnp.concatenate([grad * even, grad * odd], 0)
            query = jnp.concatenate([query * even, query * odd], 0)
            keys = jnp.concatenate([keys * even, keys * odd], 0)
            probs_low = probs_ref[s, p]
            probs = probs_low.astype(jnp.float32)
            probs_grad = dot_cols(grad, values)
            weighted = probs * probs_grad
            inner = jnp.sum(weighted, -1, keepdims=True)
            logits_grad = ((weighted - probs * inner) * scale).astype(low)
            both_grads = jnp.concatenate([logits_grad[:seq_len], logits_grad[seq_len:]], 1)
            projected_grad_ref[at, here] = dot_plain(both_grads, keys).astype(low)
            projected_grad_ref[at, there] = dot_rows(logits_grad, query).astype(low)
            projected_grad_ref[at, yonder] = dot_rows(probs_low, grad).astype(low)
    projected_grad = projected_grad_ref[...]
    query_sum = jnp.sum(projected_grad[:, :width].astype(jnp.float32), 0, keepdims=True)
    value_sum = jnp.sum(projected_grad[:, 2 * width :].astype(jnp.float32), 0, keepdims=True)
    normed_grad = second + dot_cols(projected_grad, qkv_ref[...])
    gain = small_ref[seq_len : seq_len + 1, :]
    embedded_grad, gain1, shift1 = normalize_back(
        normed_grad, gain, unit1_ref[...], inverse1_ref[...]
    )
    for s in range(seqs):
        positions_ref[...] += embedded_grad[s * seq_len : (s + 1) * seq_len]
    sums_ref[:4, :] += jnp.concatenate([gain1, shift1, query_sum, value_sum], 0)
    tokens_ref[pl.ds(step * rows, rows), :] = embedded_grad.astype(low)

    @pl.when(step == pl.num_programs(0) - 1)
    def _():
        half, tokens = mine_ref.shape[0], tokens_ref.shape[0]
        block = next(size for size in (256, 128, 64, 32, 16) if half % size == 0)
        for out_ref, base in ((mine_ref, 0), (theirs_ref, half)):
            for n in range(half // block):
                slot_at = lax.broadcasted_iota(jnp.int32, (block, tokens), 0)
                hit = slots_ref[...] == slot_at + (base + n * block)
                hit = jnp.where(hit, 1.0, 0.0).astype(low)
                out_ref[n * block : (n + 1) * block, :] = dot_plain(hit, tokens_ref[...]).astype(
                    out_ref.dtype
                )


def attention_back(slot, second, kept, small_rows, weights, seq_len, head_dim, slots):
    projected, probs, unit1, inverse1 = kept
    tokens, width = second.shape
    seqs = 2
    rows = seqs * seq_len
    steps = tokens // rows
    probs_block = (seqs,) + probs.shape[1:]

    def fixed(shape):
        return pl.BlockSpec(shape, lambda i, *_: (0, 0))

    return pl.pallas_call(
        functools.partial(
            attention_back_kernel, seq_len=seq_len, seqs=seqs, head_dim=head_dim
        ),
        out_shape=[
            jax.ShapeDtypeStruct((tokens, 3 * width), low),
            jax.ShapeDtypeStruct((slots // 2, width), jnp.float32),
            jax.ShapeDtypeStruct((slots // 2, width), low),
            jax.ShapeDtypeStruct((seq_len, width), jnp.float32),
            jax.ShapeDtypeStruct((8, width), jnp.float32),
        ],
        grid=(steps,),
        in_specs=[
            whole_block((1, tokens)),
            rows_block(rows, width),
            rows_block(rows, 3 * width),
            pl.BlockSpec(probs_block, lambda i: (i, 0, 0, 0)),
            rows_block(rows, width),
            rows_block(rows, 1),
            whole_block(small_rows.shape),
            whole_block(weights[0].shape),
            whole_block(weights[1].shape),
        ],
        out_specs=[
            rows_block(rows, 3 * width),
            fixed((slots // 2, width)),
            fixed((slots // 2, width)),
            fixed((seq_len, width)),
            fixed((8, width)),
        ],
        scratch_shapes=[pltpu.VMEM((tokens, width), low)],
        compiler_params=pltpu.CompilerParams(vmem_limit_bytes=VMEM_ALLOWED),
        cost_estimate=pl.CostEstimate(
            flops=10 * 10**9, bytes_accessed=30 * 10**6, transcendentals=0
        ),
        name="attention_back",
    )(slot.reshape(1, tokens), second, projected, probs, unit1, inverse1, small_rows, *weights)


def weight_grad_kernel(core_ref, *refs, jobs, xs):
    theirs_ref, mine_ref, turned_ref = refs[-3:]
    step = pl.program_id(0)
    start, base = 0, 0
    for n, (tiles, tall, piece, strips) in enumerate(jobs):
        left_ref, right_ref = refs[2 * n], refs[2 * n + 1]

        def work(start=start, base=base, left_ref=left_ref, right_ref=right_ref, job=jobs[n]):
            tiles, tall, piece, strips = job
            tile = step - start
            if tall or tiles == 1:
                grad = dot_rows(left_ref[...], right_ref[...])
            else:

                @pl.when(tile == 0)
                def _():
                    turned_ref[...] = left_ref[...].T

                grad = dot_plain(turned_ref[...], right_ref[...])
            count = grad.shape[0] // piece // xs
            for j in range(2):
                part = grad[:, j * strip : (j + 1) * strip]
                part = part.reshape(count, xs, piece, strip)
                if tall:
                    half = j
                    at = (pl.ds(tile * count, count), slice(None), pl.ds(base, piece))
                else:
                    number = 2 * tile + j
                    half = number // strips
                    row = pl.multiple_of(base + (number % strips) * piece, 16)
                    at = (slice(None), slice(None), pl.ds(row, piece))

                @pl.when(core_ref[0] == half)
                def _(at=at, part=part):
                    mine_ref[at] = part.astype(low)

                @pl.when(core_ref[0] != half)
                def _(at=at, part=part):
                    theirs_ref[at] = part.astype(low)

        pl.when((step >= start) & (step < start + tiles))(work)
        start += tiles
        base += piece * strips


def weight_grads(place, pairs):
    tile_rows = 2 * strip
    jobs, in_specs, operands = [], [], []
    start, rows = 0, 0
    tokens = pairs[0][0].shape[0]
    for left, right in pairs:
        strips = right.shape[1] // 2 // strip
        tall = left.shape[1] > tile_rows
        tiles = left.shape[1] // tile_rows if tall else strips
        piece = left.shape[1] // place.blk // place.xs

        def tile_of(i, start=start, tiles=tiles):
            return jnp.clip(i - start, 0, tiles - 1)

        def block(varies, f=tile_of):
            if varies:
                return pl.BlockSpec((tokens, tile_rows), lambda i, h: (0, f(i)))
            return whole_block((tokens, tile_rows))

        in_specs += [block(tall), block(not tall and tiles > 1)]
        jobs.append((tiles, tall, piece, strips))
        operands += [left, right]
        start += tiles
        rows += piece * strips
    shape = (place.blk, place.xs, rows, strip)
    return pl.pallas_call(
        functools.partial(weight_grad_kernel, jobs=jobs, xs=place.xs),
        out_shape=[
            jax.ShapeDtypeStruct(shape, low),
            jax.ShapeDtypeStruct(shape, low),
        ],
        grid_spec=pltpu.PrefetchScalarGridSpec(
            num_scalar_prefetch=1,
            grid=(start,),
            in_specs=in_specs,
            out_specs=[whole_block(shape), whole_block(shape)],
            scratch_shapes=[pltpu.VMEM((tile_rows, tokens), low)],
        ),
        compiler_params=pltpu.CompilerParams(vmem_limit_bytes=VMEM_ALLOWED),
        cost_estimate=pl.CostEstimate(flops=1000, bytes_accessed=1000, transcendentals=0),
        name="weight_grads",
    )(place.core.reshape(1).astype(jnp.int32), *operands)


def word_sum_kernel(
    place_ref, count_ref, id_ref, *refs, sources, chunks, room, span, own, finishing
):
    inputs, rest = refs[:sources], refs[sources:]
    if finishing:
        base_ref, out_ref, squares_ref, total_ref, rows_ref, chunk_ref = rest[:6]
        in_sems, out_sem, base_total_ref, base_sem, low_ref = rest[6:]
        base_copy = pltpu.make_async_copy(base_ref, base_total_ref, base_sem)
        base_copy.start()
    else:
        out_ref, total_ref, rows_ref, chunk_ref, in_sems, out_sem = rest
    batch = 8
    copies = [
        pltpu.make_async_copy(inputs[k], rows_ref.at[k], in_sems.at[k]) for k in range(sources)
    ]
    for copy in copies:
        copy.start()
    zeros = jnp.zeros((batch, total_ref.shape[1]), jnp.float32)

    def clear(i, _):
        total_ref[pl.ds(pl.multiple_of(i * batch, batch), batch), :] = zeros
        return 0

    lax.fori_loop(0, total_ref.shape[0] // batch, clear, 0, unroll=4)
    for copy in copies:
        copy.wait()

    def one_source(m, _):
        me = place_ref[0]
        place = m // chunks
        if sources == 2:
            x = (me // 2) ^ (own // 2)
            source = x * 2 + place
        else:
            x = place // 2
            x = x + jnp.where(x >= me // 2, 1, 0)
            source = x * 2 + place % 2
        slot = (source ^ me) - own
        n = source * chunks + m % chunks
        start = (m % chunks) * room
        count = count_ref[n]

        def widen(i, _):
            at = pl.ds(pl.multiple_of(start + i * 16, 16), 16)
            to = pl.ds(pl.multiple_of(i * 16, 16), 16)
            chunk_ref[to, :] = rows_ref[slot, at, :].astype(jnp.float32)
            return 0

        lax.fori_loop(0, (count + 15) // 16, widen, 0)

        def add(i, _):
            at = [id_ref[n * room + i * batch + j] for j in range(batch)]
            sums = [
                total_ref[pl.ds(at[j], 1), :] + chunk_ref[pl.ds(i * batch + j, 1), :]
                for j in range(batch)
            ]
            for j in range(batch):
                total_ref[pl.ds(at[j], 1), :] = sums[j]
            return 0

        lax.fori_loop(0, (count + batch - 1) // batch, add, 0)
        return 0

    lax.fori_loop(0, sources * chunks, one_source, 0)
    shard_rows = out_ref.shape[0]
    if not finishing:
        copy = pltpu.make_async_copy(total_ref.at[pl.ds(0, shard_rows)], out_ref, out_sem)
        copy.start()
        copy.wait()
        return
    base_copy.wait()

    def finish(i, squares):
        at = pl.ds(pl.multiple_of(i * span, span), span)
        part = total_ref[at, :] + base_total_ref[at, :]
        low_ref[at, :] = part.astype(low)
        pltpu.make_async_copy(low_ref.at[at], out_ref.at[at], out_sem).start()
        part = part * part
        return squares + jnp.sum(part.reshape(span // 8, 8, part.shape[1]), 0)

    squares = lax.fori_loop(
        0, shard_rows // span, finish, jnp.zeros((8, total_ref.shape[1]), jnp.float32)
    )
    squares_ref[...] = jnp.sum(squares, 0, keepdims=True)
    pltpu.make_async_copy(low_ref, out_ref, out_sem).wait()


def word_sum(grp_index, counts, ids, sources, shard_rows, chunks, room, base=None):
    count, width = len(sources), sources[0].shape[1]
    span = next(size for size in (128, 64, 32, 16, 8) if shard_rows % size == 0)
    anywhere = pl.BlockSpec(memory_space=pl.ANY)
    finishing = base is not None
    out_shape = [jax.ShapeDtypeStruct((shard_rows, width), low if finishing else jnp.float32)]
    out_specs = [anywhere]
    scratch = [
        pltpu.VMEM((shard_rows + 32, width), jnp.float32),
        pltpu.VMEM((count,) + sources[0].shape, low),
        pltpu.VMEM((room, width), jnp.float32),
        pltpu.SemaphoreType.DMA((count,)),
        pltpu.SemaphoreType.DMA,
    ]
    operands = list(sources)
    if finishing:
        out_shape.append(jax.ShapeDtypeStruct((1, width), jnp.float32))
        out_specs.append(whole_block((1, width)))
        scratch += [pltpu.VMEM((shard_rows, width), jnp.float32), pltpu.SemaphoreType.DMA]
        scratch.append(pltpu.VMEM((shard_rows, width), low))
        operands.append(base)
    results = pl.pallas_call(
        functools.partial(
            word_sum_kernel,
            sources=count,
            chunks=chunks,
            room=room,
            span=span,
            own=2 if finishing else 0,
            finishing=finishing,
        ),
        out_shape=out_shape,
        grid_spec=pltpu.PrefetchScalarGridSpec(
            num_scalar_prefetch=3,
            grid=(1,),
            in_specs=[anywhere] * len(operands),
            out_specs=out_specs,
            scratch_shapes=scratch,
        ),
        compiler_params=pltpu.CompilerParams(vmem_limit_bytes=VMEM_ALLOWED),
        cost_estimate=pl.CostEstimate(flops=1000, bytes_accessed=1000, transcendentals=0),
        name="word_sum",
    )(grp_index.reshape(1), counts, ids, *operands)
    return results if finishing else results[0]


def adam_kernel(factor_ref, grad_ref, master_ref, moments_ref, first_ref, second_ref, new_ref, *, rate):
    results = adam_update(
        grad_ref[...].astype(jnp.float32) * factor_ref[0],
        (moments_ref[0], moments_ref[1]),
        master_ref[...],
        rate,
    )
    first_ref[...], second_ref[...], new_ref[...] = results


def adam_rows(factor, grad, master, moments, rate):
    rows, width = master.shape
    span = next(size for size in (384, 320, 240, 192, 128, 96, 64, 32, 16, 8) if rows % size == 0)
    block = rows_block(span, width)
    return pl.pallas_call(
        functools.partial(adam_kernel, rate=rate),
        out_shape=[jax.ShapeDtypeStruct((rows, width), jnp.float32)] * 3,
        grid=(rows // span,),
        in_specs=[
            pl.BlockSpec(memory_space=pltpu.SMEM),
            block,
            block,
            pl.BlockSpec((2, span, width), lambda i: (0, i, 0)),
        ],
        out_specs=[block] * 3,
        compiler_params=pltpu.CompilerParams(vmem_limit_bytes=VMEM_ALLOWED),
        cost_estimate=pl.CostEstimate(
            flops=20 * rows * width, bytes_accessed=28 * rows * width, transcendentals=0
        ),
        name="adam_rows",
    )(factor, grad, master, moments)


def adam_all_kernel(place_ref, factor_ref, *refs, grp, shapes, rates, moment_at, groups):
    count = len(shapes)
    grad_ref, master_ref, moments_ref, refs = refs[0], refs[1], refs[2], refs[3:]
    inputs, refs = refs[: 2 * grp + 1 + 2 * count], refs[2 * grp + 1 + 2 * count :]
    outs, refs = refs[:3], refs[3:]
    far_outs, refs = refs[: 3 * count], refs[3 * count :]
    held, refs = refs[: len(inputs)], refs[len(inputs) :]
    results, refs = refs[: 3 * count], refs[3 * count :]
    totals, (in_sems, out_sems) = refs[: count - 1], refs[count - 1 :]
    step = pl.program_id(0)
    last = pl.num_programs(0) - 1
    copies_in = [
        pltpu.make_async_copy(inputs[n], held[n], in_sems.at[n]) for n in range(len(inputs))
    ]
    copies_out = [
        pltpu.make_async_copy(results[n], far_outs[n], out_sems.at[n]) for n in range(3 * count)
    ]

    @pl.when(step == 0)
    def _():
        for copy in copies_in:
            copy.start()

    factor = factor_ref[0]
    outs[0][...], outs[1][...], outs[2][...] = adam_update(
        grad_ref[...].astype(jnp.float32) * factor,
        (moments_ref[0], moments_ref[1]),
        master_ref[...],
        rates[0],
    )
    bases = []
    for n, (rows, width) in enumerate(shapes[:-1]):
        strips = width // 2 // strip
        starts_group = n == 0 or groups[n] != groups[n - 1]
        base = 0 if starts_group else bases[-1][1]
        bases.append((base, base + strips * (rows // (grp // 2))))

    for n, (rows, width) in enumerate(shapes):

        @pl.when(step == moment_at[n])
        def _(n=n, rows=rows, width=width):
            needed = [2 * grp + 1 + n, 2 * grp + 1 + count + n]
            if n == count - 1:
                needed.append(2 * grp)
            elif n == 0 or groups[n] != groups[n - 1]:
                needed += [groups[n] * grp + k for k in range(grp)]
            for m in needed:
                copies_in[m].wait()
            if n == count - 1:
                grad = held[2 * grp][...]
            else:
                strips = width // 2 // strip
                piece = rows // (grp // 2)
                for k in range(grp):
                    source = place_ref[0] ^ k
                    x, core = source // 2, source % 2
                    for s in range(strips):
                        at = bases[n][0] + s * piece
                        part = held[groups[n] * grp + k][at : at + piece, :]
                        to_row = pl.multiple_of(x * piece, 16)
                        to_column = pl.multiple_of((core * strips + s) * strip, 128)
                        totals[n][pl.ds(to_row, piece), pl.ds(to_column, strip)] = part.astype(
                            jnp.float32
                        )
                grad = totals[n][...]
            moments = held[2 * grp + 1 + count + n]
            updates = adam_update(
                grad * factor,
                (moments[0], moments[1]),
                held[2 * grp + 1 + n][...],
                rates[n + 1],
            )
            for m in range(3):
                results[3 * n + m][...] = updates[m]
                copies_out[3 * n + m].start()

    @pl.when(step == last)
    def _():
        for copy in copies_out:
            copy.wait()


def adam_all(
    grp_index, factor, word, pieces_one, pieces_two, small, masters, moments, rates, groups
):
    grad, word_master, word_moments = word
    word_rows, width = word_master.shape
    span = next(size for size in (384, 320, 240, 192, 128, 64, 32, 16) if word_rows % size == 0)
    steps = word_rows // span
    shapes = [item.shape for item in masters]
    count = len(shapes)
    moment_at = [min(steps - 1, max(1, (n + 1) * steps // (count + 2))) for n in range(count)]
    inputs = [*pieces_one, *pieces_two, small, *masters, *moments]
    far_shapes = [s for s in shapes for _ in range(3)]
    block = rows_block(span, width)
    return pl.pallas_call(
        functools.partial(
            adam_all_kernel,
            grp=len(pieces_one),
            shapes=shapes,
            rates=rates,
            moment_at=moment_at,
            groups=groups,
        ),
        out_shape=[jax.ShapeDtypeStruct((word_rows, width), jnp.float32)] * 3
        + [jax.ShapeDtypeStruct(s, jnp.float32) for s in far_shapes],
        grid_spec=pltpu.PrefetchScalarGridSpec(
            num_scalar_prefetch=1,
            grid=(steps,),
            in_specs=[
                pl.BlockSpec(memory_space=pltpu.SMEM),
                block,
                block,
                pl.BlockSpec((2, span, width), lambda i, *_: (0, i, 0)),
            ]
            + [pl.BlockSpec(memory_space=pl.ANY)] * len(inputs),
            out_specs=[block] * 3 + [pl.BlockSpec(memory_space=pl.ANY)] * len(far_shapes),
            scratch_shapes=[pltpu.VMEM(item.shape, item.dtype) for item in inputs]
            + [pltpu.VMEM(s, jnp.float32) for s in far_shapes]
            + [pltpu.VMEM(s, jnp.float32) for s in shapes[:-1]]
            + [
                pltpu.SemaphoreType.DMA((len(inputs),)),
                pltpu.SemaphoreType.DMA((len(far_shapes),)),
            ],
        ),
        compiler_params=pltpu.CompilerParams(vmem_limit_bytes=VMEM_ALLOWED),
        cost_estimate=pl.CostEstimate(
            flops=20 * word_rows * width, bytes_accessed=28 * word_rows * width, transcendentals=0
        ),
        name="adam_all",
    )(grp_index.reshape(1), factor, grad, word_master, word_moments, *inputs)


class Place:
    def __init__(self):
        self.blk, self.grp = lax.axis_size("blk"), lax.axis_size("grp")
        self.count = self.blk * self.grp
        self.b, self.g = lax.axis_index("blk"), lax.axis_index("grp")
        self.xs, self.far = self.grp // 2, self.blk // 2
        self.core, self.x = self.g % 2, self.g // 2
        self.y, self.z = self.b % 2, self.b // 2
        self.core_masks = [0, 1]
        self.x_masks = [2 * i for i in range(self.xs)]
        self.y_masks = [0, self.grp]
        self.z_masks = [2 * self.grp * i for i in range(self.far)]

    def send_split(self, value, far_mask):
        masks = [2 * self.grp * far_mask + self.grp * core for core in range(2)]
        return lax.ppermute(value, both, [(i, i ^ masks[i % 2]) for i in range(self.count)])

    def send(self, value, mask):
        pairs = [(i, i ^ mask) for i in range(self.count)]
        return lax.ppermute(value, both, pairs)


def in_order(pieces, index):
    step = 1
    while step < len(pieces):
        odd = (index & step) != 0
        pieces = [jnp.where(odd, pieces[i ^ step], pieces[i]) for i in range(len(pieces))]
        step *= 2
    return pieces


def gather_stage(place, value, masks, index):
    pieces = [value] + [place.send(value, mask) for mask in masks[1:]]
    return jnp.stack(in_order(pieces, index))


def gather_far_first(place, value):
    shape = value.shape
    value = gather_stage(place, value, place.z_masks, place.z)
    middle = [a + b for a in place.y_masks for b in place.x_masks]
    value = gather_stage(place, value, middle, place.y * place.xs + place.x)
    value = gather_stage(place, value, place.core_masks, place.core)
    value = value.reshape((2, 2, place.xs, place.far) + shape)
    return jnp.transpose(value, (3, 1, 2, 0) + tuple(range(4, 4 + len(shape)))).reshape(
        (place.blk, place.grp) + shape
    )


def two_terms(value):
    high = lax.reduce_precision(value, 8, 7)
    return jnp.concatenate([high, value - high], -2).astype(low)


def one_term(value):
    value = value.astype(jnp.float32)
    rows = value.shape[-2] // 2
    return value[..., :rows, :] + value[..., rows:, :]


def add_up(terms):
    while len(terms) > 1:
        terms = [terms[i] + terms[i + 1] for i in range(0, len(terms), 2)]
    return terms[0]


class Reduction:
    def __init__(self, place, value, x_first, small=None):
        self.place = place
        self.value, self.small = self.shaped(value), self.shaped(small)
        x_stage = (place.x_masks, place.x)
        y_stage = (place.y_masks, place.y)
        if x_first:
            self.stages = [(*x_stage, 2), (*y_stage, 1)]
        else:
            self.stages = [(*y_stage, 1), (*x_stage, 1)]
        self.stages.append((place.z_masks, place.z, 0))

    def shaped(self, value):
        if value is None:
            return None
        place = self.place
        return value.reshape((place.far, 2, place.xs) + value.shape[2:])

    def prepare(self):
        self.masks, index, axis = self.stages.pop(0)

        def part_of(value, at):
            return lax.dynamic_index_in_dim(jnp.moveaxis(value, axis, 0), at, 0, keepdims=False)

        self.keep = part_of(self.value, index)
        self.parts = []
        for k in range(1, len(self.masks)):
            part = part_of(self.value, index ^ k).astype(low)
            if self.small is not None:
                small = part_of(self.small, index ^ k)
                part = jnp.concatenate([part, two_terms(small)], -2)
            self.parts.append(part)
        self.keep, self.parts = tie(self.keep, self.parts)
        if self.small is not None:
            self.small = part_of(self.small, index)

    def send(self):
        self.arrived = [
            self.place.send(part, mask) for part, mask in zip(self.parts, self.masks[1:])
        ]

    def add(self):
        rows = self.keep.shape[-2]
        arrived = [item[..., :rows, :].astype(jnp.float32) for item in self.arrived]
        self.value = add_up([self.keep] + arrived)
        if self.small is not None:
            tails = [one_term(item[..., rows:, :]) for item in self.arrived]
            self.small = add_up([self.small] + tails)


def tie(*items):
    return lax.optimization_barrier(items)


def half_gradient(place, left, right, core):
    width = right.shape[1] // 2
    part = lax.dynamic_slice_in_dim(right, core * width, width, 1)
    grad = contract_rows(left, part).astype(jnp.bfloat16)
    rows = grad.shape[0] // place.blk // place.xs
    strips = width // strip
    grad = grad.reshape(place.blk, place.xs, rows, strips, strip)
    return jnp.transpose(grad, (0, 1, 3, 2, 4)).reshape(
        place.blk, place.xs, strips * rows, strip
    )


def group_products(place, pairs):
    if all(a.shape[1] % (16 * place.blk * place.xs) == 0 for a, _ in pairs):
        return weight_grads(place, pairs)
    mine = [half_gradient(place, a, b, place.core) for a, b in pairs]
    theirs = [half_gradient(place, a, b, 1 - place.core) for a, b in pairs]
    return jnp.concatenate(theirs, 2), jnp.concatenate(mine, 2)


def merge_ids(left, right, length):
    hits = []
    for own, other in ((left, right), (right, left)):
        repeated = jnp.any(other[..., :, None] == own[..., None, :], -1)
        lower = (
            (other >= 0)[..., None, :]
            & ~repeated[..., None, :]
            & (other[..., None, :] < own[..., :, None])
        )
        rank = jnp.arange(own.shape[-1]) + jnp.sum(lower.astype(jnp.int32), -1)
        hit = rank[..., None, :] == jnp.arange(length)[:, None]
        hits.append(jnp.max(jnp.where(hit, own[..., None, :], -1), -1))
    return jnp.maximum(*hits)


def whole_rows(place, pieces, rows, width):
    strips = width // 2 // strip
    pieces = pieces.reshape(place.xs, 2, strips, rows, strip)
    return jnp.transpose(pieces, (0, 3, 1, 2, 4)).reshape(place.xs * rows, width)


def on_device(
    token_ids,
    lengths,
    valid,
    false_neg,
    word_table,
    qkv_weight,
    out_weight,
    up_weight,
    down_weight,
    word_master,
    qkv_master,
    out_master,
    up_master,
    down_master,
    word_moments,
    qkv_moments,
    out_moments,
    up_moments,
    down_moments,
    small_rows,
    small_moments,
):
    place = Place()
    pairs_here = token_ids.shape[0]
    total_pairs = pairs_here * place.count
    seq_count = 2 * pairs_here
    seq_len = token_ids.shape[2]
    width = word_table.shape[1]
    head_dim = width // HEADS
    flat_ids = token_ids.reshape(-1)
    tokens = flat_ids.shape[0]
    lengths_flat = lengths.reshape(-1)

    shard_rows = word_master.shape[0]
    table_rows = word_table.shape[0]
    per_owner = table_rows // shard_rows
    room = max(16, tokens * 7 // 8 // place.blk)
    shard = flat_ids // shard_rows
    same_id = flat_ids[:, None] == flat_ids[None, :]
    before = jnp.arange(tokens)[:, None] < jnp.arange(tokens)[None, :]
    first = ~jnp.any(same_id & before, 0)
    smaller = (
        (shard[:, None] == shard[None, :])
        & (flat_ids[None, :] < flat_ids[:, None])
        & first[None, :]
    )
    rank = jnp.sum(smaller.astype(jnp.int32), 1)
    slots = place.blk * room

    owner = shard // per_owner
    relative = ((owner ^ place.g) * per_owner + shard % per_owner) * room + rank
    lookup_slots = jnp.where(rank < room, relative, slots)

    def fetch(grp_ids):
        span = per_owner * room
        asked = [lax.dynamic_slice_in_dim(ids, place.g * span, span) for ids in grp_ids]
        local = jnp.concatenate(asked) - place.g * table_rows
        found = word_table.at[jnp.clip(local, 0, table_rows - 1)].get(mode="clip")
        found, sibling = tie(found, grp_ids[1])
        parts = [found[k * span : (k + 1) * span] for k in range(place.grp)]
        rows = [parts[0]] + [place.send(parts[k], k) for k in range(1, place.grp)]
        rows.append(jnp.zeros((tokens - slots, width), low))
        return rows, sibling

    def pack(values, length):
        return jnp.concatenate([values, jnp.zeros((length - values.shape[0],), values.dtype)])

    slot = jnp.where(rank < room, shard * room + rank, slots)
    hit = slot[None, :] == jnp.arange(slots)[:, None]
    slot_ids = jnp.max(jnp.where(hit, flat_ids[None, :], -1), 1)
    early = jnp.concatenate(
        [
            slot_ids,
            false_neg.reshape(-1),
            valid,
            (jnp.max(rank) >= room).astype(jnp.int32)[None],
        ]
    )
    early = pack(early, -(-early.shape[0] // 1024) * 1024).reshape(-1, 128)
    grp_early = [early] + [place.send(early, k) for k in range(1, place.grp)]
    looked_up, sibling = fetch([item.reshape(-1)[:slots] for item in grp_early])
    early_all = jnp.stack(in_order(grp_early, place.g))
    early_all = gather_stage(place, early_all, place.y_masks, place.y)
    early_all, looked_up[1] = tie(early_all, looked_up[1])
    early_all = gather_stage(place, early_all, place.z_masks, place.z)
    early_all = early_all.reshape(place.count, -1)
    ids_all = early_all[:, :slots].reshape(place.blk, place.xs, 2, place.blk, room)
    at = slots
    false_neg_all = early_all[:, at : at + pairs_here * total_pairs].reshape(
        total_pairs, total_pairs
    )
    at += pairs_here * total_pairs
    valid_all = early_all[:, at : at + pairs_here].reshape(-1)
    at += pairs_here
    crowded = jnp.max(early_all[:, at]) > 0

    chip_room = max(16, tokens * 3 // 2 // place.blk // 16 * 16)
    chip_slots = place.blk * chip_room
    known = jnp.any(sibling[:, None] == flat_ids[None, :], 1)
    extra = (
        (sibling[None, :] >= 0)
        & ~known[None, :]
        & (sibling[None, :] // shard_rows == shard[:, None])
        & (sibling[None, :] < flat_ids[:, None])
    )
    chip_rank = rank + jnp.sum(extra.astype(jnp.int32), 1)
    shard_y, shard_z = shard % 2, shard // 2
    order = jnp.where(shard_y ^ place.y == place.core, 0, place.far) + (shard_z ^ place.z)
    gradient_slot = jnp.where(
        chip_rank < chip_room, order * chip_room + chip_rank, chip_slots
    )
    weights = (qkv_weight, out_weight, up_weight, down_weight)

    def encode(slot, found):
        return forward(
            lengths_flat, slot[:, None], found, small_rows, weights, seq_len, head_dim
        )

    ids = lax.dynamic_index_in_dim(ids_all, place.b, 3, keepdims=False)
    ids = merge_ids(ids[:, :, 0], ids[:, :, 1], chip_room)
    ids = ids.reshape(place.far, 2, place.xs, chip_room)
    ids = jnp.stack(in_order([ids[i] for i in range(place.far)], place.z))
    ids = jnp.stack(in_order([ids[:, 0], ids[:, 1]], place.y), 1)
    ids = jnp.transpose(ids, (2, 1, 0, 3))
    local = ids - place.b * shard_rows
    inside = ids >= 0
    counts = jnp.sum(inside.astype(jnp.int32), -1).reshape(-1)
    local = jnp.where(inside, local, shard_rows).reshape(-1)
    counts, local, looked_up[2:] = tie(counts, local, looked_up[2:])
    looked_up = jnp.concatenate(looked_up)

    def look_up_all():
        whole = lax.all_gather(word_table, "grp", axis=0, tiled=True)
        return jnp.arange(tokens, dtype=jnp.int32), whole[flat_ids]

    slot, found = lax.cond(
        crowded, look_up_all, lambda: (lookup_slots.astype(jnp.int32), looked_up)
    )
    (
        unit1,
        inverse1,
        normed_low,
        projected,
        probs,
        attended,
        unit2,
        inverse2,
        middle_low,
        activated_low,
        slope,
        unit3,
        inverse3,
        pooled,
        own_embed,
    ) = encode(slot, found)

    chip_crowded = (jnp.max(rank) >= room) | (jnp.max(chip_rank) >= chip_room)
    embed_rows = jnp.concatenate(
        [own_embed.reshape(-1, width), jnp.full((8, width), chip_crowded, low)]
    )
    gathered = gather_far_first(place, embed_rows).reshape(place.count, -1, width)
    rows_crowded = jnp.max(gathered[:, -1, 0].astype(jnp.float32)) > 0.5
    gathered = gathered[:, : 2 * pairs_here].reshape(total_pairs, 2, width)
    queries, documents = gathered[:, 0], gathered[:, 1]
    diagonal = jnp.arange(total_pairs)[:, None] == jnp.arange(total_pairs)[None, :]
    allowed = (valid_all[None, :] > 0) & ((false_neg_all == 0) | diagonal)
    scores = contract_cols(queries, documents) / logit_divisor_constant
    query_lse, query_probs = masked_softmax(scores, allowed)
    doc_lse, doc_probs = masked_softmax(scores.T, allowed)
    diag = jnp.sum(jnp.where(diagonal, scores, 0.0), -1)
    valid_floats = valid_all.astype(jnp.float32)
    pair_count = jnp.maximum(jnp.sum(valid_floats), 1.0)
    loss_total = jnp.sum(valid_floats * (query_lse + doc_lse - 2.0 * diag)) / 2.0
    row_weight = valid_floats / (2.0 * pair_count)
    identity_mask = diagonal.astype(jnp.float32)
    score_grad = (
        row_weight[:, None] * (query_probs - identity_mask)
        + (row_weight[:, None] * (doc_probs - identity_mask)).T
    )
    row_start = (place.b * place.grp + place.g) * pairs_here
    query_grad_rows = lax.dynamic_slice_in_dim(score_grad, row_start, pairs_here, 0)
    doc_grad_rows = lax.dynamic_slice_in_dim(score_grad, row_start, pairs_here, 1).T
    embed_grad = (
        jnp.stack(
            [
                jnp.dot(
                    query_grad_rows, documents.astype(jnp.float32), precision=finest_arithmetic
                ),
                jnp.dot(doc_grad_rows, queries.astype(jnp.float32), precision=finest_arithmetic),
            ],
            1,
        )
        / logit_divisor_constant
    )

    lowered_grad, lifted_low, second, branch_grad, feed_sums = feed_back(
        lengths_flat,
        embed_grad,
        (unit2, inverse2, slope, unit3, inverse3, pooled),
        small_rows,
        (up_weight, down_weight),
        seq_len,
    )
    theirs_down, mine_down = group_products(place, [(activated_low, lowered_grad)])
    lifted_low, theirs_down, mine_down = tie(lifted_low, theirs_down, mine_down)
    core_down = place.send(theirs_down, 1)
    theirs_up, mine_up = group_products(
        place, [(middle_low, lifted_low), (attended, branch_grad)]
    )
    down = Reduction(place, mine_down.astype(jnp.float32) + core_down.astype(jnp.float32), True)
    down.prepare()
    core_up = place.send(theirs_up, 1)
    up = Reduction(place, mine_up.astype(jnp.float32) + core_up.astype(jnp.float32), False)
    up.prepare()
    second, up.parts, down.parts = tie(second, up.parts, down.parts)
    up.send()
    down.send()
    projected_grad, mine_rows, theirs_rows, position_grad, attention_sums = attention_back(
        gradient_slot,
        second,
        (projected, probs, unit1, inverse1),
        small_rows,
        (qkv_weight, out_weight),
        seq_len,
        head_dim,
        chip_slots,
    )

    theirs_rows, position_grad, down.arrived, up.arrived = tie(
        theirs_rows, position_grad, down.arrived, up.arrived
    )
    small_grad = jnp.concatenate([position_grad, attention_sums[:4], feed_sums[:10]], 0)
    small_flat = small_grad.reshape(-1, strip)
    small_piece = -(-small_flat.shape[0] // (16 * place.count)) * 16
    small_padded = jnp.concatenate(
        [
            small_flat,
            jnp.zeros((small_piece * place.count - small_flat.shape[0], strip), jnp.float32),
        ]
    )
    small_parts = small_padded.reshape(place.blk, place.xs, 2, small_piece, strip)
    small_mine = lax.dynamic_index_in_dim(small_parts, place.core, 2, keepdims=False)
    small_theirs = lax.dynamic_index_in_dim(small_parts, 1 - place.core, 2, keepdims=False)
    rows = mine_rows + place.send(theirs_rows, 1).astype(jnp.float32)
    small_value = small_mine + one_term(place.send(two_terms(small_theirs), 1))
    rows = rows.astype(low).reshape(place.far, chip_room, width)
    down.add()
    down.prepare()
    up.add()
    up.prepare()
    first_rows = jnp.concatenate([rows[0, :, :strip], rows[0, :, strip:]])
    rows, first_rows, small_value, projected_grad, down.parts, up.parts = tie(
        rows, first_rows, small_value, projected_grad, down.parts, up.parts
    )
    arrived = [place.send_split(rows[k], k) for k in range(1, place.far)]
    up.send()
    down_shape = down.parts[0].shape
    down_y = place.send(
        jnp.concatenate([down.parts[0].reshape(-1, strip), first_rows]), place.grp
    )
    theirs_two, mine_two = group_products(place, [(normed_low, projected_grad)])
    arrived, up.arrived, down_y, theirs_two, mine_two = tie(
        arrived, up.arrived, down_y, theirs_two, mine_two
    )
    cut = down_y.shape[0] - first_rows.shape[0]
    down.arrived = [down_y[:cut].reshape(down_shape)]
    other_y = jnp.concatenate([down_y[cut : cut + chip_room], down_y[cut + chip_room :]], 1)
    arrived = jnp.concatenate([jnp.where(place.core == 0, rows[0], other_y)] + arrived)
    over_x = [arrived] + [place.send(arrived, mask) for mask in place.x_masks[1:]]
    core_two = place.send(theirs_two, 1)
    near = [arrived, place.send(arrived, 1)]
    two = Reduction(
        place, mine_two.astype(jnp.float32) + core_two.astype(jnp.float32), False, small_value
    )
    two.prepare()
    down.add()
    up.add()
    one = Reduction(place, jnp.zeros((place.blk, place.xs, 16, strip), low), False)
    one.stages = one.stages[-1:]
    one.value = jnp.concatenate([down.value, up.value], 1)
    one.prepare()
    near, two.parts, one.parts = tie(near, two.parts, one.parts)
    two.send()
    one.send()
    own_total = word_sum(
        place.g, counts, local, near, shard_rows, place.far, chip_room
    )
    own_total, two.arrived, over_x = tie(own_total, two.arrived, over_x)
    others = [item for value in over_x[1:] for item in (value, place.send(value, 1))]
    two.add()
    two.prepare()
    others, two.parts = tie(others, two.parts)
    two.send()

    def few_rows():
        return word_sum(
            place.g, counts, local, others, shard_rows, place.far, chip_room, own_total
        )

    def all_rows():
        token_halves = attention_back(
            jnp.arange(tokens, dtype=jnp.int32),
            second,
            (projected, probs, unit1, inverse1),
            small_rows,
            (qkv_weight, out_weight),
            seq_len,
            head_dim,
            tokens,
        )[1:3]
        token_grads = jnp.concatenate([token_halves[0].astype(low), token_halves[1]])
        every_id = lax.all_gather(flat_ids, "blk", axis=0, tiled=True) - place.b * shard_rows
        every_row = lax.all_gather(token_grads, "blk", axis=0, tiled=True)
        inside = (every_id >= 0) & (every_id < shard_rows)
        total = (
            jnp.zeros((shard_rows, width), jnp.float32)
            .at[jnp.where(inside, every_id, shard_rows)]
            .add(every_row.astype(jnp.float32), mode="drop")
        )
        total = lax.psum(total, "grp")
        return total.astype(low), jnp.sum(total * total, 0, keepdims=True)

    word_rows, word_squares = lax.cond(rows_crowded, all_rows, few_rows)
    word_rows, word_squares, two.arrived, one.arrived = tie(
        word_rows, word_squares, two.arrived, one.arrived
    )
    two.add()
    two.prepare()
    two.send()
    one.add()
    two.add()
    piece_one = one.value.astype(low)
    one_x = [piece_one] + [place.send(piece_one, mask) for mask in place.x_masks[1:]]
    piece_two, small_own = two.value.astype(low), two.small
    squares = jnp.sum(small_own * small_own, 0, keepdims=True)
    for item in (piece_one, piece_two):
        item = item.astype(jnp.float32)
        squares = squares + jnp.sum(item * item, 0, keepdims=True)
    squares = squares + jnp.sum(word_squares.reshape(-1, 1, strip), 0) / place.grp
    late = jnp.concatenate([small_own, jnp.broadcast_to(squares, (8, strip))])
    late, one_x = tie(late, one_x)
    late = gather_stage(place, late, place.z_masks, place.z)
    two_x = [piece_two] + [place.send(piece_two, mask) for mask in place.x_masks[1:]]
    late, two_x = tie(late, two_x)
    middle = [a + b for a in place.y_masks for b in place.x_masks]
    late = gather_stage(place, late, middle, place.y * place.xs + place.x)
    late = gather_stage(place, late, place.core_masks, place.core)
    late, one_x, two_x = tie(late, one_x, two_x)
    pieces_one = [item for value in one_x for item in (value, place.send(value, 1))]
    pieces_two = [item for value in two_x for item in (value, place.send(value, 1))]
    late = late.reshape((2, 2, place.xs, place.far) + late.shape[3:])
    late = jnp.transpose(late, (3, 1, 2, 0, 4, 5)).reshape(place.count, -1, strip)
    small_total = late[:, :small_piece].reshape(-1, strip)[: small_flat.shape[0]]
    small_total = small_total.reshape(small_grad.shape)
    grad_norm = jnp.sqrt(jnp.sum(late[:, small_piece]))
    factor = (clip_bound / jnp.maximum(grad_norm, clip_bound)).reshape(1)
    masters = (down_master, up_master, out_master, qkv_master, small_rows)
    moments = (down_moments, up_moments, out_moments, qkv_moments, small_moments)
    rates = tuple(rate_table[i] for i in (4, 3, 2, 1, 5))
    if all(item.shape[0] % (16 * place.xs) == 0 for item in masters[:4]):
        results = adam_all(
            place.g,
            factor,
            (word_rows, word_master, word_moments),
            pieces_one,
            pieces_two,
            small_total,
            masters,
            moments,
            (rate_table[0], *rates),
            (0, 0, 0, 1),
        )
    else:
        ordered = [
            jnp.concatenate(pair)
            for pair in zip(in_order(pieces_one, place.g), in_order(pieces_two, place.g))
        ]
        ordered = jnp.stack(ordered).reshape((place.xs, 2) + ordered[0].shape)
        grads, at = [], 0
        for master in masters[:4]:
            rows, columns = master.shape[0] // place.xs, master.shape[1]
            length = rows * (columns // 2 // strip)
            part = ordered[:, :, at : at + length]
            grads.append(whole_rows(place, part, rows, columns).astype(jnp.float32))
            at += length
        grads.append(small_total)
        results = list(
            adam_rows(factor, word_rows, word_master, word_moments, rate_table[0])
        )
        for grad, moment, master, rate in zip(grads, moments, masters, rates):
            results.extend(adam_update(grad * factor[0], moment, master, rate))
    word, down, up, out, qkv, small = (results[3 * n : 3 * n + 3] for n in range(6))
    results = [*word, *qkv, *out, *up, *down, *small]
    return (loss_total, pair_count, grad_norm, *results)


def solution(mesh):
    in_specs = (
        P(both, None, None),
        P(both, None),
        P(both),
        P(both, None),
        P("grp", None),
        P(),
        P(),
        P(),
        P(),
        P("blk", None),
        P("blk", None),
        P("blk", None),
        P("blk", None),
        P("blk", None),
        P(None, "blk", None),
        P(None, "blk", None),
        P(None, "blk", None),
        P(None, "blk", None),
        P(None, "blk", None),
        P(),
        P(),
    )
    out_specs = (P(), P(), P()) + (P("blk", None),) * 15 + (P(), P(), P())
    return jax.shard_map(
        on_device, mesh=mesh, in_specs=in_specs, out_specs=out_specs, check_vma=False
    )
```

```python
import functools

import jax
import jax.numpy as jnp
from jax import lax
from jax.experimental import pallas as pl
from jax.experimental.pallas import tpu as pltpu
from jax.sharding import PartitionSpec as P

HEADS = 12
STEP = 5


logit_divisor_constant = 0.01
clip_bound = 0.001
beta_first = 0.5
beta_second = 0.5
decay_weight = 0.01
epsilon = 1e-08
rate_table = (0.1, 0.02, 0.1, 0.02, 0.01, 0.2)
finest_arithmetic = lax.Precision.HIGHEST
both = ("blk", "grp")
strip = 384


def contract_rows(left, right):
    return lax.dot_general(
        left, right, (((0,), (0,)), ((), ())), preferred_element_type=jnp.float32
    )


def contract_cols(left, right):
    return lax.dot_general(
        left, right, (((1,), (1,)), ((), ())), preferred_element_type=jnp.float32
    )


def adam_update(grad, moments, master, rate):
    first = beta_first * moments[0] + (1.0 - beta_first) * grad
    second = beta_second * moments[1] + (1.0 - beta_second) * grad * grad
    first_hat = first * (1.0 / (1.0 - beta_first**STEP))
    second_hat = second * (1.0 / (1.0 - beta_second**STEP))
    updated = master - rate * (first_hat / (jnp.sqrt(second_hat) + epsilon) + decay_weight * master)
    return (first, second, updated)


def masked_softmax(pairwise_affinity_matrix, allowed):
    masked = jnp.where(allowed, pairwise_affinity_matrix, -1000000000.0)
    top = jnp.max(masked, -1, keepdims=True)
    expo = jnp.where(allowed, jnp.exp(masked - top), 0.0)
    total = jnp.sum(expo, -1, keepdims=True)
    return (top[:, 0] + jnp.log(total[:, 0]), expo / total)


VMEM_ALLOWED = 56 * 1024 * 1024
low = jnp.bfloat16


def whole_block(shape):
    return pl.BlockSpec(shape, lambda *_: (0,) * len(shape), pipeline_mode=pl.Buffered(1))


def rows_block(rows, columns):
    return pl.BlockSpec((rows, columns), lambda i, *_: (i, 0))


def normalize(states):
    mean = jnp.mean(states, -1, keepdims=True)
    centered = states - mean
    inverse = lax.rsqrt(jnp.mean(centered * centered, -1, keepdims=True) + 1e-06)
    return centered * inverse, inverse


def normalize_back(grad, gain, unit_states, inverse):
    unit_states = unit_states.astype(jnp.float32)
    scaled = grad * gain
    inner = jnp.mean(scaled * unit_states, -1, keepdims=True)
    back = inverse * (scaled - jnp.mean(scaled, -1, keepdims=True) - unit_states * inner)
    return back, jnp.sum(grad * unit_states, 0, keepdims=True), jnp.sum(grad, 0, keepdims=True)


def gelu_and_slope(values):
    size = jnp.abs(values) * 0.7071067811865476
    t = 1.0 / (1.0 + 0.3275911 * size)
    series = t * (
        0.254829592
        + t * (-0.284496736 + t * (1.421413741 + t * (-1.453152027 + t * 1.061405429)))
    )
    bell = jnp.exp(-size * size)
    tail = 0.5 * series * bell
    below = jnp.where(values >= 0.0, 1.0 - tail, tail)
    return values * below, below + values * (0.3989422804014327 * bell)


def dot_rows(left, right):
    return lax.dot_general(
        left, right, (((0,), (0,)), ((), ())), preferred_element_type=jnp.float32
    )


def dot_cols(left, right):
    return lax.dot_general(
        left, right, (((1,), (1,)), ((), ())), preferred_element_type=jnp.float32
    )


def dot_plain(left, right):
    return jnp.dot(left, right, preferred_element_type=jnp.float32)


def head_masks(lanes, head_dim):
    even = (lax.broadcasted_iota(jnp.int32, (1, lanes), 1) < head_dim).astype(low)
    return even, (1.0 - even.astype(jnp.float32)).astype(low)


def forward_kernel(
    lengths_ref,
    slots_ref,
    found_ref,
    small_ref,
    qkv_ref,
    out_ref,
    up_ref,
    down_ref,
    unit1_ref,
    inverse1_ref,
    normed_ref,
    projected_ref,
    probs_ref,
    attended_ref,
    unit2_ref,
    inverse2_ref,
    middle_ref,
    activated_ref,
    slope_ref,
    unit3_ref,
    inverse3_ref,
    pooled_ref,
    embed_ref,
    *,
    seq_len,
    seqs,
    head_dim,
):
    step = pl.program_id(0)
    width = found_ref.shape[1]
    rows = seqs * seq_len
    slots = found_ref.shape[0]

    def vector(index):
        return small_ref[seq_len + index : seq_len + index + 1, :]

    pick = slots_ref[...] == lax.broadcasted_iota(jnp.int32, (rows, slots), 1)
    pick = jnp.where(pick, 1.0, 0.0).astype(low)
    embedded = dot_plain(pick, found_ref[...])
    positions = small_ref[:seq_len, :]
    embedded = embedded + jnp.concatenate([positions] * seqs, 0)
    unit1, inverse1 = normalize(embedded)
    unit1_ref[...] = unit1.astype(low)
    inverse1_ref[...] = inverse1
    normed = unit1 * vector(0) + vector(1)
    normed_low = normed.astype(low)
    normed_ref[...] = normed_low
    zeros = jnp.zeros((1, width), jnp.float32)
    for part, bias in enumerate((vector(2), zeros, vector(3))):
        at = slice(part * width, (part + 1) * width)
        projected_ref[:, at] = (dot_plain(normed_low, qkv_ref[:, at]) + bias).astype(low)
    lanes = 2 * head_dim
    even, odd = head_masks(lanes, head_dim)
    key_at = lax.broadcasted_iota(jnp.int32, (2 * seq_len, seq_len), 1)
    for s in range(seqs):
        at = slice(s * seq_len, (s + 1) * seq_len)
        live = key_at < lengths_ref[step * seqs + s]
        for p in range(width // lanes):
            query = projected_ref[at, p * lanes : (p + 1) * lanes]
            keys = projected_ref[at, width + p * lanes : width + (p + 1) * lanes]
            values = projected_ref[at, 2 * width + p * lanes : 2 * width + (p + 1) * lanes]
            query = jnp.concatenate([query * even, query * odd], 0)
            logits = dot_cols(query, keys) * head_dim ** (-0.5)
            logits = jnp.where(live, logits, -1000000000.0)
            expo = jnp.exp(logits - jnp.max(logits, -1, keepdims=True))
            probs = (expo / jnp.sum(expo, -1, keepdims=True)).astype(low)
            probs_ref[s, p] = probs
            both_probs = jnp.concatenate([probs[:seq_len], probs[seq_len:]], 1)
            both_values = jnp.concatenate([values * even, values * odd], 0)
            attended_ref[at, p * lanes : (p + 1) * lanes] = dot_plain(
                both_probs, both_values
            ).astype(low)
    branch = dot_plain(attended_ref[...], out_ref[...]) + vector(4)
    unit2, inverse2 = normalize(normed + branch)
    unit2_ref[...] = unit2.astype(low)
    inverse2_ref[...] = inverse2
    middle = unit2 * vector(5) + vector(6)
    middle_low = middle.astype(low)
    middle_ref[...] = middle_low
    lowered = middle + vector(7)
    for j in range(up_ref.shape[1] // width):
        at = slice(j * width, (j + 1) * width)
        lifted = dot_plain(middle_low, up_ref[:, at]) + vector(10 + j)
        activated, slope = gelu_and_slope(lifted)
        activated = activated.astype(low)
        activated_ref[:, at] = activated
        slope_ref[:, at] = slope.astype(low)
        lowered = lowered + dot_plain(activated, down_ref[at, :])
    unit3, inverse3 = normalize(lowered)
    unit3_ref[...] = unit3.astype(low)
    inverse3_ref[...] = inverse3
    final = unit3 * vector(8) + vector(9)
    row_at = lax.broadcasted_iota(jnp.int32, (seq_len, 1), 0)
    pooled = []
    for s in range(seqs):
        length = lengths_ref[step * seqs + s]
        weights = (row_at < length).astype(jnp.float32)
        total = jnp.sum(final[s * seq_len : (s + 1) * seq_len] * weights, 0, keepdims=True)
        pooled.append(total / length.astype(jnp.float32))
    pooled = jnp.concatenate(pooled, 0)
    pooled_ref[0] = pooled
    squares = jnp.sum(pooled * pooled, -1, keepdims=True)
    embed_ref[0] = (pooled * lax.rsqrt(squares + 1e-06)).astype(low)


def forward(lengths_flat, slot, found, small_rows, weights, seq_len, head_dim):
    tokens, width = slot.shape[0], found.shape[1]
    seqs = 2
    rows = seqs * seq_len
    steps = tokens // rows
    lifted = weights[2].shape[1]
    f32 = jnp.float32
    outs = [
        ((tokens, width), low),
        ((tokens, 1), f32),
        ((tokens, width), low),
        ((tokens, 3 * width), low),
        ((steps * seqs, width // (2 * head_dim), 2 * seq_len, seq_len), low),
        ((tokens, width), low),
        ((tokens, width), low),
        ((tokens, 1), f32),
        ((tokens, width), low),
        ((tokens, lifted), low),
        ((tokens, lifted), low),
        ((tokens, width), low),
        ((tokens, 1), f32),
        ((steps, seqs, width), f32),
        ((steps, seqs, width), low),
    ]

    def spec(shape):
        if shape[0] == tokens:
            return rows_block(rows, shape[1])
        block = (shape[0] // steps,) + shape[1:]
        return pl.BlockSpec(block, lambda i, *_: (i,) + (0,) * (len(shape) - 1))

    return pl.pallas_call(
        functools.partial(forward_kernel, seq_len=seq_len, seqs=seqs, head_dim=head_dim),
        out_shape=[jax.ShapeDtypeStruct(*item) for item in outs],
        grid_spec=pltpu.PrefetchScalarGridSpec(
            num_scalar_prefetch=1,
            grid=(steps,),
            in_specs=[rows_block(rows, 1), whole_block(found.shape), whole_block(small_rows.shape)]
            + [whole_block(item.shape) for item in weights],
            out_specs=[spec(item[0]) for item in outs],
        ),
        compiler_params=pltpu.CompilerParams(vmem_limit_bytes=VMEM_ALLOWED),
        cost_estimate=pl.CostEstimate(
            flops=20 * 10**9, bytes_accessed=50 * 10**6, transcendentals=10**7
        ),
        name="encoder_forward",
    )(lengths_flat, slot, found, small_rows, *weights)


def feed_back_kernel(
    lengths_ref,
    embed_grad_ref,
    pooled_ref,
    small_ref,
    unit3_ref,
    inverse3_ref,
    slope_ref,
    unit2_ref,
    inverse2_ref,
    up_ref,
    down_ref,
    lowered_ref,
    lifted_ref,
    second_ref,
    branch_ref,
    sums_ref,
    *,
    seq_len,
    seqs,
):
    step = pl.program_id(0)
    width = unit3_ref.shape[1]

    @pl.when(step == 0)
    def _():
        sums_ref[...] = jnp.zeros_like(sums_ref)

    def vector(index):
        return small_ref[seq_len + index : seq_len + index + 1, :]

    pooled, grad = pooled_ref[0], embed_grad_ref[0]
    inverse = lax.rsqrt(jnp.sum(pooled * pooled, -1, keepdims=True) + 1e-06)
    inner = jnp.sum(pooled * grad, -1, keepdims=True)
    pooled_grad = inverse * (grad - pooled * (inverse * inverse * inner))
    row_at = lax.broadcasted_iota(jnp.int32, (seq_len, 1), 0)
    final_grad = []
    for s in range(seqs):
        length = lengths_ref[step * seqs + s]
        weights = (row_at < length).astype(jnp.float32)
        final_grad.append(weights * (pooled_grad[s : s + 1] / length.astype(jnp.float32)))
    final_grad = jnp.concatenate(final_grad, 0)
    third, gain3, shift3 = normalize_back(
        final_grad, vector(8), unit3_ref[...], inverse3_ref[...]
    )
    lowered_grad = third.astype(low)
    lowered_ref[...] = lowered_grad
    middle_grad = third
    up_sums = []
    for j in range(up_ref.shape[1] // width):
        at = slice(j * width, (j + 1) * width)
        grad = dot_cols(lowered_grad, down_ref[at, :]) * slope_ref[:, at].astype(jnp.float32)
        grad = grad.astype(low)
        lifted_ref[:, at] = grad
        up_sums.append(jnp.sum(grad.astype(jnp.float32), 0, keepdims=True))
        middle_grad = middle_grad + dot_cols(grad, up_ref[:, at])
    second, gain2, shift2 = normalize_back(
        middle_grad, vector(5), unit2_ref[...], inverse2_ref[...]
    )
    second_ref[...] = second
    branch = second.astype(low)
    branch_ref[...] = branch
    branch_sum = jnp.sum(branch.astype(jnp.float32), 0, keepdims=True)
    lowered_sum = jnp.sum(lowered_grad.astype(jnp.float32), 0, keepdims=True)
    sums = [branch_sum, gain2, shift2, lowered_sum, gain3, shift3] + up_sums
    sums_ref[: len(sums), :] += jnp.concatenate(sums, 0)


def feed_back(lengths_flat, embed_grad, kept, small_rows, weights, seq_len):
    unit2, inverse2, slope, unit3, inverse3, pooled = kept
    tokens, width = unit2.shape
    lifted = slope.shape[1]
    seqs = 2
    rows = seqs * seq_len
    steps = tokens // rows
    pair = pl.BlockSpec((1, seqs, width), lambda i, *_: (i, 0, 0))
    return pl.pallas_call(
        functools.partial(feed_back_kernel, seq_len=seq_len, seqs=seqs),
        out_shape=[
            jax.ShapeDtypeStruct((tokens, width), low),
            jax.ShapeDtypeStruct((tokens, lifted), low),
            jax.ShapeDtypeStruct((tokens, width), jnp.float32),
            jax.ShapeDtypeStruct((tokens, width), low),
            jax.ShapeDtypeStruct((16, width), jnp.float32),
        ],
        grid_spec=pltpu.PrefetchScalarGridSpec(
            num_scalar_prefetch=1,
            grid=(steps,),
            in_specs=[
                pair,
                pair,
                whole_block(small_rows.shape),
                rows_block(rows, width),
                rows_block(rows, 1),
                rows_block(rows, lifted),
                rows_block(rows, width),
                rows_block(rows, 1),
                whole_block(weights[0].shape),
                whole_block(weights[1].shape),
            ],
            out_specs=[
                rows_block(rows, width),
                rows_block(rows, lifted),
                rows_block(rows, width),
                rows_block(rows, width),
                pl.BlockSpec((16, width), lambda i, *_: (0, 0)),
            ],
        ),
        compiler_params=pltpu.CompilerParams(vmem_limit_bytes=VMEM_ALLOWED),
        cost_estimate=pl.CostEstimate(
            flops=10 * 10**9, bytes_accessed=40 * 10**6, transcendentals=0
        ),
        name="feed_back",
    )(
        lengths_flat,
        embed_grad,
        pooled,
        small_rows,
        unit3,
        inverse3,
        slope,
        unit2,
        inverse2,
        *weights,
    )


def attention_back_kernel(
    slots_ref,
    second_ref,
    projected_ref,
    probs_ref,
    unit1_ref,
    inverse1_ref,
    small_ref,
    qkv_ref,
    out_ref,
    projected_grad_ref,
    mine_ref,
    theirs_ref,
    positions_ref,
    sums_ref,
    tokens_ref,
    *,
    seq_len,
    seqs,
    head_dim,
):
    step = pl.program_id(0)
    width = second_ref.shape[1]
    rows = seqs * seq_len
    lanes = 2 * head_dim
    scale = head_dim ** (-0.5)

    @pl.when(step == 0)
    def _():
        sums_ref[...] = jnp.zeros_like(sums_ref)
        positions_ref[...] = jnp.zeros_like(positions_ref)

    second = second_ref[...]
    attended_grad = dot_cols(second.astype(low), out_ref[...]).astype(low)
    even, odd = head_masks(lanes, head_dim)
    for s in range(seqs):
        at = slice(s * seq_len, (s + 1) * seq_len)
        for p in range(width // lanes):
            here = slice(p * lanes, (p + 1) * lanes)
            there = slice(width + p * lanes, width + (p + 1) * lanes)
            yonder = slice(2 * width + p * lanes, 2 * width + (p + 1) * lanes)
            query = projected_ref[at, here]
            keys = projected_ref[at, there]
            values = projected_ref[at, yonder]
            grad = attended_grad[at, here]
            grad = jnp.concatenate([grad * even, grad * odd], 0)
            query = jnp.concatenate([query * even, query * odd], 0)
            keys = jnp.concatenate([keys * even, keys * odd], 0)
            probs_low = probs_ref[s, p]
            probs = probs_low.astype(jnp.float32)
            probs_grad = dot_cols(grad, values)
            weighted = probs * probs_grad
            inner = jnp.sum(weighted, -1, keepdims=True)
            logits_grad = ((weighted - probs * inner) * scale).astype(low)
            both_grads = jnp.concatenate([logits_grad[:seq_len], logits_grad[seq_len:]], 1)
            projected_grad_ref[at, here] = dot_plain(both_grads, keys).astype(low)
            projected_grad_ref[at, there] = dot_rows(logits_grad, query).astype(low)
            projected_grad_ref[at, yonder] = dot_rows(probs_low, grad).astype(low)
    projected_grad = projected_grad_ref[...]
    query_sum = jnp.sum(projected_grad[:, :width].astype(jnp.float32), 0, keepdims=True)
    value_sum = jnp.sum(projected_grad[:, 2 * width :].astype(jnp.float32), 0, keepdims=True)
    normed_grad = second + dot_cols(projected_grad, qkv_ref[...])
    gain = small_ref[seq_len : seq_len + 1, :]
    embedded_grad, gain1, shift1 = normalize_back(
        normed_grad, gain, unit1_ref[...], inverse1_ref[...]
    )
    for s in range(seqs):
        positions_ref[...] += embedded_grad[s * seq_len : (s + 1) * seq_len]
    sums_ref[:4, :] += jnp.concatenate([gain1, shift1, query_sum, value_sum], 0)
    tokens_ref[pl.ds(step * rows, rows), :] = embedded_grad.astype(low)

    @pl.when(step == pl.num_programs(0) - 1)
    def _():
        half, tokens = mine_ref.shape[0], tokens_ref.shape[0]
        block = next(size for size in (384, 256, 128, 64, 32, 16) if half % size == 0)
        for out_ref, base in ((mine_ref, 0), (theirs_ref, half)):
            for n in range(half // block):
                slot_at = lax.broadcasted_iota(jnp.int32, (block, tokens), 0)
                hit = slots_ref[...] == slot_at + (base + n * block)
                hit = jnp.where(hit, 1.0, 0.0).astype(low)
                out_ref[n * block : (n + 1) * block, :] = dot_plain(hit, tokens_ref[...]).astype(
                    out_ref.dtype
                )


def attention_back(slot, second, kept, small_rows, weights, seq_len, head_dim, slots):
    projected, probs, unit1, inverse1 = kept
    tokens, width = second.shape
    seqs = 2
    rows = seqs * seq_len
    steps = tokens // rows
    probs_block = (seqs,) + probs.shape[1:]

    def fixed(shape):
        return pl.BlockSpec(shape, lambda i, *_: (0, 0))

    return pl.pallas_call(
        functools.partial(
            attention_back_kernel, seq_len=seq_len, seqs=seqs, head_dim=head_dim
        ),
        out_shape=[
            jax.ShapeDtypeStruct((tokens, 3 * width), low),
            jax.ShapeDtypeStruct((slots // 2, width), jnp.float32),
            jax.ShapeDtypeStruct((slots // 2, width), low),
            jax.ShapeDtypeStruct((seq_len, width), jnp.float32),
            jax.ShapeDtypeStruct((8, width), jnp.float32),
        ],
        grid=(steps,),
        in_specs=[
            whole_block((1, tokens)),
            rows_block(rows, width),
            rows_block(rows, 3 * width),
            pl.BlockSpec(probs_block, lambda i: (i, 0, 0, 0)),
            rows_block(rows, width),
            rows_block(rows, 1),
            whole_block(small_rows.shape),
            whole_block(weights[0].shape),
            whole_block(weights[1].shape),
        ],
        out_specs=[
            rows_block(rows, 3 * width),
            fixed((slots // 2, width)),
            fixed((slots // 2, width)),
            fixed((seq_len, width)),
            fixed((8, width)),
        ],
        scratch_shapes=[pltpu.VMEM((tokens, width), low)],
        compiler_params=pltpu.CompilerParams(vmem_limit_bytes=VMEM_ALLOWED),
        cost_estimate=pl.CostEstimate(
            flops=10 * 10**9, bytes_accessed=30 * 10**6, transcendentals=0
        ),
        name="attention_back",
    )(slot.reshape(1, tokens), second, projected, probs, unit1, inverse1, small_rows, *weights)


def weight_grad_kernel(core_ref, *refs, jobs, xs):
    theirs_ref, mine_ref, turned_ref = refs[-3:]
    step = pl.program_id(0)
    start, base = 0, 0
    for n, (tiles, tall, piece, strips) in enumerate(jobs):
        left_ref, right_ref = refs[2 * n], refs[2 * n + 1]

        def work(start=start, base=base, left_ref=left_ref, right_ref=right_ref, job=jobs[n]):
            tiles, tall, piece, strips = job
            tile = step - start
            if tall or tiles == 1:
                grad = dot_rows(left_ref[...], right_ref[...])
            else:

                @pl.when(tile == 0)
                def _():
                    turned_ref[...] = left_ref[...].T

                grad = dot_plain(turned_ref[...], right_ref[...])
            count = grad.shape[0] // piece // xs
            for j in range(2):
                part = grad[:, j * strip : (j + 1) * strip]
                part = part.reshape(count, xs, piece, strip)
                if tall:
                    half = j
                    at = (pl.ds(tile * count, count), slice(None), pl.ds(base, piece))
                else:
                    number = 2 * tile + j
                    half = number // strips
                    row = pl.multiple_of(base + (number % strips) * piece, 16)
                    at = (slice(None), slice(None), pl.ds(row, piece))

                @pl.when(core_ref[0] == half)
                def _(at=at, part=part):
                    mine_ref[at] = part.astype(low)

                @pl.when(core_ref[0] != half)
                def _(at=at, part=part):
                    theirs_ref[at] = part.astype(low)

        pl.when((step >= start) & (step < start + tiles))(work)
        start += tiles
        base += piece * strips


def weight_grads(place, pairs):
    tile_rows = 2 * strip
    jobs, in_specs, operands = [], [], []
    start, rows = 0, 0
    tokens = pairs[0][0].shape[0]
    for left, right in pairs:
        strips = right.shape[1] // 2 // strip
        tall = left.shape[1] > tile_rows
        tiles = left.shape[1] // tile_rows if tall else strips
        piece = left.shape[1] // place.blk // place.xs

        def tile_of(i, start=start, tiles=tiles):
            return jnp.clip(i - start, 0, tiles - 1)

        def block(varies, f=tile_of):
            if varies:
                return pl.BlockSpec((tokens, tile_rows), lambda i, h: (0, f(i)))
            return whole_block((tokens, tile_rows))

        in_specs += [block(tall), block(not tall and tiles > 1)]
        jobs.append((tiles, tall, piece, strips))
        operands += [left, right]
        start += tiles
        rows += piece * strips
    shape = (place.blk, place.xs, rows, strip)
    return pl.pallas_call(
        functools.partial(weight_grad_kernel, jobs=jobs, xs=place.xs),
        out_shape=[
            jax.ShapeDtypeStruct(shape, low),
            jax.ShapeDtypeStruct(shape, low),
        ],
        grid_spec=pltpu.PrefetchScalarGridSpec(
            num_scalar_prefetch=1,
            grid=(start,),
            in_specs=in_specs,
            out_specs=[whole_block(shape), whole_block(shape)],
            scratch_shapes=[pltpu.VMEM((tile_rows, tokens), low)],
        ),
        compiler_params=pltpu.CompilerParams(vmem_limit_bytes=VMEM_ALLOWED),
        cost_estimate=pl.CostEstimate(flops=1000, bytes_accessed=1000, transcendentals=0),
        name="weight_grads",
    )(place.core.reshape(1).astype(jnp.int32), *operands)


def word_sum_kernel(
    place_ref, count_ref, id_ref, *refs, sources, chunks, room, span, own, finishing
):
    inputs, rest = refs[:sources], refs[sources:]
    if finishing:
        base_ref, out_ref, squares_ref, total_ref, rows_ref, chunk_ref = rest[:6]
        in_sems, out_sem, base_total_ref, base_sem, low_ref = rest[6:]
        base_copy = pltpu.make_async_copy(base_ref, base_total_ref, base_sem)
        base_copy.start()
    else:
        out_ref, total_ref, rows_ref, chunk_ref, in_sems, out_sem = rest
    batch = 8
    copies = [
        pltpu.make_async_copy(inputs[k], rows_ref.at[k], in_sems.at[k]) for k in range(sources)
    ]
    for copy in copies:
        copy.start()
    zeros = jnp.zeros((batch, total_ref.shape[1]), jnp.float32)

    def clear(i, _):
        total_ref[pl.ds(pl.multiple_of(i * batch, batch), batch), :] = zeros
        return 0

    lax.fori_loop(0, total_ref.shape[0] // batch, clear, 0, unroll=4)
    for copy in copies:
        copy.wait()

    def one_source(m, _):
        me = place_ref[0]
        place = m // chunks
        if sources == 2:
            x = (me // 2) ^ (own // 2)
            source = x * 2 + place
        else:
            x = place // 2
            x = x + jnp.where(x >= me // 2, 1, 0)
            source = x * 2 + place % 2
        slot = (source ^ me) - own
        n = source * chunks + m % chunks
        start = (m % chunks) * room
        count = count_ref[n]

        def widen(i, _):
            at = pl.ds(pl.multiple_of(start + i * 16, 16), 16)
            to = pl.ds(pl.multiple_of(i * 16, 16), 16)
            chunk_ref[to, :] = rows_ref[slot, at, :].astype(jnp.float32)
            return 0

        lax.fori_loop(0, (count + 15) // 16, widen, 0)

        def add(i, _):
            at = [id_ref[n * room + i * batch + j] for j in range(batch)]
            sums = [
                total_ref[pl.ds(at[j], 1), :] + chunk_ref[pl.ds(i * batch + j, 1), :]
                for j in range(batch)
            ]
            for j in range(batch):
                total_ref[pl.ds(at[j], 1), :] = sums[j]
            return 0

        lax.fori_loop(0, (count + batch - 1) // batch, add, 0)
        return 0

    lax.fori_loop(0, sources * chunks, one_source, 0)
    shard_rows = out_ref.shape[0]
    if not finishing:
        copy = pltpu.make_async_copy(total_ref.at[pl.ds(0, shard_rows)], out_ref, out_sem)
        copy.start()
        copy.wait()
        return
    base_copy.wait()

    def finish(i, squares):
        at = pl.ds(pl.multiple_of(i * span, span), span)
        part = total_ref[at, :] + base_total_ref[at, :]
        low_ref[at, :] = part.astype(low)
        pltpu.make_async_copy(low_ref.at[at], out_ref.at[at], out_sem).start()
        part = part * part
        return squares + jnp.sum(part.reshape(span // 8, 8, part.shape[1]), 0)

    squares = lax.fori_loop(
        0, shard_rows // span, finish, jnp.zeros((8, total_ref.shape[1]), jnp.float32)
    )
    squares_ref[...] = jnp.sum(squares, 0, keepdims=True)
    pltpu.make_async_copy(low_ref, out_ref, out_sem).wait()


def word_sum(grp_index, counts, ids, sources, shard_rows, chunks, room, base=None):
    count, width = len(sources), sources[0].shape[1]
    span = next(size for size in (128, 64, 32, 16, 8) if shard_rows % size == 0)
    anywhere = pl.BlockSpec(memory_space=pl.ANY)
    finishing = base is not None
    out_shape = [jax.ShapeDtypeStruct((shard_rows, width), low if finishing else jnp.float32)]
    out_specs = [anywhere]
    scratch = [
        pltpu.VMEM((shard_rows + 32, width), jnp.float32),
        pltpu.VMEM((count,) + sources[0].shape, low),
        pltpu.VMEM((room, width), jnp.float32),
        pltpu.SemaphoreType.DMA((count,)),
        pltpu.SemaphoreType.DMA,
    ]
    operands = list(sources)
    if finishing:
        out_shape.append(jax.ShapeDtypeStruct((1, width), jnp.float32))
        out_specs.append(whole_block((1, width)))
        scratch += [pltpu.VMEM((shard_rows, width), jnp.float32), pltpu.SemaphoreType.DMA]
        scratch.append(pltpu.VMEM((shard_rows, width), low))
        operands.append(base)
    results = pl.pallas_call(
        functools.partial(
            word_sum_kernel,
            sources=count,
            chunks=chunks,
            room=room,
            span=span,
            own=2 if finishing else 0,
            finishing=finishing,
        ),
        out_shape=out_shape,
        grid_spec=pltpu.PrefetchScalarGridSpec(
            num_scalar_prefetch=3,
            grid=(1,),
            in_specs=[anywhere] * len(operands),
            out_specs=out_specs,
            scratch_shapes=scratch,
        ),
        compiler_params=pltpu.CompilerParams(vmem_limit_bytes=VMEM_ALLOWED),
        cost_estimate=pl.CostEstimate(flops=1000, bytes_accessed=1000, transcendentals=0),
        name="word_sum",
    )(grp_index.reshape(1), counts, ids, *operands)
    return results if finishing else results[0]


def adam_kernel(factor_ref, grad_ref, master_ref, moments_ref, first_ref, second_ref, new_ref, *, rate):
    results = adam_update(
        grad_ref[...].astype(jnp.float32) * factor_ref[0],
        (moments_ref[0], moments_ref[1]),
        master_ref[...],
        rate,
    )
    first_ref[...], second_ref[...], new_ref[...] = results


def adam_rows(factor, grad, master, moments, rate):
    rows, width = master.shape
    span = next(size for size in (384, 320, 240, 192, 128, 96, 64, 32, 16, 8) if rows % size == 0)
    block = rows_block(span, width)
    return pl.pallas_call(
        functools.partial(adam_kernel, rate=rate),
        out_shape=[jax.ShapeDtypeStruct((rows, width), jnp.float32)] * 3,
        grid=(rows // span,),
        in_specs=[
            pl.BlockSpec(memory_space=pltpu.SMEM),
            block,
            block,
            pl.BlockSpec((2, span, width), lambda i: (0, i, 0)),
        ],
        out_specs=[block] * 3,
        compiler_params=pltpu.CompilerParams(vmem_limit_bytes=VMEM_ALLOWED),
        cost_estimate=pl.CostEstimate(
            flops=20 * rows * width, bytes_accessed=28 * rows * width, transcendentals=0
        ),
        name="adam_rows",
    )(factor, grad, master, moments)


def adam_all_kernel(place_ref, factor_ref, *refs, grp, shapes, rates, moment_at, groups):
    count = len(shapes)
    grad_ref, master_ref, moments_ref, refs = refs[0], refs[1], refs[2], refs[3:]
    inputs, refs = refs[: 2 * grp + 1 + 2 * count], refs[2 * grp + 1 + 2 * count :]
    outs, refs = refs[:3], refs[3:]
    far_outs, refs = refs[: 3 * count], refs[3 * count :]
    held, refs = refs[: len(inputs)], refs[len(inputs) :]
    results, refs = refs[: 3 * count], refs[3 * count :]
    totals, (in_sems, out_sems) = refs[: count - 1], refs[count - 1 :]
    step = pl.program_id(0)
    last = pl.num_programs(0) - 1
    copies_in = [
        pltpu.make_async_copy(inputs[n], held[n], in_sems.at[n]) for n in range(len(inputs))
    ]
    copies_out = [
        pltpu.make_async_copy(results[n], far_outs[n], out_sems.at[n]) for n in range(3 * count)
    ]

    @pl.when(step == 0)
    def _():
        for copy in copies_in:
            copy.start()

    factor = factor_ref[0]
    outs[0][...], outs[1][...], outs[2][...] = adam_update(
        grad_ref[...].astype(jnp.float32) * factor,
        (moments_ref[0], moments_ref[1]),
        master_ref[...],
        rates[0],
    )
    bases = []
    for n, (rows, width) in enumerate(shapes[:-1]):
        strips = width // 2 // strip
        starts_group = n == 0 or groups[n] != groups[n - 1]
        base = 0 if starts_group else bases[-1][1]
        bases.append((base, base + strips * (rows // (grp // 2))))

    for n, (rows, width) in enumerate(shapes):

        @pl.when(step == moment_at[n])
        def _(n=n, rows=rows, width=width):
            needed = [2 * grp + 1 + n, 2 * grp + 1 + count + n]
            if n == count - 1:
                needed.append(2 * grp)
            elif n == 0 or groups[n] != groups[n - 1]:
                needed += [groups[n] * grp + k for k in range(grp)]
            for m in needed:
                copies_in[m].wait()
            if n == count - 1:
                grad = held[2 * grp][...]
            else:
                strips = width // 2 // strip
                piece = rows // (grp // 2)
                for k in range(grp):
                    source = place_ref[0] ^ k
                    x, core = source // 2, source % 2
                    for s in range(strips):
                        at = bases[n][0] + s * piece
                        part = held[groups[n] * grp + k][at : at + piece, :]
                        to_row = pl.multiple_of(x * piece, 16)
                        to_column = pl.multiple_of((core * strips + s) * strip, 128)
                        totals[n][pl.ds(to_row, piece), pl.ds(to_column, strip)] = part.astype(
                            jnp.float32
                        )
                grad = totals[n][...]
            moments = held[2 * grp + 1 + count + n]
            updates = adam_update(
                grad * factor,
                (moments[0], moments[1]),
                held[2 * grp + 1 + n][...],
                rates[n + 1],
            )
            for m in range(3):
                results[3 * n + m][...] = updates[m]
                copies_out[3 * n + m].start()

    @pl.when(step == last)
    def _():
        for copy in copies_out:
            copy.wait()


def adam_all(
    grp_index, factor, word, pieces_one, pieces_two, small, masters, moments, rates, groups
):
    grad, word_master, word_moments = word
    word_rows, width = word_master.shape
    span = next(size for size in (480, 320, 240, 192, 128, 64, 32, 16) if word_rows % size == 0)
    steps = word_rows // span
    shapes = [item.shape for item in masters]
    count = len(shapes)
    moment_at = [min(steps - 1, max(1, (n + 1) * steps // (count + 2))) for n in range(count)]
    inputs = [*pieces_one, *pieces_two, small, *masters, *moments]
    far_shapes = [s for s in shapes for _ in range(3)]
    block = rows_block(span, width)
    return pl.pallas_call(
        functools.partial(
            adam_all_kernel,
            grp=len(pieces_one),
            shapes=shapes,
            rates=rates,
            moment_at=moment_at,
            groups=groups,
        ),
        out_shape=[jax.ShapeDtypeStruct((word_rows, width), jnp.float32)] * 3
        + [jax.ShapeDtypeStruct(s, jnp.float32) for s in far_shapes],
        grid_spec=pltpu.PrefetchScalarGridSpec(
            num_scalar_prefetch=1,
            grid=(steps,),
            in_specs=[
                pl.BlockSpec(memory_space=pltpu.SMEM),
                block,
                block,
                pl.BlockSpec((2, span, width), lambda i, *_: (0, i, 0)),
            ]
            + [pl.BlockSpec(memory_space=pl.ANY)] * len(inputs),
            out_specs=[block] * 3 + [pl.BlockSpec(memory_space=pl.ANY)] * len(far_shapes),
            scratch_shapes=[pltpu.VMEM(item.shape, item.dtype) for item in inputs]
            + [pltpu.VMEM(s, jnp.float32) for s in far_shapes]
            + [pltpu.VMEM(s, jnp.float32) for s in shapes[:-1]]
            + [
                pltpu.SemaphoreType.DMA((len(inputs),)),
                pltpu.SemaphoreType.DMA((len(far_shapes),)),
            ],
        ),
        compiler_params=pltpu.CompilerParams(vmem_limit_bytes=VMEM_ALLOWED),
        cost_estimate=pl.CostEstimate(
            flops=20 * word_rows * width, bytes_accessed=28 * word_rows * width, transcendentals=0
        ),
        name="adam_all",
    )(grp_index.reshape(1), factor, grad, word_master, word_moments, *inputs)


class Place:
    def __init__(self):
        self.blk, self.grp = lax.axis_size("blk"), lax.axis_size("grp")
        self.count = self.blk * self.grp
        self.b, self.g = lax.axis_index("blk"), lax.axis_index("grp")
        self.xs, self.far = self.grp // 2, self.blk // 2
        self.core, self.x = self.g % 2, self.g // 2
        self.y, self.z = self.b % 2, self.b // 2
        self.core_masks = [0, 1]
        self.x_masks = [2 * i for i in range(self.xs)]
        self.y_masks = [0, self.grp]
        self.z_masks = [2 * self.grp * i for i in range(self.far)]

    def send_split(self, value, far_mask):
        masks = [2 * self.grp * far_mask + self.grp * core for core in range(2)]
        return lax.ppermute(value, both, [(i, i ^ masks[i % 2]) for i in range(self.count)])

    def send(self, value, mask):
        pairs = [(i, i ^ mask) for i in range(self.count)]
        return lax.ppermute(value, both, pairs)


def in_order(pieces, index):
    step = 1
    while step < len(pieces):
        odd = (index & step) != 0
        pieces = [jnp.where(odd, pieces[i ^ step], pieces[i]) for i in range(len(pieces))]
        step *= 2
    return pieces


def gather_stage(place, value, masks, index):
    pieces = [value] + [place.send(value, mask) for mask in masks[1:]]
    return jnp.stack(in_order(pieces, index))


def gather_far_first(place, value):
    shape = value.shape
    value = gather_stage(place, value, place.z_masks, place.z)
    middle = [a + b for a in place.y_masks for b in place.x_masks]
    value = gather_stage(place, value, middle, place.y * place.xs + place.x)
    value = gather_stage(place, value, place.core_masks, place.core)
    value = value.reshape((2, 2, place.xs, place.far) + shape)
    return jnp.transpose(value, (3, 1, 2, 0) + tuple(range(4, 4 + len(shape)))).reshape(
        (place.blk, place.grp) + shape
    )


def two_terms(value):
    high = lax.reduce_precision(value, 8, 7)
    return jnp.concatenate([high, value - high], -2).astype(low)


def one_term(value):
    value = value.astype(jnp.float32)
    rows = value.shape[-2] // 2
    return value[..., :rows, :] + value[..., rows:, :]


def add_up(terms):
    while len(terms) > 1:
        terms = [terms[i] + terms[i + 1] for i in range(0, len(terms), 2)]
    return terms[0]


class Reduction:
    def __init__(self, place, value, x_first, small=None):
        self.place = place
        self.value, self.small = self.shaped(value), self.shaped(small)
        x_stage = (place.x_masks, place.x)
        y_stage = (place.y_masks, place.y)
        if x_first:
            self.stages = [(*x_stage, 2), (*y_stage, 1)]
        else:
            self.stages = [(*y_stage, 1), (*x_stage, 1)]
        self.stages.append((place.z_masks, place.z, 0))

    def shaped(self, value):
        if value is None:
            return None
        place = self.place
        return value.reshape((place.far, 2, place.xs) + value.shape[2:])

    def prepare(self):
        self.masks, index, axis = self.stages.pop(0)

        def part_of(value, at):
            return lax.dynamic_index_in_dim(jnp.moveaxis(value, axis, 0), at, 0, keepdims=False)

        self.keep = part_of(self.value, index)
        self.parts = []
        for k in range(1, len(self.masks)):
            part = part_of(self.value, index ^ k).astype(low)
            if self.small is not None:
                small = part_of(self.small, index ^ k)
                part = jnp.concatenate([part, two_terms(small)], -2)
            self.parts.append(part)
        self.keep, self.parts = tie(self.keep, self.parts)
        if self.small is not None:
            self.small = part_of(self.small, index)

    def send(self):
        self.arrived = [
            self.place.send(part, mask) for part, mask in zip(self.parts, self.masks[1:])
        ]

    def add(self):
        rows = self.keep.shape[-2]
        arrived = [item[..., :rows, :].astype(jnp.float32) for item in self.arrived]
        self.value = add_up([self.keep] + arrived)
        if self.small is not None:
            tails = [one_term(item[..., rows:, :]) for item in self.arrived]
            self.small = add_up([self.small] + tails)


def tie(*items):
    return lax.optimization_barrier(items)


def half_gradient(place, left, right, core):
    width = right.shape[1] // 2
    part = lax.dynamic_slice_in_dim(right, core * width, width, 1)
    grad = contract_rows(left, part).astype(jnp.bfloat16)
    rows = grad.shape[0] // place.blk // place.xs
    strips = width // strip
    grad = grad.reshape(place.blk, place.xs, rows, strips, strip)
    return jnp.transpose(grad, (0, 1, 3, 2, 4)).reshape(
        place.blk, place.xs, strips * rows, strip
    )


def group_products(place, pairs):
    if all(a.shape[1] % (16 * place.blk * place.xs) == 0 for a, _ in pairs):
        return weight_grads(place, pairs)
    mine = [half_gradient(place, a, b, place.core) for a, b in pairs]
    theirs = [half_gradient(place, a, b, 1 - place.core) for a, b in pairs]
    return jnp.concatenate(theirs, 2), jnp.concatenate(mine, 2)


def merge_ids(left, right, length):
    hits = []
    for own, other in ((left, right), (right, left)):
        repeated = jnp.any(other[..., :, None] == own[..., None, :], -1)
        lower = (
            (other >= 0)[..., None, :]
            & ~repeated[..., None, :]
            & (other[..., None, :] < own[..., :, None])
        )
        rank = jnp.arange(own.shape[-1]) + jnp.sum(lower.astype(jnp.int32), -1)
        hit = rank[..., None, :] == jnp.arange(length)[:, None]
        hits.append(jnp.max(jnp.where(hit, own[..., None, :], -1), -1))
    return jnp.maximum(*hits)


def whole_rows(place, pieces, rows, width):
    strips = width // 2 // strip
    pieces = pieces.reshape(place.xs, 2, strips, rows, strip)
    return jnp.transpose(pieces, (0, 3, 1, 2, 4)).reshape(place.xs * rows, width)


def on_device(
    token_ids,
    lengths,
    valid,
    false_neg,
    word_table,
    qkv_weight,
    out_weight,
    up_weight,
    down_weight,
    word_master,
    qkv_master,
    out_master,
    up_master,
    down_master,
    word_moments,
    qkv_moments,
    out_moments,
    up_moments,
    down_moments,
    small_rows,
    small_moments,
):
    place = Place()
    pairs_here = token_ids.shape[0]
    total_pairs = pairs_here * place.count
    seq_count = 2 * pairs_here
    seq_len = token_ids.shape[2]
    width = word_table.shape[1]
    head_dim = width // HEADS
    flat_ids = token_ids.reshape(-1)
    tokens = flat_ids.shape[0]
    lengths_flat = lengths.reshape(-1)

    shard_rows = word_master.shape[0]
    table_rows = word_table.shape[0]
    per_owner = table_rows // shard_rows
    room = max(16, tokens * 7 // 8 // place.blk)
    shard = flat_ids // shard_rows
    same_id = flat_ids[:, None] == flat_ids[None, :]
    before = jnp.arange(tokens)[:, None] < jnp.arange(tokens)[None, :]
    first = ~jnp.any(same_id & before, 0)
    smaller = (
        (shard[:, None] == shard[None, :])
        & (flat_ids[None, :] < flat_ids[:, None])
        & first[None, :]
    )
    rank = jnp.sum(smaller.astype(jnp.int32), 1)
    slots = place.blk * room

    owner = shard // per_owner
    relative = ((owner ^ place.g) * per_owner + shard % per_owner) * room + rank
    lookup_slots = jnp.where(rank < room, relative, slots)

    def fetch(grp_ids):
        span = per_owner * room
        asked = [lax.dynamic_slice_in_dim(ids, place.g * span, span) for ids in grp_ids]
        local = jnp.concatenate(asked) - place.g * table_rows
        found = word_table.at[jnp.clip(local, 0, table_rows - 1)].get(mode="clip")
        found, sibling = tie(found, grp_ids[1])
        parts = [found[k * span : (k + 1) * span] for k in range(place.grp)]
        rows = [parts[0]] + [place.send(parts[k], k) for k in range(1, place.grp)]
        rows.append(jnp.zeros((tokens - slots, width), low))
        return rows, sibling

    def pack(values, length):
        return jnp.concatenate([values, jnp.zeros((length - values.shape[0],), values.dtype)])

    slot = jnp.where(rank < room, shard * room + rank, slots)
    hit = slot[None, :] == jnp.arange(slots)[:, None]
    slot_ids = jnp.max(jnp.where(hit, flat_ids[None, :], -1), 1)
    early = jnp.concatenate(
        [
            slot_ids,
            false_neg.reshape(-1),
            valid,
            (jnp.max(rank) >= room).astype(jnp.int32)[None],
        ]
    )
    early = pack(early, -(-early.shape[0] // 1024) * 1024).reshape(-1, 128)
    grp_early = [early] + [place.send(early, k) for k in range(1, place.grp)]
    looked_up, sibling = fetch([item.reshape(-1)[:slots] for item in grp_early])
    early_all = jnp.stack(in_order(grp_early, place.g))
    early_all = gather_stage(place, early_all, place.y_masks, place.y)
    early_all, looked_up[1] = tie(early_all, looked_up[1])
    early_all = gather_stage(place, early_all, place.z_masks, place.z)
    early_all = early_all.reshape(place.count, -1)
    ids_all = early_all[:, :slots].reshape(place.blk, place.xs, 2, place.blk, room)
    at = slots
    false_neg_all = early_all[:, at : at + pairs_here * total_pairs].reshape(
        total_pairs, total_pairs
    )
    at += pairs_here * total_pairs
    valid_all = early_all[:, at : at + pairs_here].reshape(-1)
    at += pairs_here
    crowded = jnp.max(early_all[:, at]) > 0

    chip_room = max(16, tokens * 3 // 2 // place.blk // 16 * 16)
    chip_slots = place.blk * chip_room
    known = jnp.any(sibling[:, None] == flat_ids[None, :], 1)
    extra = (
        (sibling[None, :] >= 0)
        & ~known[None, :]
        & (sibling[None, :] // shard_rows == shard[:, None])
        & (sibling[None, :] < flat_ids[:, None])
    )
    chip_rank = rank + jnp.sum(extra.astype(jnp.int32), 1)
    shard_y, shard_z = shard % 2, shard // 2
    order = jnp.where(shard_y ^ place.y == place.core, 0, place.far) + (shard_z ^ place.z)
    gradient_slot = jnp.where(
        chip_rank < chip_room, order * chip_room + chip_rank, chip_slots
    )
    weights = (qkv_weight, out_weight, up_weight, down_weight)

    def encode(slot, found):
        return forward(
            lengths_flat, slot[:, None], found, small_rows, weights, seq_len, head_dim
        )

    ids = lax.dynamic_index_in_dim(ids_all, place.b, 3, keepdims=False)
    ids = merge_ids(ids[:, :, 0], ids[:, :, 1], chip_room)
    ids = ids.reshape(place.far, 2, place.xs, chip_room)
    ids = jnp.stack(in_order([ids[i] for i in range(place.far)], place.z))
    ids = jnp.stack(in_order([ids[:, 0], ids[:, 1]], place.y), 1)
    ids = jnp.transpose(ids, (2, 1, 0, 3))
    local = ids - place.b * shard_rows
    inside = ids >= 0
    counts = jnp.sum(inside.astype(jnp.int32), -1).reshape(-1)
    local = jnp.where(inside, local, shard_rows).reshape(-1)
    counts, local, looked_up[2:] = tie(counts, local, looked_up[2:])
    looked_up = jnp.concatenate(looked_up)

    def look_up_all():
        whole = lax.all_gather(word_table, "grp", axis=0, tiled=True)
        return jnp.arange(tokens, dtype=jnp.int32), whole[flat_ids]

    slot, found = lax.cond(
        crowded, look_up_all, lambda: (lookup_slots.astype(jnp.int32), looked_up)
    )
    (
        unit1,
        inverse1,
        normed_low,
        projected,
        probs,
        attended,
        unit2,
        inverse2,
        middle_low,
        activated_low,
        slope,
        unit3,
        inverse3,
        pooled,
        own_embed,
    ) = encode(slot, found)

    chip_crowded = (jnp.max(rank) >= room) | (jnp.max(chip_rank) >= chip_room)
    embed_rows = jnp.concatenate(
        [own_embed.reshape(-1, width), jnp.full((8, width), chip_crowded, low)]
    )
    gathered = gather_far_first(place, embed_rows).reshape(place.count, -1, width)
    rows_crowded = jnp.max(gathered[:, -1, 0].astype(jnp.float32)) > 0.5
    gathered = gathered[:, : 2 * pairs_here].reshape(total_pairs, 2, width)
    queries, documents = gathered[:, 0], gathered[:, 1]
    diagonal = jnp.arange(total_pairs)[:, None] == jnp.arange(total_pairs)[None, :]
    allowed = (valid_all[None, :] > 0) & ((false_neg_all == 0) | diagonal)
    scores = contract_cols(queries, documents) / logit_divisor_constant
    query_lse, query_probs = masked_softmax(scores, allowed)
    doc_lse, doc_probs = masked_softmax(scores.T, allowed)
    diag = jnp.sum(jnp.where(diagonal, scores, 0.0), -1)
    valid_floats = valid_all.astype(jnp.float32)
    pair_count = jnp.maximum(jnp.sum(valid_floats), 1.0)
    loss_total = jnp.sum(valid_floats * (query_lse + doc_lse - 2.0 * diag)) / 2.0
    row_weight = valid_floats / (2.0 * pair_count)
    identity_mask = diagonal.astype(jnp.float32)
    score_grad = (
        row_weight[:, None] * (query_probs - identity_mask)
        + (row_weight[:, None] * (doc_probs - identity_mask)).T
    )
    row_start = (place.b * place.grp + place.g) * pairs_here
    query_grad_rows = lax.dynamic_slice_in_dim(score_grad, row_start, pairs_here, 0)
    doc_grad_rows = lax.dynamic_slice_in_dim(score_grad, row_start, pairs_here, 1).T
    embed_grad = (
        jnp.stack(
            [
                jnp.dot(
                    query_grad_rows, documents.astype(jnp.float32), precision=finest_arithmetic
                ),
                jnp.dot(doc_grad_rows, queries.astype(jnp.float32), precision=finest_arithmetic),
            ],
            1,
        )
        / logit_divisor_constant
    )

    lowered_grad, lifted_low, second, branch_grad, feed_sums = feed_back(
        lengths_flat,
        embed_grad,
        (unit2, inverse2, slope, unit3, inverse3, pooled),
        small_rows,
        (up_weight, down_weight),
        seq_len,
    )
    theirs_down, mine_down = group_products(place, [(activated_low, lowered_grad)])
    lifted_low, theirs_down, mine_down = tie(lifted_low, theirs_down, mine_down)
    core_down = place.send(theirs_down, 1)
    theirs_up, mine_up = group_products(
        place, [(middle_low, lifted_low), (attended, branch_grad)]
    )
    down = Reduction(place, mine_down.astype(jnp.float32) + core_down.astype(jnp.float32), True)
    down.prepare()
    core_up = place.send(theirs_up, 1)
    up = Reduction(place, mine_up.astype(jnp.float32) + core_up.astype(jnp.float32), False)
    up.prepare()
    second, up.parts, down.parts = tie(second, up.parts, down.parts)
    up.send()
    down.send()
    projected_grad, mine_rows, theirs_rows, position_grad, attention_sums = attention_back(
        gradient_slot,
        second,
        (projected, probs, unit1, inverse1),
        small_rows,
        (qkv_weight, out_weight),
        seq_len,
        head_dim,
        chip_slots,
    )

    theirs_rows, position_grad, down.arrived, up.arrived = tie(
        theirs_rows, position_grad, down.arrived, up.arrived
    )
    small_grad = jnp.concatenate([position_grad, attention_sums[:4], feed_sums[:10]], 0)
    small_flat = small_grad.reshape(-1, strip)
    small_piece = -(-small_flat.shape[0] // (16 * place.count)) * 16
    small_padded = jnp.concatenate(
        [
            small_flat,
            jnp.zeros((small_piece * place.count - small_flat.shape[0], strip), jnp.float32),
        ]
    )
    small_parts = small_padded.reshape(place.blk, place.xs, 2, small_piece, strip)
    small_mine = lax.dynamic_index_in_dim(small_parts, place.core, 2, keepdims=False)
    small_theirs = lax.dynamic_index_in_dim(small_parts, 1 - place.core, 2, keepdims=False)
    rows = mine_rows + place.send(theirs_rows, 1).astype(jnp.float32)
    small_value = small_mine + one_term(place.send(two_terms(small_theirs), 1))
    rows = rows.astype(low).reshape(place.far, chip_room, width)
    down.add()
    down.prepare()
    up.add()
    up.prepare()
    first_rows = jnp.concatenate([rows[0, :, :strip], rows[0, :, strip:]])
    rows, first_rows, small_value, projected_grad, down.parts, up.parts = tie(
        rows, first_rows, small_value, projected_grad, down.parts, up.parts
    )
    arrived = [place.send_split(rows[k], k) for k in range(1, place.far)]
    up.send()
    down_shape = down.parts[0].shape
    down_y = place.send(
        jnp.concatenate([down.parts[0].reshape(-1, strip), first_rows]), place.grp
    )
    theirs_two, mine_two = group_products(place, [(normed_low, projected_grad)])
    arrived, up.arrived, down_y, theirs_two, mine_two = tie(
        arrived, up.arrived, down_y, theirs_two, mine_two
    )
    cut = down_y.shape[0] - first_rows.shape[0]
    down.arrived = [down_y[:cut].reshape(down_shape)]
    other_y = jnp.concatenate([down_y[cut : cut + chip_room], down_y[cut + chip_room :]], 1)
    arrived = jnp.concatenate([jnp.where(place.core == 0, rows[0], other_y)] + arrived)
    over_x = [arrived] + [place.send(arrived, mask) for mask in place.x_masks[1:]]
    core_two = place.send(theirs_two, 1)
    near = [arrived, place.send(arrived, 1)]
    two = Reduction(
        place, mine_two.astype(jnp.float32) + core_two.astype(jnp.float32), False, small_value
    )
    two.prepare()
    down.add()
    up.add()
    one = Reduction(place, jnp.zeros((place.blk, place.xs, 16, strip), low), False)
    one.stages = one.stages[-1:]
    one.value = jnp.concatenate([down.value, up.value], 1)
    one.prepare()
    near, two.parts, one.parts, rows_crowded = tie(near, two.parts, one.parts, rows_crowded)
    two.send()
    one.send()
    own_total = word_sum(
        place.g, counts, local, near, shard_rows, place.far, chip_room
    )
    own_total, over_x = tie(own_total, over_x)
    others = [item for value in over_x[1:] for item in (value, place.send(value, 1))]
    two.add()
    two.prepare()
    others, two.parts = tie(others, two.parts)
    two.send()

    def few_rows():
        return word_sum(
            place.g, counts, local, others, shard_rows, place.far, chip_room, own_total
        )

    def all_rows():
        token_halves = attention_back(
            jnp.arange(tokens, dtype=jnp.int32),
            second,
            (projected, probs, unit1, inverse1),
            small_rows,
            (qkv_weight, out_weight),
            seq_len,
            head_dim,
            tokens,
        )[1:3]
        token_grads = jnp.concatenate([token_halves[0].astype(low), token_halves[1]])
        every_id = lax.all_gather(flat_ids, "blk", axis=0, tiled=True) - place.b * shard_rows
        every_row = lax.all_gather(token_grads, "blk", axis=0, tiled=True)
        inside = (every_id >= 0) & (every_id < shard_rows)
        total = (
            jnp.zeros((shard_rows, width), jnp.float32)
            .at[jnp.where(inside, every_id, shard_rows)]
            .add(every_row.astype(jnp.float32), mode="drop")
        )
        total = lax.psum(total, "grp")
        return total.astype(low), jnp.sum(total * total, 0, keepdims=True)

    word_rows, word_squares = lax.cond(rows_crowded, all_rows, few_rows)
    word_rows, word_squares, two.arrived, one.arrived = tie(
        word_rows, word_squares, two.arrived, one.arrived
    )
    two.add()
    two.prepare()
    two.send()
    one.add()
    two.add()
    piece_one = one.value.astype(low)
    one_x = [piece_one] + [place.send(piece_one, mask) for mask in place.x_masks[1:]]
    piece_two, small_own = two.value.astype(low), two.small
    squares = jnp.sum(small_own * small_own, 0, keepdims=True)
    for item in (piece_one, piece_two):
        item = item.astype(jnp.float32)
        squares = squares + jnp.sum(item * item, 0, keepdims=True)
    squares = squares + jnp.sum(word_squares.reshape(-1, 1, strip), 0) / place.grp
    late = jnp.concatenate([small_own, jnp.broadcast_to(squares, (8, strip))])
    late, one_x = tie(late, one_x)
    late = gather_stage(place, late, place.z_masks, place.z)
    two_x = [piece_two] + [place.send(piece_two, mask) for mask in place.x_masks[1:]]
    late, two_x = tie(late, two_x)
    middle = [a + b for a in place.y_masks for b in place.x_masks]
    late = gather_stage(place, late, middle, place.y * place.xs + place.x)
    late = gather_stage(place, late, place.core_masks, place.core)
    late, one_x, two_x = tie(late, one_x, two_x)
    pieces_one = [item for value in one_x for item in (value, place.send(value, 1))]
    pieces_two = [item for value in two_x for item in (value, place.send(value, 1))]
    late = late.reshape((2, 2, place.xs, place.far) + late.shape[3:])
    late = jnp.transpose(late, (3, 1, 2, 0, 4, 5)).reshape(place.count, -1, strip)
    small_total = late[:, :small_piece].reshape(-1, strip)[: small_flat.shape[0]]
    small_total = small_total.reshape(small_grad.shape)
    grad_norm = jnp.sqrt(jnp.sum(late[:, small_piece]))
    factor = (clip_bound / jnp.maximum(grad_norm, clip_bound)).reshape(1)
    masters = (down_master, up_master, out_master, qkv_master, small_rows)
    moments = (down_moments, up_moments, out_moments, qkv_moments, small_moments)
    rates = tuple(rate_table[i] for i in (4, 3, 2, 1, 5))
    if all(item.shape[0] % (16 * place.xs) == 0 for item in masters[:4]):
        results = adam_all(
            place.g,
            factor,
            (word_rows, word_master, word_moments),
            pieces_one,
            pieces_two,
            small_total,
            masters,
            moments,
            (rate_table[0], *rates),
            (0, 0, 0, 1),
        )
    else:
        ordered = [
            jnp.concatenate(pair)
            for pair in zip(in_order(pieces_one, place.g), in_order(pieces_two, place.g))
        ]
        ordered = jnp.stack(ordered).reshape((place.xs, 2) + ordered[0].shape)
        grads, at = [], 0
        for master in masters[:4]:
            rows, columns = master.shape[0] // place.xs, master.shape[1]
            length = rows * (columns // 2 // strip)
            part = ordered[:, :, at : at + length]
            grads.append(whole_rows(place, part, rows, columns).astype(jnp.float32))
            at += length
        grads.append(small_total)
        results = list(
            adam_rows(factor, word_rows, word_master, word_moments, rate_table[0])
        )
        for grad, moment, master, rate in zip(grads, moments, masters, rates):
            results.extend(adam_update(grad * factor[0], moment, master, rate))
    word, down, up, out, qkv, small = (results[3 * n : 3 * n + 3] for n in range(6))
    results = [*word, *qkv, *out, *up, *down, *small]
    return (loss_total, pair_count, grad_norm, *results)


def solution(mesh):
    in_specs = (
        P(both, None, None),
        P(both, None),
        P(both),
        P(both, None),
        P("grp", None),
        P(),
        P(),
        P(),
        P(),
        P("blk", None),
        P("blk", None),
        P("blk", None),
        P("blk", None),
        P("blk", None),
        P(None, "blk", None),
        P(None, "blk", None),
        P(None, "blk", None),
        P(None, "blk", None),
        P(None, "blk", None),
        P(),
        P(),
    )
    out_specs = (P(), P(), P()) + (P("blk", None),) * 15 + (P(), P(), P())
    return jax.shard_map(
        on_device, mesh=mesh, in_specs=in_specs, out_specs=out_specs, check_vma=False
    )
```
